512 devices in a mesh: leaf: 64 (over x, z, core), head: 8 (over y).
Axes of the slice: x: 4, y: 8, z: 8, core: 2. Of those that a mesh axis runs over, the one named last changes fastest.
Arguments:
- queries: bfloat16 [2, 4096, 8192], P(None, 'leaf', 'head'), may hold values from -64 to 64
- keys: bfloat16 [2, 4096, 1024], P(None, 'leaf', 'head'), may hold values from -64 to 64
- values: bfloat16 [2, 4096, 1024], P(None, 'leaf', 'head'), may hold values from -6 to 6
- output_gradient: bfloat16 [2, 4096, 8192], P(None, 'leaf', 'head'), may hold values from -6 to 6
- q_gain: float32 [128], replicated, may hold values from 0.5 to 6
- k_gain: float32 [128], replicated, may hold values from 0.5 to 6
- leaf_len: int32 [64], P('leaf'), may hold values from 16 to 64, as said below
Outputs:
- dq: bfloat16 [2, 4096, 8192], P(None, 'leaf', 'head')
- dk: bfloat16 [2, 4096, 1024], P(None, 'leaf', 'head')
- dv: bfloat16 [2, 4096, 1024], P(None, 'leaf', 'head')
- dq_gain: float32 [128], replicated
- dk_gain: float32 [128], replicated
The draws below stay inside these ranges and needn't reach their ends.
Inputs may be any that keep to these rules, and one draw needn't show every extreme that they name: `leaf_len`: at least one leaf is full (64 live tokens).
All inputs are finite; a program needn't handle non-finite values.
Results may differ from the reference program's by a relative error of at most 0.039.
The reference program's roundings to bfloat16 on the way count: a program that leaves them out, or rounds other values in their place, can miss the bound.
Values may be sent and summed in bfloat16 or wider, within the bound.
A program may use at most 64 MiB of HBM per device.

```python
import jax
import jax.numpy as jnp
from jax import lax

QUERY_HEADS = 64
KEY_VALUE_HEADS = 8
HEAD_SIZE = 128
NODE_SLOTS = 64
DEPTH = 6
KIND_TOKENS = 4096
N_LEAF = 64


def gaussian_spread(key, shape):
    entries = jnp.clip(jax.random.normal(jax.random.fold_in(key, 1), shape, jnp.float32), -4.0, 4.0)
    row_shape = shape[:3] + (1,) * (len(shape) - 3)
    row_scale = jnp.exp(jax.random.uniform(jax.random.fold_in(key, 2), row_shape, jnp.float32, -1.2, 1.2))
    col_scale = jnp.exp(jax.random.uniform(jax.random.fold_in(key, 3), (shape[-1],), jnp.float32, -1.2, 1.2))
    return entries * row_scale * col_scale


def shared_keys(key):
    return gaussian_spread(jax.random.fold_in(key, 101), (2, N_LEAF, NODE_SLOTS, KEY_VALUE_HEADS, HEAD_SIZE))


def draw_keys(key, part):
    starting_rows = shared_keys(key)
    return starting_rows.reshape(2, KIND_TOKENS, KEY_VALUE_HEADS * HEAD_SIZE).astype(jnp.bfloat16)


def draw_queries(key, part):
    key = jax.random.fold_in(key, 9)
    query_group_count = QUERY_HEADS // KEY_VALUE_HEADS
    owned_rows = gaussian_spread(key, (2, N_LEAF, NODE_SLOTS, KEY_VALUE_HEADS, query_group_count, HEAD_SIZE))
    return owned_rows.reshape(2, KIND_TOKENS, QUERY_HEADS * HEAD_SIZE).astype(jnp.bfloat16)


def draw_q_gain(key, part):
    key = jax.random.fold_in(key, 13)
    return jax.random.uniform(key, (HEAD_SIZE,), jnp.float32, 0.6, 1.6)


def draw_k_gain(key, part):
    key = jax.random.fold_in(key, 17)
    return jax.random.uniform(key, (HEAD_SIZE,), jnp.float32, 0.6, 1.6)


def draw_leaf_len(key, part):
    key = jax.random.fold_in(key, 11)
    lengths = jax.random.randint(jax.random.fold_in(key, 1), (N_LEAF,), NODE_SLOTS // 4, NODE_SLOTS + 1)
    full_leaf = jax.random.randint(jax.random.fold_in(key, 2), (), 0, N_LEAF)
    return jnp.where(jnp.arange(N_LEAF) == full_leaf, NODE_SLOTS, lengths).astype(jnp.int32)


def shard_levels(own_key, dims, shards, smallest, top_value):
    factor_of = 1.0
    for axis_at, blocks in shards:
        draws = jax.random.uniform(jax.random.fold_in(jax.random.fold_in(own_key, 6), axis_at), (blocks,), jnp.float32, smallest / len(shards), top_value / len(shards))
        factor_of = factor_of * jnp.repeat(jnp.exp(draws), dims[axis_at] // blocks).reshape((-1,) + (1,) * (len(dims) - 1 - axis_at))
    return factor_of


def scatter_about(own_key, dims, spread, limit, shards=(), kind=jnp.bfloat16):
    factor_of = shard_levels(own_key, dims, shards, -0.22, 0.18) if shards else 1.0
    result = jax.random.normal(own_key, dims, jnp.float32) * spread * factor_of
    return jnp.minimum(jnp.maximum(result, -limit), limit).astype(kind)


def setup_inputs(seed: int = 0) -> dict:
    arg_keys = jax.random.split(jax.random.key(seed), 8)
    return {
        "queries": draw_queries(jax.random.fold_in(arg_keys[7], 71), 0),
        "keys": draw_keys(jax.random.fold_in(arg_keys[7], 71), 0),
        "values": scatter_about(arg_keys[2], (2, KIND_TOKENS, KEY_VALUE_HEADS * HEAD_SIZE), 1.0, 6.0, ((1, 64), (2, 8))),
        "output_gradient": scatter_about(arg_keys[3], (2, KIND_TOKENS, QUERY_HEADS * HEAD_SIZE), 1.0, 6.0, ((1, 64), (2, 8))),
        "q_gain": draw_q_gain(jax.random.fold_in(arg_keys[7], 71), 0),
        "k_gain": draw_k_gain(jax.random.fold_in(arg_keys[7], 71), 0),
        "leaf_len": draw_leaf_len(jax.random.fold_in(arg_keys[7], 71), 0),
    }


NEG_BIG = -1000000000.0
NORM_EPS = 1e-06
ROPE_BASE = 1000000.0

def rotate(values_in, positions, direction):
    half_width = values_in.shape[-1] // 2
    frequency = ROPE_BASE ** (-(jnp.arange(half_width, dtype=jnp.float32) * 2.0 / values_in.shape[-1]))
    angles = positions.astype(jnp.float32)[..., None] * frequency
    extra_dims = values_in.ndim - 1 - positions.ndim
    angles = angles.reshape(positions.shape + (1,) * extra_dims + (half_width,))
    cosine = jnp.cos(angles)
    sine_part = direction * jnp.sin(angles)
    lower_half = values_in[..., :half_width]
    upper_half = values_in[..., half_width:]
    return jnp.concatenate([lower_half * cosine - upper_half * sine_part, upper_half * cosine + lower_half * sine_part], axis=-1)

def normalize(values_in, gain_vec):
    mean_square = lax.optimization_barrier(jnp.mean(values_in * values_in, axis=-1, keepdims=True))
    factor = lax.rsqrt(mean_square + NORM_EPS)
    unit_rows = values_in * factor
    return (unit_rows * gain_vec, unit_rows, factor)

def norm_back(upstream, unit_rows, factor, gain_vec):
    scaled = upstream * gain_vec
    inner_sum = lax.optimization_barrier(jnp.mean(scaled * unit_rows, axis=-1, keepdims=True))
    gain_grad = lax.optimization_barrier(jnp.sum((upstream * unit_rows).reshape(-1, upstream.shape[-1]), axis=0))
    return (factor * (scaled - unit_rows * inner_sum), gain_grad)

def rounded(values_in):
    return lax.optimization_barrier(values_in.astype(jnp.bfloat16))

def attend(query_rows, key_matrix_rows, value_matrix_rows, out_rows, allowed):
    score_scale = query_rows.shape[-1] ** (-0.5)
    query_f = query_rows.astype(jnp.float32)
    key_f = key_matrix_rows.astype(jnp.float32)
    value_f = value_matrix_rows.astype(jnp.float32)
    out_f = out_rows.astype(jnp.float32)
    scores = jnp.einsum('rkgd,skd->kgrs', query_f, key_f) * score_scale
    scores = jnp.where(allowed, scores, NEG_BIG)
    row_top = lax.optimization_barrier(jnp.max(scores, axis=-1, keepdims=True))
    log_total = row_top + jnp.log(lax.optimization_barrier(jnp.sum(jnp.exp(scores - row_top), axis=-1, keepdims=True)))
    probs = jnp.exp(scores - log_total)
    probs_low = rounded(probs).astype(jnp.float32)
    output = jnp.einsum('kgrs,skd->rkgd', probs_low, value_f)
    delta_sum = jnp.transpose(lax.optimization_barrier(jnp.sum(out_f * output, axis=-1)), (1, 2, 0))[..., None]
    dprob = jnp.einsum('rkgd,skd->kgrs', out_f, value_f)
    dscore = rounded(probs * (dprob - delta_sum)).astype(jnp.float32)
    query_gradient_rows = jnp.einsum('kgrs,skd->rkgd', dscore, key_f) * score_scale
    key_gradient_rows = jnp.einsum('kgrs,rkgd->skd', dscore, query_f) * score_scale
    value_gradient_rows = jnp.einsum('kgrs,rkgd->skd', probs_low, out_f)
    return (query_gradient_rows, key_gradient_rows, value_gradient_rows)

def reference(queries, keys, values, output_gradient, q_gain, k_gain, leaf_len):
    leaves_count = N_LEAF
    rollout_depth = DEPTH
    query_group_count = QUERY_HEADS // KEY_VALUE_HEADS
    segment_length = NODE_SLOTS
    leaves = jnp.arange(leaves_count, dtype=jnp.int32)
    hosted = jnp.ones((leaves_count,), jnp.int32)
    for tree_level in range(1, rollout_depth + 1):
        hosted = hosted + (leaves % 2 ** tree_level == 0).astype(jnp.int32)
    row_ids = jnp.arange(segment_length, dtype=jnp.int32)
    leaf_place = jnp.broadcast_to(rollout_depth * segment_length + row_ids, (leaves_count, segment_length))
    host_place = jnp.maximum(rollout_depth - hosted, 0)[:, None] * segment_length + row_ids[None, :]
    positions = jnp.stack([leaf_place, host_place])
    query_input = queries.astype(jnp.float32).reshape(2, leaves_count, segment_length, KEY_VALUE_HEADS, query_group_count, HEAD_SIZE)
    q_normed, q_unit, q_factor = normalize(query_input, q_gain)
    q_rot = rounded(rotate(q_normed, positions, 1.0))
    key_input = keys.astype(jnp.float32).reshape(2, leaves_count, segment_length, KEY_VALUE_HEADS, HEAD_SIZE)
    k_normed, k_unit, k_factor = normalize(key_input, k_gain)
    key_rotary = rounded(rotate(k_normed, positions, 1.0))
    value_total = values.reshape(2, leaves_count, segment_length, KEY_VALUE_HEADS, HEAD_SIZE)
    retained_rows = jnp.stack([row_ids[None, :] < leaf_len[:, None], jnp.broadcast_to((hosted <= rollout_depth)[:, None], (leaves_count, segment_length))])
    output_gradient_rows = jnp.where(retained_rows[..., None, None, None], output_gradient.reshape(2, leaves_count, segment_length, KEY_VALUE_HEADS, query_group_count, HEAD_SIZE), jnp.zeros((), jnp.bfloat16))
    span_sizes = jnp.array([2 ** tree_level for tree_level in range(1, rollout_depth + 1)], jnp.int32)
    owners = leaves[:, None] // span_sizes[None, :] * span_sizes[None, :] + span_sizes[None, :] // 2
    key_index = jnp.arange((rollout_depth + 1) * segment_length, dtype=jnp.int32)
    slot_of_key = key_index // segment_length
    key_in_slot = key_index % segment_length
    row_index = jnp.arange(2 * segment_length, dtype=jnp.int32)
    is_leaf = row_index < segment_length
    row_in_slot = row_index % segment_length

    def one_leaf(leaf_position_index):
        owning_row = owners[leaf_position_index]
        key_matrix_rows = jnp.concatenate([key_rotary[0, leaf_position_index][None], key_rotary[1][owning_row]], axis=0).reshape((rollout_depth + 1) * segment_length, KEY_VALUE_HEADS, HEAD_SIZE)
        value_matrix_rows = jnp.concatenate([value_total[0, leaf_position_index][None], value_total[1][owning_row]], axis=0).reshape((rollout_depth + 1) * segment_length, KEY_VALUE_HEADS, HEAD_SIZE)
        query_rows = jnp.concatenate([q_rot[0, leaf_position_index], q_rot[1, leaf_position_index]], axis=0)
        out_rows = jnp.concatenate([output_gradient_rows[0, leaf_position_index], output_gradient_rows[1, leaf_position_index]], axis=0)
        own_level = hosted[leaf_position_index]
        causal = key_in_slot[None, :] <= row_in_slot[:, None]
        own_part = is_leaf[:, None] & causal & (key_in_slot[None, :] < leaf_len[leaf_position_index])
        chain_part = is_leaf[:, None] | (slot_of_key[None, :] > own_level) | (slot_of_key[None, :] == own_level) & causal
        allowed = jnp.where(slot_of_key[None, :] == 0, own_part, chain_part)
        return attend(query_rows, key_matrix_rows, value_matrix_rows, out_rows, allowed)
    query_gradient_rows, key_gradient_rows, value_gradient_rows = lax.map(one_leaf, leaves)
    query_rotary_gradient = jnp.swapaxes(query_gradient_rows.reshape(leaves_count, 2, segment_length, KEY_VALUE_HEADS, query_group_count, HEAD_SIZE), 0, 1)
    key_gradient_rows = key_gradient_rows.reshape(leaves_count, rollout_depth + 1, segment_length, KEY_VALUE_HEADS, HEAD_SIZE)
    value_gradient_rows = value_gradient_rows.reshape(leaves_count, rollout_depth + 1, segment_length, KEY_VALUE_HEADS, HEAD_SIZE)
    flattened_owner_list = owners.reshape(-1)
    key_gradient_node = jnp.zeros((leaves_count, segment_length, KEY_VALUE_HEADS, HEAD_SIZE), jnp.float32).at[flattened_owner_list].add(key_gradient_rows[:, 1:].reshape(leaves_count * rollout_depth, segment_length, KEY_VALUE_HEADS, HEAD_SIZE))
    value_gradient_node = jnp.zeros((leaves_count, segment_length, KEY_VALUE_HEADS, HEAD_SIZE), jnp.float32).at[flattened_owner_list].add(value_gradient_rows[:, 1:].reshape(leaves_count * rollout_depth, segment_length, KEY_VALUE_HEADS, HEAD_SIZE))
    dk_rot = jnp.stack([key_gradient_rows[:, 0], key_gradient_node])
    value_gradient_total = jnp.stack([value_gradient_rows[:, 0], value_gradient_node])
    q_back = rotate(query_rotary_gradient, positions, -1.0)
    dq_in, dq_gain = norm_back(q_back, q_unit, q_factor, q_gain)
    k_back = rotate(dk_rot, positions, -1.0)
    key_input_gradient, dk_gain = norm_back(k_back, k_unit, k_factor, k_gain)
    dq = dq_in.astype(jnp.bfloat16).reshape(2, KIND_TOKENS, QUERY_HEADS * HEAD_SIZE)
    dk = key_input_gradient.astype(jnp.bfloat16).reshape(2, KIND_TOKENS, KEY_VALUE_HEADS * HEAD_SIZE)
    dv = value_gradient_total.astype(jnp.bfloat16).reshape(2, KIND_TOKENS, KEY_VALUE_HEADS * HEAD_SIZE)
    return (dq, dk, dv, dq_gain, dk_gain)
```

```python
import jax
import jax.numpy as jnp
import numpy as np
from jax import lax
from jax.experimental import pallas as pl
from jax.experimental.pallas import tpu as pltpu
from jax.sharding import PartitionSpec as P

NEG_BIG = -1000000000.0
NORM_EPS = 1e-06
ROPE_BASE = 1000000.0
DEPTH = 6
T = 64
D = 128
G = 8
SLOTS = DEPTH + 1
KEYS = SLOTS * T
ROWS = G * T
NX, NZ, NC, NY = 4, 8, 2, 8
NQ = NZ * NC
SCALE = D ** (-0.5)
BF = jnp.bfloat16
F32 = jnp.float32
MESH = pl.DeviceIdType.MESH


def rope_table():
    frequency = (ROPE_BASE ** (-(np.arange(D // 2, dtype=np.float32) * 2.0 / D))).astype(np.float32)
    angles = np.arange(KEYS, dtype=np.float32)[:, None] * frequency
    return np.concatenate([np.cos(angles), np.sin(angles)], axis=1).astype(np.float32)


def spread(table):
    lane = lax.broadcasted_iota(jnp.int32, table.shape, 1)
    other = pltpu.roll(table, D // 2, axis=1)
    low = lane < D // 2
    return jnp.where(low, table, other), jnp.where(low, -other, table)


def turn(x, cosine, sine):
    return x * cosine + pltpu.roll(x, D // 2, axis=1) * sine


def unturn(x, cosine, sine):
    return x * cosine - pltpu.roll(x, D // 2, axis=1) * sine


def unit_of(x):
    factor = lax.rsqrt(jnp.mean(x * x, axis=-1, keepdims=True) + NORM_EPS)
    return x * factor, factor


def dot(a, b, contract):
    return lax.dot_general(a, b, (contract, ((), ())), preferred_element_type=F32)


def kernel(
    q_in, k_in, v_in, g_in, qg_in, kg_in, len_in, table_in,
    dq_out, dk_out, dv_out, dqg_out, dkg_out,
    q_raw, g_raw, own, kv, qg, kg, length, table,
    q_rot, q_unit, g_rows, k_rot, k_unit, v_all, part, y_q, dq_buf, dkv_buf,
    send_kv, send_sum, x_recv, z_recv, gain_send, gain_z, gain_x, gain_y, gain_total,
    load_sem, store_sem, b_send, b_recv, r_send, r_recv, x_sem, xr_sem, s_send,
    gz_send, gz_recv, gx_send, gx_recv, gy_send, gy_recv,
):
    leaf = lax.axis_index("leaf")
    y = lax.axis_index("head")
    x = leaf // NQ
    q = lax.rem(leaf, NQ)
    z = q // NC
    c = lax.rem(q, NC)

    def at(xx, qq, yy=None):
        return (xx * NQ + qq, y if yy is None else yy)

    hosted = jnp.int32(1)
    for level in range(1, DEPTH + 1):
        hosted = hosted + jnp.where(lax.rem(leaf, 2**level) == 0, 1, 0)

    def remote(src, dst, send, recv, device):
        return pltpu.make_async_remote_copy(
            src_ref=src, dst_ref=dst, send_sem=send, recv_sem=recv, device_id=device, device_id_type=MESH
        )

    holder = {level: q // 2**level * 2**level + 2 ** (level - 1) for level in range(1, 5)}
    is_relay = q == 1
    far_owner = jnp.logical_and(q == 0, x > 0)

    loads = [
        pltpu.make_async_copy(k_in.at[1], own.at[0], load_sem.at[0]),
        pltpu.make_async_copy(v_in.at[1], own.at[1], load_sem.at[1]),
        pltpu.make_async_copy(k_in.at[0], kv.at[0, 0], load_sem.at[2]),
        pltpu.make_async_copy(v_in.at[0], kv.at[0, 1], load_sem.at[3]),
        pltpu.make_async_copy(table_in, table, load_sem.at[4]),
        pltpu.make_async_copy(qg_in, qg, load_sem.at[5]),
        pltpu.make_async_copy(kg_in, kg, load_sem.at[6]),
        pltpu.make_async_copy(q_in, q_raw, load_sem.at[7]),
        pltpu.make_async_copy(g_in, g_raw, load_sem.at[8]),
        pltpu.make_async_copy(len_in, length, load_sem.at[9]),
    ]
    for load in loads:
        load.start()

    barrier = pltpu.get_barrier_semaphore()

    def greet(device):
        pl.semaphore_signal(barrier, inc=1, device_id=device, device_id_type=MESH)

    @pl.when(is_relay)
    def _():
        greet(at(2, 0))
        greet(at(x // 2 * 2 + 1, 0))

    for other in range(1, NX):
        greet(at(lax.rem(x + other, NX), q))

    @pl.when(jnp.logical_not(is_relay))
    def _():
        greet(at(x, 1))

    for level in (4, 3, 2, 1):

        @pl.when(q != holder[level])
        def _(level=level):
            greet(at(x, holder[level]))

    for other in range(1, NY):
        greet(at(x, z * NC + 1, lax.rem(y + other, NY)))

    early = jnp.int32(NX - 1)
    early = early + jnp.where(c == 1, 1 + (NY - 1) * NC, 0)
    early = early + jnp.where(is_relay, NQ - 1, 0)
    for level in (2, 3, 4):
        early = early + jnp.where(hosted == level, 2**level - 1, 0)
    early = early + jnp.where(hosted == 5, 2, 0) + jnp.where(hosted == 6, NX, 0)

    loads[0].wait()
    loads[1].wait()

    @pl.when(far_owner)
    def _():
        pl.semaphore_wait(barrier, early)

        @pl.when(x == 2)
        def _():
            for xx in range(NX):
                remote(own, kv.at[6], b_send.at[xx], b_recv.at[6], at(xx, 1)).start()

        @pl.when(x != 2)
        def _():
            for n in range(2):
                remote(own, kv.at[5], b_send.at[n], b_recv.at[5], at(x - n, 1)).start()

    @pl.when(jnp.logical_not(far_owner))
    def _():
        pl.semaphore_wait(barrier, early)

    for level in (4, 3, 2, 1):

        @pl.when(hosted == level)
        def _(level=level):
            half = 2 ** (level - 1)
            offsets = sorted((o for o in range(-half, half) if o), key=lambda o: -abs(o))
            for n, offset in enumerate(offsets):
                remote(own, kv.at[level], b_send.at[n], b_recv.at[level], at(x, q + offset)).start()
            for n in range(2):
                pltpu.make_async_copy((k_in, v_in)[n].at[1], kv.at[level, n], load_sem.at[10 + n]).start()

    others = [qq for zz in (4, 3, 5, 2, 6, 1, 7, 0) for qq in (2 * zz, 2 * zz + 1) if qq != 1]

    @pl.when(is_relay)
    def _():
        for level in (5, 6):
            remote(own, kv.at[level], b_send.at[0], b_recv.at[level], at(x, 0)).wait_recv()
            for n, qq in enumerate(others):
                remote(
                    kv.at[level], kv.at[level], b_send.at[1 + (level - 5) * 15 + n], b_recv.at[level], at(x, qq)
                ).start()

    for load in loads[4:]:
        load.wait()
    q_gain, k_gain = qg[...], kg[...]
    place = [DEPTH * T, jnp.maximum(DEPTH - hosted, 0) * T]
    live = [
        lax.broadcasted_iota(jnp.int32, (T, D), 0) < length[0],
        jnp.broadcast_to(hosted <= DEPTH, (T, D)),
    ]
    for kind in range(2):
        cosine, sine = spread(table[pl.ds(pl.multiple_of(place[kind], T), T), :])
        for head in range(G):
            rows = pl.ds(kind * ROWS + head * T, T)
            unit, _ = unit_of(q_raw[kind, :, head * D : (head + 1) * D].astype(F32))
            q_unit[rows, :] = unit
            q_rot[rows, :] = turn(unit * q_gain, cosine, sine).astype(BF)
            grad = g_raw[kind, :, head * D : (head + 1) * D]
            g_rows[rows, :] = jnp.where(live[kind], grad, jnp.zeros((), BF))

    loads[2].wait()
    loads[3].wait()

    def take(slot):
        rows = pl.ds(slot * T, T)
        cosine, sine = spread(table[(DEPTH - slot) * T : (DEPTH - slot + 1) * T, :])
        unit, _ = unit_of(kv[slot, 0].astype(F32))
        k_unit[rows, :] = unit
        k_rot[rows, :] = turn(unit * k_gain, cosine, sine).astype(BF)
        v_all[rows, :] = kv[slot, 1]

    take(0)
    for level in range(1, 5):

        @pl.when(q != holder[level])
        def _(level=level):
            remote(own, kv.at[level], b_send.at[0], b_recv.at[level], at(x, holder[level])).wait_recv()

        @pl.when(hosted == level)
        def _(level=level):
            for n in range(2):
                pltpu.make_async_copy((k_in, v_in)[n].at[1], kv.at[level, n], load_sem.at[10 + n]).wait()

        take(level)

    @pl.when(jnp.logical_not(is_relay))
    def _():
        for level in (5, 6):
            remote(own, kv.at[level], b_send.at[0], b_recv.at[level], at(x, 1)).wait_recv()

    take(5)
    take(6)

    key_at = lax.broadcasted_iota(jnp.int32, (T, ROWS), 0)
    row_at = lax.rem(lax.broadcasted_iota(jnp.int32, (T, ROWS), 1), T)
    ahead = key_at - row_at
    dk = dv = None
    for kind in range(2):
        rows = slice(kind * ROWS, (kind + 1) * ROWS)
        first = 0 if kind == 0 else T
        keys, vals = k_rot[first:, :], v_all[first:, :]
        queries, grads = q_rot[rows, :], g_rows[rows, :]
        scores = dot(keys, queries, ((1,), (1,))) * SCALE
        pieces = []
        for slot in range(SLOTS):
            if kind == 0:
                piece = scores[slot * T : (slot + 1) * T]
                if slot == 0:
                    seen = jnp.logical_and(ahead <= 0, key_at < length[0])
                    piece = jnp.where(seen, piece, NEG_BIG)
            elif slot == 0:
                continue
            else:
                piece = scores[(slot - 1) * T : slot * T]
                bound = jnp.where(hosted == slot, 0, jnp.where(hosted < slot, T, -T))
                piece = jnp.where(ahead <= bound, piece, NEG_BIG)
            pieces.append(piece)
        scores = jnp.concatenate(pieces, axis=0)
        top = jnp.max(scores, axis=0, keepdims=True)
        raised = jnp.exp(scores - top)
        probs = raised * (1.0 / jnp.sum(raised, axis=0, keepdims=True))
        probs_low = probs.astype(BF)
        dprobs = dot(vals, grads, ((1,), (1,)))
        delta = jnp.sum(probs_low.astype(F32) * dprobs, axis=0, keepdims=True)
        dscores = (probs * (dprobs - delta)).astype(BF)
        dv_part = dot(probs_low, grads, ((1,), (0,)))
        dk_part = dot(dscores, queries, ((1,), (0,))) * SCALE
        dq_turned = dot(keys, dscores, ((0,), (0,))) * SCALE
        y_q[rows, :] = jnp.transpose(dq_turned)
        for slot in range(SLOTS):
            if kind == 1 and slot == 0:
                continue
            here = slice(slot * T - first, (slot + 1) * T - first)
            if kind == 0:
                part[slot, 0] = dk_part[here]
                part[slot, 1] = dv_part[here]
            else:
                part[slot, 0] += dk_part[here]
                part[slot, 1] += dv_part[here]

    for slot in range(1, SLOTS):
        send_kv[slot - 1] = part[slot].astype(BF)

    @pl.when(x != 2)
    def _():
        n = jnp.minimum(x, 2)
        remote(send_kv.at[5], x_recv.at[n], x_sem.at[0], xr_sem.at[n], at(2, q)).start()

    @pl.when(lax.rem(x, 2) == 0)
    def _():
        remote(send_kv.at[4], x_recv.at[3], x_sem.at[1], xr_sem.at[3], at(x + 1, q)).start()

    gain_q = jnp.zeros((1, D), F32)
    for kind in range(2):
        cosine, sine = spread(table[pl.ds(pl.multiple_of(place[kind], T), T), :])
        for head in range(G):
            rows = pl.ds(kind * ROWS + head * T, T)
            back = unturn(y_q[rows, :], cosine, sine)
            y_q[rows, :] = back
            gain_q = gain_q + jnp.sum(back * q_unit[rows, :], axis=0, keepdims=True)
    gain_k = jnp.zeros((1, D), F32)
    for slot in range(SLOTS):
        cosine, sine = spread(table[(DEPTH - slot) * T : (DEPTH - slot + 1) * T, :])
        back = unturn(part[slot, 0], cosine, sine)
        gain_k = gain_k + jnp.sum(back * k_unit[slot * T : (slot + 1) * T, :], axis=0, keepdims=True)
    row = lax.broadcasted_iota(jnp.int32, (8, D), 0)
    terms = jnp.where(row == 0, gain_q, jnp.where(row == 1, gain_k, 0.0))
    gain_send[0] = terms

    for zz in range(NZ):
        qq = 2 * zz + 1

        @pl.when(q != qq)
        def _(zz=zz, qq=qq):
            remote(gain_send.at[0], gain_z.at[q], gz_send.at[zz], gz_recv.at[q], at(x, qq)).start()

    for level in range(1, 5):

        @pl.when(q != holder[level])
        def _(level=level):
            n = lax.rem(q, 2**level)
            remote(send_kv.at[level - 1], z_recv.at[n], r_send.at[level], r_recv.at[n], at(x, holder[level])).start()

    for kind in range(2):
        for head in range(G):
            rows = pl.ds(kind * ROWS + head * T, T)
            columns = slice(head * D, (head + 1) * D)
            raw = q_raw[kind, :, columns].astype(F32)
            unit, factor = unit_of(raw)
            scaled = y_q[rows, :] * q_gain
            inner = jnp.mean(scaled * unit, axis=-1, keepdims=True)
            dq_buf[kind, :, columns] = (factor * (scaled - unit * inner)).astype(BF)
    stores = [pltpu.make_async_copy(dq_buf, dq_out, store_sem.at[0])]
    stores[0].start()

    def key_gradient(raw, turned, start):
        cosine, sine = spread(table[pl.ds(start, T), :])
        unit, factor = unit_of(raw.astype(F32))
        scaled = unturn(turned, cosine, sine) * k_gain
        inner = jnp.mean(scaled * unit, axis=-1, keepdims=True)
        return (factor * (scaled - unit * inner)).astype(BF)

    dkv_buf[0, 0] = key_gradient(kv[0, 0], part[0, 0], DEPTH * T)
    dkv_buf[1, 0] = part[0, 1].astype(BF)

    def from_x(n):
        remote(own, x_recv.at[n], x_sem.at[0], xr_sem.at[n], at(x, q)).wait_recv()

    @pl.when(x == 2)
    def _():
        total = part[6]
        for n in range(3):
            from_x(n)
            total = total + x_recv[n].astype(F32)
        part[6] = total
        send_sum[...] = total.astype(BF)

    @pl.when(lax.rem(x, 2) == 1)
    def _():
        from_x(3)
        total = part[5] + x_recv[3].astype(F32)
        part[5] = total
        send_sum[...] = total.astype(BF)

    @pl.when(jnp.logical_and(x > 0, q != 0))
    def _():
        remote(send_sum, z_recv.at[q], s_send, r_recv.at[q], at(x, 0)).start()

    @pl.when(c == 1)
    def _():
        gain_z[q] = terms
        for zz in range(NZ):
            for cc in range(NC):
                qq = zz * NC + cc

                @pl.when(q != qq)
                def _(qq=qq):
                    remote(gain_send.at[0], gain_z.at[qq], gz_send.at[0], gz_recv.at[qq], at(x, qq)).wait_recv()

        total = gain_z[0]
        for qq in range(1, NQ):
            total = total + gain_z[qq]
        gain_send[1] = total
        gain_x[x] = total
        for other in range(1, NX):
            remote(
                gain_send.at[1], gain_x.at[x], gx_send.at[other], gx_recv.at[x], at(lax.rem(x + other, NX), q)
            ).start()
        for other in range(1, NX):
            xx = lax.rem(x + other, NX)
            remote(gain_send.at[1], gain_x.at[xx], gx_send.at[other], gx_recv.at[xx], at(xx, q)).wait_recv()
        total = gain_x[0]
        for xx in range(1, NX):
            total = total + gain_x[xx]
        gain_send[2] = total
        gain_y[y] = total
        for other in (4, 3, 5, 2, 6, 1, 7):
            yy = lax.rem(y + other, NY)
            for cc in range(NC):
                remote(
                    gain_send.at[2], gain_y.at[y], gy_send.at[2 * other + cc], gy_recv.at[y], at(x, z * NC + cc, yy)
                ).start()
        remote(gain_send.at[2], gain_y.at[y], gy_send.at[0], gy_recv.at[y], at(x, z * NC)).start()

    @pl.when(hosted <= DEPTH)
    def _():
        size = jnp.int32(NQ)
        for level in range(1, 4):
            size = jnp.where(hosted == level, 2**level, size)
        mine = jnp.where(hosted < 5, size // 2, 0)

        def add(n, total):
            remote(own, z_recv.at[n], s_send, r_recv.at[n], at(x, q)).wait_recv()
            return total + z_recv[n].astype(F32)

        total = lax.fori_loop(0, mine, add, part[hosted])
        total = lax.fori_loop(mine + 1, size, add, total)
        dkv_buf[0, 1] = key_gradient(own[0], total[0], pl.multiple_of(place[1], T))
        dkv_buf[1, 1] = total[1].astype(BF)

    @pl.when(hosted > DEPTH)
    def _():
        dkv_buf[0, 1] = jnp.zeros((T, D), BF)
        dkv_buf[1, 1] = jnp.zeros((T, D), BF)

    stores.append(pltpu.make_async_copy(dkv_buf.at[0], dk_out, store_sem.at[1]))
    stores.append(pltpu.make_async_copy(dkv_buf.at[1], dv_out, store_sem.at[2]))
    stores[1].start()
    stores[2].start()

    for yy in range(NY):

        @pl.when(jnp.logical_or(c == 0, y != yy))
        def _(yy=yy):
            remote(gain_send.at[2], gain_y.at[yy], gy_send.at[0], gy_recv.at[yy], at(x, q)).wait_recv()

    total = gain_y[0]
    for yy in range(1, NY):
        total = total + gain_y[yy]
    gain_total[...] = total
    stores.append(pltpu.make_async_copy(gain_total.at[pl.ds(0, 1)], dqg_out, store_sem.at[3]))
    stores.append(pltpu.make_async_copy(gain_total.at[pl.ds(1, 1)], dkg_out, store_sem.at[4]))
    stores[3].start()
    stores[4].start()

    def sent(src, sem):
        remote(src, src, sem, sem, at(x, q)).wait_send()

    @pl.when(hosted == 6)
    def _():
        for n in range(NX):
            sent(own, b_send.at[n])

    @pl.when(hosted == 5)
    def _():
        for n in range(2):
            sent(own, b_send.at[n])

    for level in range(1, 5):

        @pl.when(hosted == level)
        def _(level=level):
            for n in range(2**level - 1):
                sent(own, b_send.at[n])

    @pl.when(is_relay)
    def _():
        for n in range(1, 31):
            sent(own, b_send.at[n])

    @pl.when(x != 2)
    def _():
        sent(own, x_sem.at[0])

    @pl.when(lax.rem(x, 2) == 0)
    def _():
        sent(own, x_sem.at[1])

    for zz in range(NZ):

        @pl.when(q != 2 * zz + 1)
        def _(zz=zz):
            sent(gain_send.at[0], gz_send.at[zz])

    for level in range(1, 5):

        @pl.when(q != holder[level])
        def _(level=level):
            sent(own, r_send.at[level])

    @pl.when(jnp.logical_and(x > 0, q != 0))
    def _():
        sent(own, s_send)

    @pl.when(c == 1)
    def _():
        for other in range(1, NX):
            sent(gain_send.at[0], gx_send.at[other])
        for n in range(2, 2 * NY):
            sent(gain_send.at[0], gy_send.at[n])
        sent(gain_send.at[0], gy_send.at[0])

    for store in stores:
        store.wait()


def on_device(queries, keys, values, output_gradient, q_gain, k_gain, leaf_len):
    dma = pltpu.SemaphoreType.DMA
    anywhere = pl.BlockSpec(memory_space=pl.ANY)
    dq, dk, dv, dq_gain, dk_gain = pl.pallas_call(
        kernel,
        name="tree_backward",
        out_shape=[
            jax.ShapeDtypeStruct(queries.shape, BF),
            jax.ShapeDtypeStruct(keys.shape, BF),
            jax.ShapeDtypeStruct(values.shape, BF),
            jax.ShapeDtypeStruct((1, D), F32),
            jax.ShapeDtypeStruct((1, D), F32),
        ],
        in_specs=[anywhere] * 8,
        out_specs=[anywhere] * 5,
        scratch_shapes=[
            pltpu.VMEM((2, T, G * D), BF),
            pltpu.VMEM((2, T, G * D), BF),
            pltpu.VMEM((2, T, D), BF),
            pltpu.VMEM((SLOTS, 2, T, D), BF),
            pltpu.VMEM((1, D), F32),
            pltpu.VMEM((1, D), F32),
            pltpu.SMEM((1,), jnp.int32),
            pltpu.VMEM((KEYS, D), F32),
            pltpu.VMEM((2 * ROWS, D), BF),
            pltpu.VMEM((2 * ROWS, D), F32),
            pltpu.VMEM((2 * ROWS, D), BF),
            pltpu.VMEM((KEYS, D), BF),
            pltpu.VMEM((KEYS, D), F32),
            pltpu.VMEM((KEYS, D), BF),
            pltpu.VMEM((SLOTS, 2, T, D), F32),
            pltpu.VMEM((2 * ROWS, D), F32),
            pltpu.VMEM((2, T, G * D), BF),
            pltpu.VMEM((2, 2, T, D), BF),
            pltpu.VMEM((DEPTH, 2, T, D), BF),
            pltpu.VMEM((2, T, D), BF),
            pltpu.VMEM((4, 2, T, D), BF),
            pltpu.VMEM((NQ, 2, T, D), BF),
            pltpu.VMEM((3, 8, D), F32),
            pltpu.VMEM((NQ, 8, D), F32),
            pltpu.VMEM((NX, 8, D), F32),
            pltpu.VMEM((NY, 8, D), F32),
            pltpu.VMEM((8, D), F32),
            dma((12,)),
            dma((5,)),
            dma((31,)),
            dma((SLOTS,)),
            dma((5,)),
            dma((NQ,)),
            dma((2,)),
            dma((4,)),
            dma(()),
            dma((NZ,)),
            dma((NQ,)),
            dma((NX,)),
            dma((NX,)),
            dma((2 * NY,)),
            dma((NY,)),
        ],
        compiler_params=pltpu.CompilerParams(
            collective_id=0, has_side_effects=True, vmem_limit_bytes=40 * 2**20
        ),
        cost_estimate=pl.CostEstimate(flops=10 * 2 * ROWS * KEYS * D, bytes_accessed=2**20, transcendentals=2 * ROWS * KEYS),
    )(
        queries,
        keys,
        values,
        output_gradient,
        q_gain.reshape(1, D),
        k_gain.reshape(1, D),
        leaf_len,
        jnp.asarray(rope_table()),
    )
    return dq, dk, dv, dq_gain.reshape(D), dk_gain.reshape(D)


def solution(mesh):
    shape = dict(mesh.shape)
    if shape != {"leaf": NX * NZ * NC, "head": NY}:
        raise ValueError("another mesh")
    split = P(None, "leaf", "head")
    return jax.shard_map(
        on_device,
        mesh=mesh,
        in_specs=(split, split, split, split, P(), P(), P("leaf")),
        out_specs=(split, split, split, P(), P()),
        check_vma=False,
    )
```

```python
import jax
import jax.numpy as jnp
import numpy as np
from jax import lax
from jax.experimental import pallas as pl
from jax.experimental.pallas import tpu as pltpu
from jax.sharding import PartitionSpec as P

NEG_BIG = -1000000000.0
NORM_EPS = 1e-06
ROPE_BASE = 1000000.0
DEPTH = 6
T = 64
D = 128
G = 8
SLOTS = DEPTH + 1
KEYS = SLOTS * T
ROWS = G * T
NX, NZ, NC, NY = 4, 8, 2, 8
NQ = NZ * NC
SCALE = D ** (-0.5)
BF = jnp.bfloat16
F32 = jnp.float32
MESH = pl.DeviceIdType.MESH
AWAY = sorted(
    ((dx, dy) for dx in range(NX) for dy in range(NY) if dx or dy),
    key=lambda step: -min(step[0], NX - step[0]) - min(step[1], NY - step[1]),
)


def rope_table():
    frequency = (ROPE_BASE ** (-(np.arange(D // 2, dtype=np.float32) * 2.0 / D))).astype(np.float32)
    angles = np.arange(KEYS, dtype=np.float32)[:, None] * frequency
    return np.concatenate([np.cos(angles), np.sin(angles)], axis=1).astype(np.float32)


def spread(table):
    lane = lax.broadcasted_iota(jnp.int32, table.shape, 1)
    other = pltpu.roll(table, D // 2, axis=1)
    low = lane < D // 2
    return jnp.where(low, table, other), jnp.where(low, -other, table)


def turn(x, cosine, sine):
    return x * cosine + pltpu.roll(x, D // 2, axis=1) * sine


def unturn(x, cosine, sine):
    return x * cosine - pltpu.roll(x, D // 2, axis=1) * sine


def unit_of(x):
    factor = lax.rsqrt(jnp.mean(x * x, axis=-1, keepdims=True) + NORM_EPS)
    return x * factor, factor


def dot(a, b, contract):
    return lax.dot_general(a, b, (contract, ((), ())), preferred_element_type=F32)


def kernel(
    q_in, k_in, v_in, g_in, qg_in, kg_in, table_in, length,
    dq_out, dk_out, dv_out, dqg_out, dkg_out,
    q_raw, g_raw, own, kv, qg, kg, table,
    q_rot, q_unit, g_rows, k_rot, k_unit, v_all, part, y_q, dq_buf, dkv_buf,
    send_kv, send_sum, x_recv, z_recv, gain_send, gain_z, gain_p, gain_total,
    load_sem, store_sem, b_send, b_recv, r_send, r_recv, x_sem, xr_sem, s_send,
    gz_send, gz_recv, gp_send, gp_recv, gt_send, gt_recv,
):
    leaf = lax.axis_index("leaf")
    y = lax.axis_index("head")
    x = leaf // NQ
    q = lax.rem(leaf, NQ)
    z = q // NC
    c = lax.rem(q, NC)

    def at(xx, qq, yy=None):
        return (xx * NQ + qq, y if yy is None else yy)

    hosted = jnp.int32(1)
    for level in range(1, DEPTH + 1):
        hosted = hosted + jnp.where(lax.rem(leaf, 2**level) == 0, 1, 0)

    def remote(src, dst, send, recv, device):
        return pltpu.make_async_remote_copy(
            src_ref=src, dst_ref=dst, send_sem=send, recv_sem=recv, device_id=device, device_id_type=MESH
        )

    holder = {level: q // 2**level * 2**level + 2 ** (level - 1) for level in range(1, 5)}
    is_relay = q == 1
    plane = x * NY + y
    far_owner = jnp.logical_and(q == 0, x > 0)

    loads = [
        pltpu.make_async_copy(k_in.at[1], own.at[0], load_sem.at[0]),
        pltpu.make_async_copy(v_in.at[1], own.at[1], load_sem.at[1]),
        pltpu.make_async_copy(k_in.at[0], kv.at[0, 0], load_sem.at[2]),
        pltpu.make_async_copy(v_in.at[0], kv.at[0, 1], load_sem.at[3]),
        pltpu.make_async_copy(table_in, table, load_sem.at[4]),
        pltpu.make_async_copy(qg_in, qg, load_sem.at[5]),
        pltpu.make_async_copy(kg_in, kg, load_sem.at[6]),
        pltpu.make_async_copy(q_in, q_raw, load_sem.at[7]),
        pltpu.make_async_copy(g_in, g_raw, load_sem.at[8]),
    ]
    for load in loads:
        load.start()

    barrier = pltpu.get_barrier_semaphore()

    def greet(device):
        pl.semaphore_signal(barrier, inc=1, device_id=device, device_id_type=MESH)

    @pl.when(is_relay)
    def _():
        greet(at(2, 0))
        greet(at(x // 2 * 2 + 1, 0))

    for other in range(1, NX):
        greet(at(lax.rem(x + other, NX), q))

    @pl.when(jnp.logical_not(is_relay))
    def _():
        greet(at(x, 1))

    for level in (4, 3, 2, 1):

        @pl.when(q != holder[level])
        def _(level=level):
            greet(at(x, holder[level]))

    @pl.when(is_relay)
    def _():
        def greet_plane(n, carry):
            there = lax.rem(plane + n, NX * NY)
            greet(at(there // NY, 1, lax.rem(there, NY)))
            return carry

        lax.fori_loop(1, NX * NY, greet_plane, 0)

    early = jnp.int32(NX - 1)
    early = early + jnp.where(c == 1, 1, 0)
    early = early + jnp.where(is_relay, NQ - 1 + NX * NY - 1, 0)
    for level in (2, 3, 4):
        early = early + jnp.where(hosted == level, 2**level - 1, 0)
    early = early + jnp.where(hosted == 5, 2, 0) + jnp.where(hosted == 6, NX, 0)

    loads[0].wait()
    loads[1].wait()

    @pl.when(far_owner)
    def _():
        pl.semaphore_wait(barrier, early)

        @pl.when(x == 2)
        def _():
            for xx in range(NX):
                remote(own, kv.at[6], b_send.at[xx], b_recv.at[6], at(xx, 1)).start()

        @pl.when(x != 2)
        def _():
            for n in range(2):
                remote(own, kv.at[5], b_send.at[n], b_recv.at[5], at(x - n, 1)).start()

    @pl.when(jnp.logical_not(far_owner))
    def _():
        pl.semaphore_wait(barrier, early)

    for level in (4, 3, 2, 1):

        @pl.when(hosted == level)
        def _(level=level):
            half = 2 ** (level - 1)
            offsets = sorted((o for o in range(-half, half) if o), key=lambda o: -abs(o))
            for n, offset in enumerate(offsets):
                remote(own, kv.at[level], b_send.at[n], b_recv.at[level], at(x, q + offset)).start()
            for n in range(2):
                pltpu.make_async_copy((k_in, v_in)[n].at[1], kv.at[level, n], load_sem.at[10 + n]).start()

    others = [qq for zz in (4, 3, 5, 2, 6, 1, 7, 0) for qq in (2 * zz, 2 * zz + 1) if qq != 1]

    @pl.when(is_relay)
    def _():
        for level in (5, 6):
            remote(own, kv.at[level], b_send.at[0], b_recv.at[level], at(x, 0)).wait_recv()
            for n, qq in enumerate(others):
                remote(
                    kv.at[level], kv.at[level], b_send.at[1 + (level - 5) * 15 + n], b_recv.at[level], at(x, qq)
                ).start()

    for load in loads[4:]:
        load.wait()
    q_gain, k_gain = qg[...], kg[...]
    leaf_len = length[0]
    place = [DEPTH * T, jnp.maximum(DEPTH - hosted, 0) * T]
    live = [
        lax.broadcasted_iota(jnp.int32, (T, D), 0) < leaf_len,
        jnp.broadcast_to(hosted <= DEPTH, (T, D)),
    ]
    for kind in range(2):
        cosine, sine = spread(table[pl.ds(pl.multiple_of(place[kind], T), T), :])
        for head in range(G):
            rows = pl.ds(kind * ROWS + head * T, T)
            unit, _ = unit_of(q_raw[kind, :, head * D : (head + 1) * D].astype(F32))
            q_unit[rows, :] = unit
            q_rot[rows, :] = turn(unit * q_gain, cosine, sine).astype(BF)
            grad = g_raw[kind, :, head * D : (head + 1) * D]
            g_rows[rows, :] = jnp.where(live[kind], grad, jnp.zeros((), BF))

    loads[2].wait()
    loads[3].wait()

    def take(slot):
        rows = pl.ds(slot * T, T)
        cosine, sine = spread(table[(DEPTH - slot) * T : (DEPTH - slot + 1) * T, :])
        unit, _ = unit_of(kv[slot, 0].astype(F32))
        k_unit[rows, :] = unit
        k_rot[rows, :] = turn(unit * k_gain, cosine, sine).astype(BF)
        v_all[rows, :] = kv[slot, 1]

    take(0)
    for level in range(1, 5):

        @pl.when(q != holder[level])
        def _(level=level):
            remote(own, kv.at[level], b_send.at[0], b_recv.at[level], at(x, holder[level])).wait_recv()

        @pl.when(hosted == level)
        def _(level=level):
            for n in range(2):
                pltpu.make_async_copy((k_in, v_in)[n].at[1], kv.at[level, n], load_sem.at[10 + n]).wait()

        take(level)

    @pl.when(jnp.logical_not(is_relay))
    def _():
        for level in (5, 6):
            remote(own, kv.at[level], b_send.at[0], b_recv.at[level], at(x, 1)).wait_recv()

    take(5)
    take(6)

    key_at = lax.broadcasted_iota(jnp.int32, (T, ROWS), 0)
    row_at = lax.rem(lax.broadcasted_iota(jnp.int32, (T, ROWS), 1), T)
    ahead = key_at - row_at
    dk = dv = None
    for kind in range(2):
        rows = slice(kind * ROWS, (kind + 1) * ROWS)
        first = 0 if kind == 0 else T
        keys, vals = k_rot[first:, :], v_all[first:, :]
        queries, grads = q_rot[rows, :], g_rows[rows, :]
        scores = dot(keys, queries, ((1,), (1,))) * SCALE
        pieces = []
        for slot in range(SLOTS):
            if kind == 0:
                piece = scores[slot * T : (slot + 1) * T]
                if slot == 0:
                    seen = jnp.logical_and(ahead <= 0, key_at < leaf_len)
                    piece = jnp.where(seen, piece, NEG_BIG)
            elif slot == 0:
                continue
            else:
                piece = scores[(slot - 1) * T : slot * T]
                bound = jnp.where(hosted == slot, 0, jnp.where(hosted < slot, T, -T))
                piece = jnp.where(ahead <= bound, piece, NEG_BIG)
            pieces.append(piece)
        scores = jnp.concatenate(pieces, axis=0)
        top = jnp.max(scores, axis=0, keepdims=True)
        raised = jnp.exp(scores - top)
        probs = raised * (1.0 / jnp.sum(raised, axis=0, keepdims=True))
        probs_low = probs.astype(BF)
        dprobs = dot(vals, grads, ((1,), (1,)))
        delta = jnp.sum(probs_low.astype(F32) * dprobs, axis=0, keepdims=True)
        dscores = (probs * (dprobs - delta)).astype(BF)
        dv_part = dot(probs_low, grads, ((1,), (0,)))
        dk_part = dot(dscores, queries, ((1,), (0,))) * SCALE
        dq_turned = dot(keys, dscores, ((0,), (0,))) * SCALE
        y_q[rows, :] = jnp.transpose(dq_turned)
        for slot in range(SLOTS):
            if kind == 1 and slot == 0:
                continue
            here = slice(slot * T - first, (slot + 1) * T - first)
            if kind == 0:
                part[slot, 0] = dk_part[here]
                part[slot, 1] = dv_part[here]
            else:
                part[slot, 0] += dk_part[here]
                part[slot, 1] += dv_part[here]

    for slot in range(1, SLOTS):
        send_kv[slot - 1] = part[slot].astype(BF)

    @pl.when(x != 2)
    def _():
        n = jnp.minimum(x, 2)
        remote(send_kv.at[5], x_recv.at[n], x_sem.at[0], xr_sem.at[n], at(2, q)).start()

    @pl.when(lax.rem(x, 2) == 0)
    def _():
        remote(send_kv.at[4], x_recv.at[3], x_sem.at[1], xr_sem.at[3], at(x + 1, q)).start()

    gain_q = jnp.zeros((1, D), F32)
    for kind in range(2):
        cosine, sine = spread(table[pl.ds(pl.multiple_of(place[kind], T), T), :])
        for head in range(G):
            rows = pl.ds(kind * ROWS + head * T, T)
            back = unturn(y_q[rows, :], cosine, sine)
            y_q[rows, :] = back
            gain_q = gain_q + jnp.sum(back * q_unit[rows, :], axis=0, keepdims=True)
    gain_k = jnp.zeros((1, D), F32)
    for slot in range(SLOTS):
        cosine, sine = spread(table[(DEPTH - slot) * T : (DEPTH - slot + 1) * T, :])
        back = unturn(part[slot, 0], cosine, sine)
        gain_k = gain_k + jnp.sum(back * k_unit[slot * T : (slot + 1) * T, :], axis=0, keepdims=True)
    terms = jnp.concatenate([gain_q, gain_k], axis=0)
    gain_send[0] = terms

    @pl.when(jnp.logical_not(is_relay))
    def _():
        remote(gain_send.at[0], gain_z.at[q], gz_send, gz_recv.at[q], at(x, 1)).start()

    for level in range(1, 5):

        @pl.when(q != holder[level])
        def _(level=level):
            n = lax.rem(q, 2**level)
            remote(send_kv.at[level - 1], z_recv.at[n], r_send.at[level], r_recv.at[n], at(x, holder[level])).start()

    for kind in range(2):
        for head in range(G):
            rows = pl.ds(kind * ROWS + head * T, T)
            columns = slice(head * D, (head + 1) * D)
            raw = q_raw[kind, :, columns].astype(F32)
            unit, factor = unit_of(raw)
            scaled = y_q[rows, :] * q_gain
            inner = jnp.mean(scaled * unit, axis=-1, keepdims=True)
            dq_buf[kind, :, columns] = (factor * (scaled - unit * inner)).astype(BF)
    stores = [pltpu.make_async_copy(dq_buf, dq_out, store_sem.at[0])]
    stores[0].start()

    def key_gradient(raw, turned, start):
        cosine, sine = spread(table[pl.ds(start, T), :])
        unit, factor = unit_of(raw.astype(F32))
        scaled = unturn(turned, cosine, sine) * k_gain
        inner = jnp.mean(scaled * unit, axis=-1, keepdims=True)
        return (factor * (scaled - unit * inner)).astype(BF)

    dkv_buf[0, 0] = key_gradient(kv[0, 0], part[0, 0], DEPTH * T)
    dkv_buf[1, 0] = part[0, 1].astype(BF)

    def from_x(n):
        remote(own, x_recv.at[n], x_sem.at[0], xr_sem.at[n], at(x, q)).wait_recv()

    @pl.when(x == 2)
    def _():
        total = part[6]
        for n in range(3):
            from_x(n)
            total = total + x_recv[n].astype(F32)
        part[6] = total
        send_sum[...] = total.astype(BF)

    @pl.when(lax.rem(x, 2) == 1)
    def _():
        from_x(3)
        total = part[5] + x_recv[3].astype(F32)
        part[5] = total
        send_sum[...] = total.astype(BF)

    @pl.when(jnp.logical_and(x > 0, q != 0))
    def _():
        remote(send_sum, z_recv.at[q], s_send, r_recv.at[q], at(x, 0)).start()

    @pl.when(is_relay)
    def _():
        gain_z[1] = terms
        for qq in range(NQ):
            if qq != 1:
                remote(gain_send.at[0], gain_z.at[qq], gz_send, gz_recv.at[qq], at(x, qq)).wait_recv()
        line = gain_z[0]
        for qq in range(1, NQ):
            line = line + gain_z[qq]
        gain_send[1] = line
        gain_p[plane] = line
        for n, (dx, dy) in enumerate(AWAY):
            device = at(lax.rem(x + dx, NX), 1, lax.rem(y + dy, NY))
            remote(gain_send.at[1], gain_p.at[plane], gp_send.at[n], gp_recv.at[plane], device).start()

        def arrived(n, carry):
            there = lax.rem(plane + n, NX * NY)
            remote(gain_send.at[1], gain_p.at[there], gp_send.at[0], gp_recv.at[there], at(x, 1)).wait_recv()
            return carry

        lax.fori_loop(1, NX * NY, arrived, 0)
        total = gain_p[0]
        for n in range(1, NX * NY):
            total = total + gain_p[n]
        gain_total[...] = total
        for n, qq in enumerate(others):
            remote(gain_total, gain_total, gt_send.at[n], gt_recv, at(x, qq)).start()

    @pl.when(hosted <= DEPTH)
    def _():
        size = jnp.int32(NQ)
        for level in range(1, 4):
            size = jnp.where(hosted == level, 2**level, size)
        mine = jnp.where(hosted < 5, size // 2, 0)

        def add(n, total):
            remote(own, z_recv.at[n], s_send, r_recv.at[n], at(x, q)).wait_recv()
            return total + z_recv[n].astype(F32)

        total = lax.fori_loop(0, mine, add, part[hosted])
        total = lax.fori_loop(mine + 1, size, add, total)
        dkv_buf[0, 1] = key_gradient(own[0], total[0], pl.multiple_of(place[1], T))
        dkv_buf[1, 1] = total[1].astype(BF)

    @pl.when(hosted > DEPTH)
    def _():
        dkv_buf[0, 1] = jnp.zeros((T, D), BF)
        dkv_buf[1, 1] = jnp.zeros((T, D), BF)

    stores.append(pltpu.make_async_copy(dkv_buf.at[0], dk_out, store_sem.at[1]))
    stores.append(pltpu.make_async_copy(dkv_buf.at[1], dv_out, store_sem.at[2]))
    stores[1].start()
    stores[2].start()

    @pl.when(jnp.logical_not(is_relay))
    def _():
        remote(gain_total, gain_total, gz_send, gt_recv, at(x, 1)).wait_recv()

    stores.append(pltpu.make_async_copy(gain_total.at[pl.ds(0, 1)], dqg_out, store_sem.at[3]))
    stores.append(pltpu.make_async_copy(gain_total.at[pl.ds(1, 1)], dkg_out, store_sem.at[4]))
    stores[3].start()
    stores[4].start()

    def sent(src, sem):
        remote(src, src, sem, sem, at(x, q)).wait_send()

    @pl.when(hosted == 6)
    def _():
        for n in range(NX):
            sent(own, b_send.at[n])

    @pl.when(hosted == 5)
    def _():
        for n in range(2):
            sent(own, b_send.at[n])

    for level in range(1, 5):

        @pl.when(hosted == level)
        def _(level=level):
            for n in range(2**level - 1):
                sent(own, b_send.at[n])

    @pl.when(is_relay)
    def _():
        for n in range(1, 31):
            sent(own, b_send.at[n])

    @pl.when(x != 2)
    def _():
        sent(own, x_sem.at[0])

    @pl.when(lax.rem(x, 2) == 0)
    def _():
        sent(own, x_sem.at[1])

    @pl.when(jnp.logical_not(is_relay))
    def _():
        sent(gain_total, gz_send)

    for level in range(1, 5):

        @pl.when(q != holder[level])
        def _(level=level):
            sent(own, r_send.at[level])

    @pl.when(jnp.logical_and(x > 0, q != 0))
    def _():
        sent(own, s_send)

    @pl.when(is_relay)
    def _():
        for n in range(len(AWAY)):
            sent(gain_total, gp_send.at[n])
        for n in range(len(others)):
            sent(gain_total, gt_send.at[n])

    for store in stores:
        store.wait()


def hand_over(*refs):
    copies = [pltpu.make_async_copy(refs[n], refs[5 + n], refs[10].at[n]) for n in range(5)]
    for copy in copies:
        copy.start()
    for copy in copies:
        copy.wait()


def on_device(queries, keys, values, output_gradient, q_gain, k_gain, leaf_len):
    dma = pltpu.SemaphoreType.DMA
    anywhere = pl.BlockSpec(memory_space=pl.ANY)
    in_hbm = pl.BlockSpec(memory_space=pltpu.HBM)
    results = pl.pallas_call(
        kernel,
        name="tree_backward",
        out_shape=[
            pltpu.VMEM(queries.shape, BF),
            pltpu.VMEM(keys.shape, BF),
            pltpu.VMEM(values.shape, BF),
            pltpu.VMEM((1, D), F32),
            pltpu.VMEM((1, D), F32),
        ],
        in_specs=[anywhere] * 7 + [pl.BlockSpec(memory_space=pltpu.SMEM)],
        out_specs=[anywhere] * 5,
        scratch_shapes=[
            pltpu.VMEM((2, T, G * D), BF),
            pltpu.VMEM((2, T, G * D), BF),
            pltpu.VMEM((2, T, D), BF),
            pltpu.VMEM((SLOTS, 2, T, D), BF),
            pltpu.VMEM((1, D), F32),
            pltpu.VMEM((1, D), F32),
            pltpu.VMEM((KEYS, D), F32),
            pltpu.VMEM((2 * ROWS, D), BF),
            pltpu.VMEM((2 * ROWS, D), F32),
            pltpu.VMEM((2 * ROWS, D), BF),
            pltpu.VMEM((KEYS, D), BF),
            pltpu.VMEM((KEYS, D), F32),
            pltpu.VMEM((KEYS, D), BF),
            pltpu.VMEM((SLOTS, 2, T, D), F32),
            pltpu.VMEM((2 * ROWS, D), F32),
            pltpu.VMEM((2, T, G * D), BF),
            pltpu.VMEM((2, 2, T, D), BF),
            pltpu.VMEM((DEPTH, 2, T, D), BF),
            pltpu.VMEM((2, T, D), BF),
            pltpu.VMEM((4, 2, T, D), BF),
            pltpu.VMEM((NQ, 2, T, D), BF),
            pltpu.VMEM((2, 2, D), F32),
            pltpu.VMEM((NQ, 2, D), F32),
            pltpu.VMEM((NX * NY, 2, D), F32),
            pltpu.VMEM((2, D), F32),
            dma((12,)),
            dma((5,)),
            dma((31,)),
            dma((SLOTS,)),
            dma((5,)),
            dma((NQ,)),
            dma((2,)),
            dma((4,)),
            dma(()),
            dma(()),
            dma((NQ,)),
            dma((NX * NY - 1,)),
            dma((NX * NY,)),
            dma((NQ - 1,)),
            dma(()),
        ],
        compiler_params=pltpu.CompilerParams(
            collective_id=0, has_side_effects=True, vmem_limit_bytes=40 * 2**20
        ),
        cost_estimate=pl.CostEstimate(flops=10 * 2 * ROWS * KEYS * D, bytes_accessed=2**20, transcendentals=2 * ROWS * KEYS),
    )(
        *(
            pltpu.with_memory_space_constraint(array, pltpu.HBM)
            for array in (
                queries,
                keys,
                values,
                output_gradient,
                q_gain.reshape(1, D),
                k_gain.reshape(1, D),
                jnp.asarray(rope_table()),
            )
        ),
        leaf_len,
    )
    dq, dk, dv, dq_gain, dk_gain = pl.pallas_call(
        hand_over,
        name="hand_over",
        out_shape=[jax.ShapeDtypeStruct(r.shape, r.dtype) for r in results],
        in_specs=[anywhere] * 5,
        out_specs=[in_hbm] * 5,
        scratch_shapes=[dma((5,))],
        compiler_params=pltpu.CompilerParams(vmem_limit_bytes=8 * 2**20),
    )(*(pltpu.with_memory_space_constraint(r, pltpu.VMEM) for r in results))
    return dq, dk, dv, dq_gain.reshape(D), dk_gain.reshape(D)


def solution(mesh):
    shape = dict(mesh.shape)
    if shape != {"leaf": NX * NZ * NC, "head": NY}:
        raise ValueError("another mesh")
    split = P(None, "leaf", "head")
    return jax.shard_map(
        on_device,
        mesh=mesh,
        in_specs=(split, split, split, split, P(), P(), P("leaf")),
        out_specs=(split, split, split, P(), P()),
        check_vma=False,
    )
```

```python
import jax
import jax.numpy as jnp
import numpy as np
from jax import lax
from jax.experimental import pallas as pl
from jax.experimental.pallas import tpu as pltpu
from jax.sharding import PartitionSpec as P

NEG_BIG = -1000000000.0
NORM_EPS = 1e-06
ROPE_BASE = 1000000.0
DEPTH = 6
T = 64
D = 128
G = 8
SLOTS = DEPTH + 1
KEYS = SLOTS * T
NEAR = 4
ROWS = G * T
NX, NZ, NC, NY = 4, 8, 2, 8
NQ = NZ * NC
SCALE = D ** (-0.5)
BF = jnp.bfloat16
F32 = jnp.float32
MESH = pl.DeviceIdType.MESH
SERVED = ((1, (13, 15, 3)), (5, (11, 9, 7)))
AWAY = sorted(
    ((dx, dy) for dx in range(NX) for dy in range(NY) if dx or dy),
    key=lambda step: -min(step[0], NX - step[0]) - min(step[1], NY - step[1]),
)


def rope_table():
    frequency = (ROPE_BASE ** (-(np.arange(D // 2, dtype=np.float32) * 2.0 / D))).astype(np.float32)
    angles = np.arange(KEYS, dtype=np.float32)[:, None] * frequency
    return np.concatenate([np.cos(angles), np.sin(angles)], axis=1).astype(np.float32)


def spread(table):
    lane = lax.broadcasted_iota(jnp.int32, table.shape, 1)
    other = pltpu.roll(table, D // 2, axis=1)
    low = lane < D // 2
    return jnp.where(low, table, other), jnp.where(low, -other, table)


def turn(x, cosine, sine):
    return x * cosine + pltpu.roll(x, D // 2, axis=1) * sine


def unturn(x, cosine, sine):
    return x * cosine - pltpu.roll(x, D // 2, axis=1) * sine


def unit_of(x):
    factor = lax.rsqrt(jnp.mean(x * x, axis=-1, keepdims=True) + NORM_EPS)
    return x * factor, factor


def dot(a, b, contract):
    return lax.dot_general(a, b, (contract, ((), ())), preferred_element_type=F32)


def kernel(
    q_in, k_in, v_in, g_in, qg_in, kg_in, table_in, length,
    dq_out, dk_out, dv_out, dqg_out, dkg_out,
    q_raw, g_raw, own, kv, qg, kg, table,
    q_rot, g_rows, k_rot, v_all, wq_cos, wq_sin, wk_cos, wk_sin, near_e, near_d, near_s, probs, dscores, part, y_q, ballast,
    send_kv, send_sum, x_recv, z_recv, gain_send, gain_z, gain_p, gain_total,
    load_sem, b_send, b_recv, r_send, r_recv, x_sem, xr_sem, s_send,
    gz_send, gz_recv, gp_send, gp_recv, gt_send, gt_recv,
):
    leaf = lax.axis_index("leaf")
    y = lax.axis_index("head")
    x = leaf // NQ
    q = lax.rem(leaf, NQ)
    z = q // NC
    c = lax.rem(q, NC)

    def at(xx, qq, yy=None):
        return (xx * NQ + qq, y if yy is None else yy)

    hosted = jnp.int32(1)
    for level in range(1, DEPTH + 1):
        hosted = hosted + jnp.where(lax.rem(leaf, 2**level) == 0, 1, 0)

    def remote(src, dst, send, recv, device):
        return pltpu.make_async_remote_copy(
            src_ref=src, dst_ref=dst, send_sem=send, recv_sem=recv, device_id=device, device_id_type=MESH
        )

    def settle(count, sem):
        blocks = ballast.at[pl.ds(0, count)]
        pltpu.make_async_copy(blocks, blocks, sem).wait()

    holder = {level: q // 2**level * 2**level + 2 ** (level - 1) for level in range(1, 5)}
    is_relay = q == 1
    is_near = q == 5
    is_second = q == 9
    far_owner = jnp.logical_and(q == 0, x > 0)
    plane = x * NY + y

    def among(places):
        here = q == places[0]
        for place in places[1:]:
            here = jnp.logical_or(here, q == place)
        return here

    barrier = pltpu.get_barrier_semaphore()

    def greet(device):
        pl.semaphore_signal(barrier, inc=1, device_id=device, device_id_type=MESH)

    for relay, served in SERVED:

        @pl.when(among(served))
        def _(relay=relay):
            greet(at(x, relay))

    @pl.when(z > 4)
    def _():
        greet(at(x, 9))

    @pl.when(jnp.logical_or(z < 4, is_second))
    def _():
        greet(at(x, 8))

    for level in (3, 2, 1):

        @pl.when(q != holder[level])
        def _(level=level):
            greet(at(x, holder[level]))

    @pl.when(jnp.logical_or(is_relay, is_near))
    def _():
        greet(at(2, 0))
        greet(at(x // 2 * 2 + 1, 0))

    for other in range(1, NX):
        greet(at(lax.rem(x + other, NX), q))

    early = jnp.int32(NX - 1)
    early = early + jnp.where(c == 1, 1, 0)
    early = early + jnp.where(is_relay, 3 + NX * NY - 1, 0) + jnp.where(is_near, 3, 0)
    early = early + jnp.where(is_second, 6, 0)
    for level, count in ((2, 3), (3, 7), (4, 9), (5, 4), (6, 2 * NX)):
        early = early + jnp.where(hosted == level, count, 0)

    loads = [
        pltpu.make_async_copy(k_in.at[1], own.at[0], load_sem.at[0]),
        pltpu.make_async_copy(v_in.at[1], own.at[1], load_sem.at[0]),
        pltpu.make_async_copy(k_in.at[0], kv.at[0, 0], load_sem.at[1]),
        pltpu.make_async_copy(v_in.at[0], kv.at[0, 1], load_sem.at[1]),
        pltpu.make_async_copy(table_in, table, load_sem.at[2]),
        pltpu.make_async_copy(qg_in, qg, load_sem.at[3]),
        pltpu.make_async_copy(kg_in, kg, load_sem.at[4]),
        pltpu.make_async_copy(q_in, q_raw, load_sem.at[5]),
        pltpu.make_async_copy(g_in, g_raw, load_sem.at[6]),
    ]
    for load in loads:
        load.start()

    @pl.when(is_relay)
    def _():
        def greet_plane(n, carry):
            there = lax.rem(plane + n, NX * NY)
            greet(at(there // NY, 1, lax.rem(there, NY)))
            return carry

        lax.fori_loop(1, NX * NY, greet_plane, 0)

    settle(1, load_sem.at[0])

    pl.semaphore_wait(barrier, early)

    @pl.when(jnp.logical_and(far_owner, x == 2))
    def _():
        for relay in (5, 1):
            for xx in range(NX):
                remote(own, kv.at[6], b_send, b_recv.at[6], at(xx, relay)).start()

    @pl.when(jnp.logical_and(far_owner, x != 2))
    def _():
        for relay in (5, 1):
            for n in range(2):
                remote(own, kv.at[5], b_send, b_recv.at[5], at(x - n, relay)).start()

    for level in (4, 3, 2, 1):

        @pl.when(hosted == level)
        def _(level=level):
            half = 2 ** (level - 1)
            offsets = sorted((o for o in range(-half, half) if o), key=lambda o: -abs(o))
            if level == 4:
                offsets = [1] + [o for o in offsets if o < 0]
            for offset in offsets:
                remote(own, kv.at[level], b_send, b_recv.at[level], at(x, q + offset)).start()
            for n in range(2):
                pltpu.make_async_copy((k_in, v_in)[n].at[1], kv.at[level, n], load_sem.at[7]).start()

    @pl.when(is_second)
    def _():
        remote(own, kv.at[4], b_send, b_recv.at[4], at(x, 8)).wait_recv()
        for qq in (15, 14, 13, 12, 11, 10):
            remote(kv.at[4], kv.at[4], b_send, b_recv.at[4], at(x, qq)).start()

    top_two = kv.at[pl.ds(5, 2)]

    for relay, served in SERVED:

        @pl.when(q == relay)
        def _(relay=relay, served=served):
            for level in (5, 6):
                remote(own, kv.at[level], b_send, b_recv.at[level], at(x, 0)).wait_recv()
            for qq in (*served, relay - 1):
                remote(top_two, top_two, b_send, b_recv.at[5], at(x, qq)).start()

    for load in loads[4:]:
        load.wait()
    q_gain, k_gain = qg[...], kg[...]
    leaf_len = length[0]
    place = [DEPTH * T, jnp.maximum(DEPTH - hosted, 0) * T]
    live = [
        lax.broadcasted_iota(jnp.int32, (T, D), 0) < leaf_len,
        jnp.broadcast_to(hosted <= DEPTH, (T, D)),
    ]
    for kind in range(2):
        cosine, sine = spread(table[pl.ds(pl.multiple_of(place[kind], T), T), :])
        w_cos, w_sin = [], []
        for head in range(G):
            rows = pl.ds(kind * ROWS + head * T, T)
            unit, _ = unit_of(q_raw[kind, :, head * D : (head + 1) * D].astype(F32))
            q_rot[rows, :] = turn(unit * q_gain, cosine, sine).astype(BF)
            w_cos.append(unit * cosine)
            w_sin.append(pltpu.roll(unit * sine, D // 2, axis=1))
            if head % 2:
                pair = slice(kind * ROWS + (head - 1) * T, kind * ROWS + (head + 1) * T)
                wq_cos[:, pair] = jnp.transpose(jnp.concatenate(w_cos[-2:], axis=0))
                wq_sin[:, pair] = jnp.transpose(jnp.concatenate(w_sin[-2:], axis=0))
            grad = g_raw[kind, :, head * D : (head + 1) * D]
            g_rows[rows, :] = jnp.where(live[kind], grad, jnp.zeros((), BF))

    settle(1, load_sem.at[1])

    def take(slot):
        rows = pl.ds(slot * T, T)
        cosine, sine = spread(table[(DEPTH - slot) * T : (DEPTH - slot + 1) * T, :])
        unit, _ = unit_of(kv[slot, 0].astype(F32))
        wk_cos[rows, :] = unit * cosine
        wk_sin[rows, :] = pltpu.roll(unit * sine, D // 2, axis=1)
        k_rot[rows, :] = turn(unit * k_gain, cosine, sine).astype(BF)
        v_all[rows, :] = kv[slot, 1]

    def from_holder(level):
        @pl.when(jnp.logical_and(q != holder[level], jnp.logical_not(jnp.logical_and(is_second, level == 4))))
        def _():
            remote(own, kv.at[level], b_send, b_recv.at[level], at(x, holder[level])).wait_recv()

        @pl.when(hosted == level)
        def _():
            settle(1, load_sem.at[7])

    take(0)
    for level in (1, 2, 3):
        from_holder(level)
        take(level)

    key_at = lax.broadcasted_iota(jnp.int32, (T, ROWS), 0)
    row_at = lax.rem(lax.broadcasted_iota(jnp.int32, (T, ROWS), 1), T)
    ahead = key_at - row_at

    def partial(first, last, kind):
        rows = slice(kind * ROWS, (kind + 1) * ROWS)
        slots = slice(first * T, last * T)
        scores = dot(k_rot[slots, :], q_rot[rows, :], ((1,), (1,))) * SCALE
        pieces = []
        for slot in range(first, last):
            piece = scores[(slot - first) * T : (slot - first + 1) * T]
            if kind == 0:
                if slot == 0:
                    seen = jnp.logical_and(ahead <= 0, key_at < leaf_len)
                    piece = jnp.where(seen, piece, NEG_BIG)
            elif slot == 0:
                piece = jnp.full_like(piece, NEG_BIG)
            else:
                bound = jnp.where(hosted == slot, 0, jnp.where(hosted < slot, T, -T))
                piece = jnp.where(ahead <= bound, piece, NEG_BIG)
            pieces.append(piece)
        scores = jnp.concatenate(pieces, axis=0)
        top = jnp.max(scores, axis=0, keepdims=True)
        raised = jnp.exp(scores - top)
        dprobs = dot(v_all[slots, :], g_rows[rows, :], ((1,), (1,)))
        return (
            raised,
            dprobs,
            top,
            jnp.sum(raised, axis=0, keepdims=True),
            jnp.sum(raised * dprobs, axis=0, keepdims=True),
        )

    for kind in range(2):
        rows = slice(kind * ROWS, (kind + 1) * ROWS)
        near_e[:, rows], near_d[:, rows], near_s[0:1, rows], near_s[1:2, rows], near_s[2:3, rows] = partial(0, NEAR, kind)

    @pl.when(jnp.logical_not(jnp.logical_or(is_relay, is_near)))
    def _():
        remote(top_two, top_two, b_send, b_recv.at[5], at(x, 1)).wait_recv()

        @pl.when(c == 1)
        def _():
            remote(top_two, top_two, b_send, b_recv.at[5], at(x, q - 1)).start()

    take(5)
    take(6)
    from_holder(4)
    take(4)

    for kind in range(2):
        rows = slice(kind * ROWS, (kind + 1) * ROWS)
        far_e, far_d, far_top, far_sum, far_delta = partial(NEAR, SLOTS, kind)
        near_top = near_s[0:1, rows]
        top = jnp.maximum(near_top, far_top)
        near_f, far_f = jnp.exp(near_top - top), jnp.exp(far_top - top)
        over = 1.0 / (near_s[1:2, rows] * near_f + far_sum * far_f)
        near_f, far_f = near_f * over, far_f * over
        delta = near_s[2:3, rows] * near_f + far_delta * far_f
        near = near_e[:, rows] * near_f
        far = far_e * far_f
        probs[: NEAR * T, rows] = near.astype(BF)
        probs[NEAR * T :, rows] = far.astype(BF)
        dscores[: NEAR * T, rows] = (near * (near_d[:, rows] - delta)).astype(BF)
        dscores[NEAR * T :, rows] = (far * (far_d - delta)).astype(BF)
    dk_all = dot(dscores[...], q_rot[...], ((1,), (0,))) * SCALE
    dv_all = dot(probs[...], g_rows[...], ((1,), (0,)))
    dq_turned = dot(k_rot[...], dscores[...], ((0,), (0,))) * SCALE
    for slot in range(SLOTS):
        part[slot, 0] = dk_all[slot * T : (slot + 1) * T]
        part[slot, 1] = dv_all[slot * T : (slot + 1) * T]

    for slot in range(1, SLOTS):
        send_kv[slot - 1] = part[slot].astype(BF)

    @pl.when(x != 2)
    def _():
        n = jnp.minimum(x, 2)
        remote(send_kv.at[5], x_recv.at[n], x_sem.at[0], xr_sem, at(2, q)).start()

    @pl.when(lax.rem(x, 2) == 0)
    def _():
        remote(send_kv.at[4], x_recv.at[3], x_sem.at[1], xr_sem, at(x + 1, q)).start()

    straight, crossed = dq_turned * wq_cos[...], dq_turned * wq_sin[...]
    both = straight - jnp.concatenate([crossed[D // 2 :], crossed[: D // 2]], axis=0)
    lanes = both[:, :D]
    for n in range(1, 2 * ROWS // D):
        lanes = lanes + both[:, n * D : (n + 1) * D]
    gain_q = jnp.sum(jnp.transpose(lanes), axis=0, keepdims=True)
    gain_k = jnp.sum(dk_all * wk_cos[...], axis=0, keepdims=True) - pltpu.roll(
        jnp.sum(dk_all * wk_sin[...], axis=0, keepdims=True), D // 2, axis=1
    )
    terms = jnp.concatenate([gain_q, gain_k], axis=0)
    gain_send[0] = terms

    @pl.when(jnp.logical_not(is_relay))
    def _():
        remote(gain_send.at[0], gain_z.at[lax.rem(q + NQ - 2, NQ)], gz_send, gz_recv, at(x, 1)).start()

    for level in range(1, 5):

        @pl.when(q != holder[level])
        def _(level=level):
            n = lax.rem(q, 2**level)
            n = jnp.where(n > 2 ** (level - 1), n - 1, n)
            remote(send_kv.at[level - 1], z_recv.at[n], r_send, r_recv, at(x, holder[level])).start()

    y_q[...] = jnp.transpose(dq_turned)
    for kind in range(2):
        cosine, sine = spread(table[pl.ds(pl.multiple_of(place[kind], T), T), :])
        for head in range(G):
            rows = pl.ds(kind * ROWS + head * T, T)
            columns = slice(head * D, (head + 1) * D)
            raw = q_raw[kind, :, columns].astype(F32)
            unit, factor = unit_of(raw)
            scaled = unturn(y_q[rows, :], cosine, sine) * q_gain
            inner = jnp.mean(scaled * unit, axis=-1, keepdims=True)
            dq_out[kind, :, columns] = (factor * (scaled - unit * inner)).astype(BF)

    def key_gradient(raw, turned, start):
        cosine, sine = spread(table[pl.ds(start, T), :])
        unit, factor = unit_of(raw.astype(F32))
        scaled = unturn(turned, cosine, sine) * k_gain
        inner = jnp.mean(scaled * unit, axis=-1, keepdims=True)
        return (factor * (scaled - unit * inner)).astype(BF)

    dk_out[0] = key_gradient(kv[0, 0], part[0, 0], DEPTH * T)
    dv_out[0] = part[0, 1].astype(BF)

    @pl.when(x == 2)
    def _():
        settle(3, xr_sem)
        total = part[6]
        for n in range(3):
            total = total + x_recv[n].astype(F32)
        part[6] = total
        send_sum[...] = total.astype(BF)

    @pl.when(lax.rem(x, 2) == 1)
    def _():
        settle(1, xr_sem)
        total = part[5] + x_recv[3].astype(F32)
        part[5] = total
        send_sum[...] = total.astype(BF)

    @pl.when(jnp.logical_and(x > 0, q != 0))
    def _():
        remote(send_sum, z_recv.at[q - 1], s_send, r_recv, at(x, 0)).start()

    @pl.when(among((1, 5, 9)))
    def _():
        settle(9, b_send)

    @pl.when(among((3, 7, 11, 13, 15)))
    def _():
        settle(3, b_send)

    for level, count in ((2, 3), (3, 7), (4, 9), (5, 4), (6, 2 * NX)):

        @pl.when(hosted == level)
        def _(count=count):
            settle(count, b_send)

    @pl.when(hosted <= DEPTH)
    def _():
        size = jnp.int32(NQ)
        for level in range(1, 4):
            size = jnp.where(hosted == level, 2**level, size)
        for level in range(1, DEPTH + 1):

            @pl.when(hosted == level)
            def _(level=level):
                settle(2 ** min(level, 4) - 1, r_recv)

        def add(n, total):
            return total + z_recv[n].astype(F32)

        total = lax.fori_loop(0, size - 1, add, part[hosted])
        dk_out[1] = key_gradient(own[0], total[0], pl.multiple_of(place[1], T))
        dv_out[1] = total[1].astype(BF)

    @pl.when(hosted > DEPTH)
    def _():
        dk_out[1] = jnp.zeros((T, D), BF)
        dv_out[1] = jnp.zeros((T, D), BF)

    @pl.when(is_relay)
    def _():
        gain_z[NQ - 1] = terms
        lines = gain_z.at[pl.ds(0, NQ - 1)]
        pltpu.make_async_copy(lines, lines, gz_recv).wait()
        line = gain_z[0]
        for qq in range(1, NQ):
            line = line + gain_z[qq]
        gain_send[1] = line
        gain_p[plane] = line
        for dx, dy in AWAY:
            device = at(lax.rem(x + dx, NX), 1, lax.rem(y + dy, NY))
            remote(gain_send.at[1], gain_p.at[plane], gp_send, gp_recv, device).start()

        away = gain_p.at[pl.ds(0, len(AWAY))]
        pltpu.make_async_copy(away, away, gp_recv).wait()
        total = gain_p[0]
        for n in range(1, NX * NY):
            total = total + gain_p[n]
        gain_total[...] = total
        for qq in (3, 5, 0):
            remote(gain_total, gain_total, gt_send, gt_recv, at(x, qq)).start()
        pltpu.make_async_copy(away, away, gp_send).wait()

    @pl.when(x != 2)
    def _():
        settle(1, x_sem.at[0])

    @pl.when(lax.rem(x, 2) == 0)
    def _():
        settle(1, x_sem.at[1])

    @pl.when(hosted < 5)
    def _():
        settle(3, r_send)

    @pl.when(hosted >= 5)
    def _():
        settle(4, r_send)

    @pl.when(jnp.logical_and(x > 0, q != 0))
    def _():
        settle(1, s_send)

    @pl.when(jnp.logical_not(is_relay))
    def _():
        pltpu.make_async_copy(gain_total, gain_total, gz_send).wait()
        pltpu.make_async_copy(gain_total, gain_total, gt_recv).wait()

    def pass_on(when, targets):
        @pl.when(when)
        def _():
            for qq in targets:
                remote(gain_total, gain_total, gt_send, gt_recv, at(x, qq)).start()

    pass_on(q == 0, (15, 13, 11))
    pass_on(q == 5, (7, 9, 4))
    pass_on(jnp.logical_and(c == 1, jnp.logical_and(q != 5, q != 1)), (q - 1,))
    dqg_out[...] = gain_total[0:1]
    dkg_out[...] = gain_total[1:2]

    def passed(when, count):
        @pl.when(when)
        def _():
            sent = gain_z.at[pl.ds(0, count)]
            pltpu.make_async_copy(sent, sent, gt_send).wait()

    passed(jnp.logical_or(q < 2, q == 5), 3)
    passed(jnp.logical_and(c == 1, jnp.logical_and(q != 5, q != 1)), 1)


def hand_over(*refs):
    copies = [pltpu.make_async_copy(refs[n], refs[5 + n], refs[10].at[n]) for n in range(5)]
    for copy in copies:
        copy.start()
    for copy in copies:
        copy.wait()


def on_device(queries, keys, values, output_gradient, q_gain, k_gain, leaf_len):
    dma = pltpu.SemaphoreType.DMA
    anywhere = pl.BlockSpec(memory_space=pl.ANY)
    in_hbm = pl.BlockSpec(memory_space=pltpu.HBM)
    results = pl.pallas_call(
        kernel,
        name="tree_backward",
        out_shape=[
            pltpu.VMEM(queries.shape, BF),
            pltpu.VMEM(keys.shape, BF),
            pltpu.VMEM(values.shape, BF),
            pltpu.VMEM((1, D), F32),
            pltpu.VMEM((1, D), F32),
        ],
        in_specs=[anywhere] * 7 + [pl.BlockSpec(memory_space=pltpu.SMEM)],
        out_specs=[pl.BlockSpec(memory_space=pltpu.VMEM)] * 5,
        scratch_shapes=[
            pltpu.VMEM((2, T, G * D), BF),
            pltpu.VMEM((2, T, G * D), BF),
            pltpu.VMEM((2, T, D), BF),
            pltpu.VMEM((SLOTS, 2, T, D), BF),
            pltpu.VMEM((1, D), F32),
            pltpu.VMEM((1, D), F32),
            pltpu.VMEM((KEYS, D), F32),
            pltpu.VMEM((2 * ROWS, D), BF),
            pltpu.VMEM((2 * ROWS, D), BF),
            pltpu.VMEM((KEYS, D), BF),
            pltpu.VMEM((KEYS, D), BF),
            pltpu.VMEM((D, 2 * ROWS), F32),
            pltpu.VMEM((D, 2 * ROWS), F32),
            pltpu.VMEM((KEYS, D), F32),
            pltpu.VMEM((KEYS, D), F32),
            pltpu.VMEM((NEAR * T, 2 * ROWS), F32),
            pltpu.VMEM((NEAR * T, 2 * ROWS), F32),
            pltpu.VMEM((8, 2 * ROWS), F32),
            pltpu.VMEM((KEYS, 2 * ROWS), BF),
            pltpu.VMEM((KEYS, 2 * ROWS), BF),
            pltpu.VMEM((SLOTS, 2, T, D), F32),
            pltpu.VMEM((2 * ROWS, D), F32),
            pltpu.VMEM((NQ, 2, T, D), BF),
            pltpu.VMEM((DEPTH, 2, T, D), BF),
            pltpu.VMEM((2, T, D), BF),
            pltpu.VMEM((4, 2, T, D), BF),
            pltpu.VMEM((NQ, 2, T, D), BF),
            pltpu.VMEM((2, 2, D), F32),
            pltpu.VMEM((NQ, 2, D), F32),
            pltpu.VMEM((NX * NY, 2, D), F32),
            pltpu.VMEM((2, D), F32),
            dma((8,)),
            dma(()),
            dma((SLOTS,)),
            dma(()),
            dma(()),
            dma((2,)),
            dma(()),
            dma(()),
            dma(()),
            dma(()),
            dma(()),
            dma(()),
            dma(()),
            dma(()),
        ],
        compiler_params=pltpu.CompilerParams(
            collective_id=0, has_side_effects=True, vmem_limit_bytes=40 * 2**20
        ),
        cost_estimate=pl.CostEstimate(flops=10 * 2 * ROWS * KEYS * D, bytes_accessed=2**20, transcendentals=2 * ROWS * KEYS),
    )(
        *(
            pltpu.with_memory_space_constraint(array, pltpu.HBM)
            for array in (
                queries,
                keys,
                values,
                output_gradient,
                q_gain.reshape(1, D),
                k_gain.reshape(1, D),
                jnp.asarray(rope_table()),
            )
        ),
        leaf_len,
    )
    dq, dk, dv, dq_gain, dk_gain = pl.pallas_call(
        hand_over,
        name="hand_over",
        out_shape=[jax.ShapeDtypeStruct(r.shape, r.dtype) for r in results],
        in_specs=[anywhere] * 5,
        out_specs=[in_hbm] * 5,
        scratch_shapes=[dma((5,))],
        compiler_params=pltpu.CompilerParams(vmem_limit_bytes=8 * 2**20),
    )(*(pltpu.with_memory_space_constraint(r, pltpu.VMEM) for r in results))
    return dq, dk, dv, dq_gain.reshape(D), dk_gain.reshape(D)


def solution(mesh):
    shape = dict(mesh.shape)
    if shape != {"leaf": NX * NZ * NC, "head": NY}:
        raise ValueError("another mesh")
    split = P(None, "leaf", "head")
    return jax.shard_map(
        on_device,
        mesh=mesh,
        in_specs=(split, split, split, split, P(), P(), P("leaf")),
        out_specs=(split, split, split, P(), P()),
        check_vma=False,
    )
```

```python
import jax
import jax.numpy as jnp
import numpy as np
from jax import lax
from jax.experimental import pallas as pl
from jax.experimental.pallas import tpu as pltpu
from jax.sharding import PartitionSpec as P

NEG_BIG = -1000000000.0
NORM_EPS = 1e-06
ROPE_BASE = 1000000.0
DEPTH = 6
T = 64
D = 128
G = 8
SLOTS = DEPTH + 1
KEYS = SLOTS * T
NEAR = 4
ROWS = G * T
NX, NZ, NC, NY = 4, 8, 2, 8
NQ = NZ * NC
SCALE = D ** (-0.5)
BF = jnp.bfloat16
F32 = jnp.float32
MESH = pl.DeviceIdType.MESH
SERVED = ((1, (13, 15, 3)), (5, (11, 9, 7)))
AWAY = sorted(
    ((dx, dy) for dx in range(NX) for dy in range(NY) if dx or dy),
    key=lambda step: -min(step[0], NX - step[0]) - min(step[1], NY - step[1]),
)


def rope_table():
    frequency = (ROPE_BASE ** (-(np.arange(D // 2, dtype=np.float32) * 2.0 / D))).astype(np.float32)
    angles = np.arange(KEYS, dtype=np.float32)[:, None] * frequency
    return np.concatenate([np.cos(angles), np.sin(angles)], axis=1).astype(np.float32)


def spread(table):
    lane = lax.broadcasted_iota(jnp.int32, table.shape, 1)
    other = pltpu.roll(table, D // 2, axis=1)
    low = lane < D // 2
    return jnp.where(low, table, other), jnp.where(low, -other, table)


def turn(x, cosine, sine):
    return x * cosine + pltpu.roll(x, D // 2, axis=1) * sine


def unturn(x, cosine, sine):
    return x * cosine - pltpu.roll(x, D // 2, axis=1) * sine


def unit_of(x):
    factor = lax.rsqrt(jnp.mean(x * x, axis=-1, keepdims=True) + NORM_EPS)
    return x * factor, factor


def dot(a, b, contract):
    return lax.dot_general(a, b, (contract, ((), ())), preferred_element_type=F32)


def kernel(
    q_in, k_in, v_in, g_in, qg_in, kg_in, table_in, length,
    dq_out, dk_out, dv_out, dqg_out, dkg_out,
    q_raw, g_raw, own, kv, qg, kg, table,
    q_rot, g_rows, k_rot, v_all, wq_cos, wq_sin, wk_cos, wk_sin, near_e, near_d, near_s, probs, dscores, part, y_q, ballast,
    send_kv, send_sum, x_recv, z_recv, gain_send, gain_z, gain_p, gain_total,
    load_sem, b_send, b_recv, r_send, r_recv, x_sem, xr_sem, s_send,
    gz_send, gz_recv, gp_send, gp_recv, gt_send, gt_recv,
):
    leaf = lax.axis_index("leaf")
    y = lax.axis_index("head")
    x = leaf // NQ
    q = lax.rem(leaf, NQ)
    z = q // NC
    c = lax.rem(q, NC)

    def at(xx, qq, yy=None):
        return (xx * NQ + qq, y if yy is None else yy)

    hosted = jnp.int32(1)
    for level in range(1, DEPTH + 1):
        hosted = hosted + jnp.where(lax.rem(leaf, 2**level) == 0, 1, 0)

    def remote(src, dst, send, recv, device):
        return pltpu.make_async_remote_copy(
            src_ref=src, dst_ref=dst, send_sem=send, recv_sem=recv, device_id=device, device_id_type=MESH
        )

    def settle(count, sem):
        blocks = ballast.at[pl.ds(0, count)]
        pltpu.make_async_copy(blocks, blocks, sem).wait()

    holder = {level: q // 2**level * 2**level + 2 ** (level - 1) for level in range(1, 5)}
    is_relay = q == 1
    is_near = q == 5
    is_extra = jnp.logical_and(leaf == 3, y == 0)
    is_second = q == 9
    far_owner = jnp.logical_and(q == 0, x > 0)
    plane = x * NY + y
    mirror = (NZ - 1 - z) * NC + c
    low = jnp.where(z < 4, q, mirror)
    sends_six = jnp.logical_or(z >= 4, x != 2)
    sends_five = jnp.logical_or(z >= 4, lax.rem(x, 2) == 0)

    def among(places):
        here = q == places[0]
        for place in places[1:]:
            here = jnp.logical_or(here, q == place)
        return here

    barrier = pltpu.get_barrier_semaphore()

    def greet(device):
        pl.semaphore_signal(barrier, inc=1, device_id=device, device_id_type=MESH)

    for relay, served in SERVED:

        @pl.when(among(served))
        def _(relay=relay):
            greet(at(x, relay))

    @pl.when(among((10, 11, 12, 13)))
    def _():
        greet(at(x, 9))

    @pl.when(z == NZ - 1)
    def _():
        greet(at(x, 13))

    @pl.when(jnp.logical_or(z < 4, is_second))
    def _():
        greet(at(x, 8))

    for level in (3, 2, 1):

        @pl.when(q != holder[level])
        def _(level=level):
            greet(at(x, holder[level]))

    @pl.when(jnp.logical_or(is_relay, is_near))
    def _():
        greet(at(2, 0))
        greet(at(x // 2 * 2 + 1, 0))

    @pl.when(jnp.logical_and(z < 4, x == 2))
    def _():
        for xx in range(NX):
            greet(at(xx, mirror))
        for xx in (0, 1, 3):
            greet(at(xx, q))

    @pl.when(jnp.logical_and(z < 4, lax.rem(x, 2) == 1))
    def _():
        greet(at(x, mirror))
        greet(at(x - 1, mirror))
        greet(at(x - 1, q))

    early = jnp.where(c == 1, 1, 0)
    early = early + jnp.where(sends_six, 1, 0) + jnp.where(sends_five, 1, 0)
    early = early + jnp.where(is_relay, 3 + NX * NY, 0) + jnp.where(is_near, 3, 0)
    early = early + jnp.where(is_second, 4, 0) + jnp.where(q == 13, 2, 0)
    for level, count in ((2, 3), (3, 7), (4, 9), (5, 4), (6, 2 * NX)):
        early = early + jnp.where(hosted == level, count, 0)

    loads = [
        pltpu.make_async_copy(k_in.at[1], own.at[0], load_sem.at[0]),
        pltpu.make_async_copy(v_in.at[1], own.at[1], load_sem.at[0]),
        pltpu.make_async_copy(k_in.at[0], kv.at[0, 0], load_sem.at[1]),
        pltpu.make_async_copy(v_in.at[0], kv.at[0, 1], load_sem.at[1]),
        pltpu.make_async_copy(table_in, table, load_sem.at[2]),
        pltpu.make_async_copy(qg_in, qg, load_sem.at[3]),
        pltpu.make_async_copy(kg_in, kg, load_sem.at[4]),
        pltpu.make_async_copy(q_in, q_raw, load_sem.at[5]),
        pltpu.make_async_copy(g_in, g_raw, load_sem.at[6]),
    ]
    for load in loads:
        load.start()

    @pl.when(is_relay)
    def _():
        def greet_plane(n, carry):
            there = lax.rem(plane + n, NX * NY)
            greet(at(there // NY, 1, lax.rem(there, NY)))
            return carry

        lax.fori_loop(1, NX * NY, greet_plane, 0)

    @pl.when(is_extra)
    def _():
        def greet_all(n, carry):
            greet(at(n // NY, 1, lax.rem(n, NY)))
            return carry

        lax.fori_loop(0, NX * NY, greet_all, 0)

    settle(1, load_sem.at[0])

    pl.semaphore_wait(barrier, early)

    @pl.when(jnp.logical_and(far_owner, x == 2))
    def _():
        for relay in (5, 1):
            for xx in range(NX):
                remote(own, kv.at[6], b_send, b_recv.at[6], at(xx, relay)).start()

    @pl.when(jnp.logical_and(far_owner, x != 2))
    def _():
        for relay in (5, 1):
            for n in range(2):
                remote(own, kv.at[5], b_send, b_recv.at[5], at(x - n, relay)).start()

    for level in (4, 3, 2, 1):

        @pl.when(hosted == level)
        def _(level=level):
            half = 2 ** (level - 1)
            offsets = sorted((o for o in range(-half, half) if o), key=lambda o: -abs(o))
            if level == 4:
                offsets = [1] + [o for o in offsets if o < 0]
            for offset in offsets:
                remote(own, kv.at[level], b_send, b_recv.at[level], at(x, q + offset)).start()
            for n in range(2):
                pltpu.make_async_copy((k_in, v_in)[n].at[1], kv.at[level, n], load_sem.at[7]).start()

    @pl.when(is_second)
    def _():
        remote(own, kv.at[4], b_send, b_recv.at[4], at(x, 8)).wait_recv()
        for qq in (13, 12, 10, 11):
            remote(kv.at[4], kv.at[4], b_send, b_recv.at[4], at(x, qq)).start()

    top_two = kv.at[pl.ds(5, 2)]

    for relay, served in SERVED:

        @pl.when(q == relay)
        def _(relay=relay, served=served):
            for level in (5, 6):
                remote(own, kv.at[level], b_send, b_recv.at[level], at(x, 0)).wait_recv()
            for qq in (*served, relay - 1):
                remote(top_two, top_two, b_send, b_recv.at[5], at(x, qq)).start()

    for load in loads[4:]:
        load.wait()
    q_gain, k_gain = qg[...], kg[...]
    leaf_len = length[0]
    place = [DEPTH * T, jnp.maximum(DEPTH - hosted, 0) * T]
    live = [
        lax.broadcasted_iota(jnp.int32, (T, D), 0) < leaf_len,
        jnp.broadcast_to(hosted <= DEPTH, (T, D)),
    ]
    for kind in range(2):
        cosine, sine = spread(table[pl.ds(pl.multiple_of(place[kind], T), T), :])
        w_cos, w_sin = [], []
        for head in range(G):
            rows = pl.ds(kind * ROWS + head * T, T)
            unit, _ = unit_of(q_raw[kind, :, head * D : (head + 1) * D].astype(F32))
            q_rot[rows, :] = turn(unit * q_gain, cosine, sine).astype(BF)
            w_cos.append(unit * cosine)
            w_sin.append(pltpu.roll(unit * sine, D // 2, axis=1))
            if head % 2:
                pair = slice(kind * ROWS + (head - 1) * T, kind * ROWS + (head + 1) * T)
                wq_cos[:, pair] = jnp.transpose(jnp.concatenate(w_cos[-2:], axis=0))
                wq_sin[:, pair] = jnp.transpose(jnp.concatenate(w_sin[-2:], axis=0))
            grad = g_raw[kind, :, head * D : (head + 1) * D]
            g_rows[rows, :] = jnp.where(live[kind], grad, jnp.zeros((), BF))

    settle(1, load_sem.at[1])

    def take(slot):
        rows = pl.ds(slot * T, T)
        cosine, sine = spread(table[(DEPTH - slot) * T : (DEPTH - slot + 1) * T, :])
        unit, _ = unit_of(kv[slot, 0].astype(F32))
        wk_cos[rows, :] = unit * cosine
        wk_sin[rows, :] = pltpu.roll(unit * sine, D // 2, axis=1)
        k_rot[rows, :] = turn(unit * k_gain, cosine, sine).astype(BF)
        v_all[rows, :] = kv[slot, 1]

    def from_holder(level):
        @pl.when(jnp.logical_and(q != holder[level], jnp.logical_not(jnp.logical_and(among((9, 13)), level == 4))))
        def _():
            remote(own, kv.at[level], b_send, b_recv.at[level], at(x, holder[level])).wait_recv()

        @pl.when(hosted == level)
        def _():
            settle(1, load_sem.at[7])

    @pl.when(q == 13)
    def _():
        remote(own, kv.at[4], b_send, b_recv.at[4], at(x, 9)).wait_recv()
        for qq in (14, 15):
            remote(kv.at[4], kv.at[4], b_send, b_recv.at[4], at(x, qq)).start()

    @pl.when(jnp.logical_and(c == 1, jnp.logical_not(jnp.logical_or(is_relay, is_near))))
    def _():
        remote(top_two, top_two, b_send, b_recv.at[5], at(x, 1)).wait_recv()
        remote(top_two, top_two, b_send, b_recv.at[5], at(x, q - 1)).start()

    take(0)
    for level in (1, 2, 3):
        from_holder(level)
        take(level)

    key_at = lax.broadcasted_iota(jnp.int32, (T, ROWS), 0)
    row_at = lax.rem(lax.broadcasted_iota(jnp.int32, (T, ROWS), 1), T)
    ahead = key_at - row_at

    def partial(first, last, kind):
        rows = slice(kind * ROWS, (kind + 1) * ROWS)
        slots = slice(first * T, last * T)
        scores = dot(k_rot[slots, :], q_rot[rows, :], ((1,), (1,))) * SCALE
        pieces = []
        for slot in range(first, last):
            piece = scores[(slot - first) * T : (slot - first + 1) * T]
            if kind == 0:
                if slot == 0:
                    seen = jnp.logical_and(ahead <= 0, key_at < leaf_len)
                    piece = jnp.where(seen, piece, NEG_BIG)
            elif slot == 0:
                piece = jnp.full_like(piece, NEG_BIG)
            else:
                bound = jnp.where(hosted == slot, 0, jnp.where(hosted < slot, T, -T))
                piece = jnp.where(ahead <= bound, piece, NEG_BIG)
            pieces.append(piece)
        scores = jnp.concatenate(pieces, axis=0)
        top = jnp.max(scores, axis=0, keepdims=True)
        raised = jnp.exp(scores - top)
        dprobs = dot(v_all[slots, :], g_rows[rows, :], ((1,), (1,)))
        return (
            raised,
            dprobs,
            top,
            jnp.sum(raised, axis=0, keepdims=True),
            jnp.sum(raised * dprobs, axis=0, keepdims=True),
        )

    for kind in range(2):
        rows = slice(kind * ROWS, (kind + 1) * ROWS)
        near_e[:, rows], near_d[:, rows], near_s[0:1, rows], near_s[1:2, rows], near_s[2:3, rows] = partial(0, NEAR, kind)

    @pl.when(c == 0)
    def _():
        remote(top_two, top_two, b_send, b_recv.at[5], at(x, 1)).wait_recv()

    take(5)
    take(6)
    from_holder(4)
    take(4)

    for kind in range(2):
        rows = slice(kind * ROWS, (kind + 1) * ROWS)
        far_e, far_d, far_top, far_sum, far_delta = partial(NEAR, SLOTS, kind)
        near_top = near_s[0:1, rows]
        top = jnp.maximum(near_top, far_top)
        near_f, far_f = jnp.exp(near_top - top), jnp.exp(far_top - top)
        over = 1.0 / (near_s[1:2, rows] * near_f + far_sum * far_f)
        near_f, far_f = near_f * over, far_f * over
        delta = near_s[2:3, rows] * near_f + far_delta * far_f
        near = near_e[:, rows] * near_f
        far = far_e * far_f
        probs[: NEAR * T, rows] = near.astype(BF)
        probs[NEAR * T :, rows] = far.astype(BF)
        dscores[: NEAR * T, rows] = (near * (near_d[:, rows] - delta)).astype(BF)
        dscores[NEAR * T :, rows] = (far * (far_d - delta)).astype(BF)
    dk_all = dot(dscores[...], q_rot[...], ((1,), (0,))) * SCALE
    dv_all = dot(probs[...], g_rows[...], ((1,), (0,)))
    dq_turned = dot(k_rot[...], dscores[...], ((0,), (0,))) * SCALE
    for slot in range(SLOTS):
        part[slot, 0] = dk_all[slot * T : (slot + 1) * T]
        part[slot, 1] = dv_all[slot * T : (slot + 1) * T]

    for slot in range(1, SLOTS):
        send_kv[slot - 1] = part[slot].astype(BF)

    straight, crossed = dq_turned * wq_cos[...], dq_turned * wq_sin[...]
    both = straight - jnp.concatenate([crossed[D // 2 :], crossed[: D // 2]], axis=0)
    lanes = both[:, :D]
    for n in range(1, 2 * ROWS // D):
        lanes = lanes + both[:, n * D : (n + 1) * D]
    gain_q = jnp.sum(jnp.transpose(lanes), axis=0, keepdims=True)
    gain_k = jnp.sum(dk_all * wk_cos[...], axis=0, keepdims=True) - pltpu.roll(
        jnp.sum(dk_all * wk_sin[...], axis=0, keepdims=True), D // 2, axis=1
    )
    terms = jnp.concatenate([gain_q, gain_k], axis=0)
    gain_send[0] = terms

    @pl.when(jnp.logical_not(is_relay))
    def _():
        remote(gain_send.at[0], gain_z.at[lax.rem(q + NQ - 2, NQ)], gz_send, gz_recv, at(x, 1)).start()

    @pl.when(sends_six)
    def _():
        n = jnp.where(z >= 4, x, NX + jnp.minimum(x, 2))
        remote(send_kv.at[5], x_recv.at[n], x_sem.at[0], xr_sem, at(2, low)).start()

    @pl.when(sends_five)
    def _():
        n = jnp.where(z >= 4, 1 + lax.rem(x, 2), 0)
        remote(send_kv.at[4], x_recv.at[n], x_sem.at[1], xr_sem, at(x // 2 * 2 + 1, low)).start()

    for level in range(1, 5):

        @pl.when(q != holder[level])
        def _(level=level):
            n = lax.rem(q, 2**level)
            n = jnp.where(n > 2 ** (level - 1), n - 1, n)
            remote(send_kv.at[level - 1], z_recv.at[n], r_send, r_recv, at(x, holder[level])).start()

    y_q[...] = jnp.transpose(dq_turned)
    for kind in range(2):
        cosine, sine = spread(table[pl.ds(pl.multiple_of(place[kind], T), T), :])
        for head in range(G):
            rows = pl.ds(kind * ROWS + head * T, T)
            columns = slice(head * D, (head + 1) * D)
            raw = q_raw[kind, :, columns].astype(F32)
            unit, factor = unit_of(raw)
            scaled = unturn(y_q[rows, :], cosine, sine) * q_gain
            inner = jnp.mean(scaled * unit, axis=-1, keepdims=True)
            dq_out[kind, :, columns] = (factor * (scaled - unit * inner)).astype(BF)

    def key_gradient(raw, turned, start):
        cosine, sine = spread(table[pl.ds(start, T), :])
        unit, factor = unit_of(raw.astype(F32))
        scaled = unturn(turned, cosine, sine) * k_gain
        inner = jnp.mean(scaled * unit, axis=-1, keepdims=True)
        return (factor * (scaled - unit * inner)).astype(BF)

    dk_out[0] = key_gradient(kv[0, 0], part[0, 0], DEPTH * T)
    dv_out[0] = part[0, 1].astype(BF)

    @pl.when(is_relay)
    def _():
        gain_z[NQ - 1] = terms
        lines = gain_z.at[pl.ds(0, NQ - 1)]
        pltpu.make_async_copy(lines, lines, gz_recv).wait()
        line = gain_z[0]
        for qq in range(1, NQ):
            line = line + gain_z[qq]
        gain_send[1] = line
        gain_p[plane] = line
        for dx, dy in AWAY:
            device = at(lax.rem(x + dx, NX), 1, lax.rem(y + dy, NY))
            remote(gain_send.at[1], gain_p.at[plane], gp_send, gp_recv, device).start()
        remote(gain_send.at[1], gain_p.at[plane], gp_send, gp_recv, at(0, 3, 0)).start()

    def gather(level, count):
        settle(count, xr_sem)
        total = part[level]
        for n in range(count):
            total = total + x_recv[n].astype(F32)
        part[level] = total
        send_sum[...] = total.astype(BF)

    @pl.when(jnp.logical_and(z < 4, x == 2))
    def _():
        gather(6, 2 * NX - 1)

    @pl.when(jnp.logical_and(z < 4, lax.rem(x, 2) == 1))
    def _():
        gather(5, 3)

    sums = jnp.logical_and(x > 0, jnp.logical_and(z < 4, q != 0))

    @pl.when(sums)
    def _():
        remote(send_sum, z_recv.at[q - 1], s_send, r_recv, at(x, 0)).start()

    for places, count in (((1, 5), 9), ((9,), 7), ((13,), 5)):

        @pl.when(among(places))
        def _(count=count):
            settle(count, b_send)

    @pl.when(among((3, 7, 11, 15)))
    def _():
        settle(3, b_send)

    for level, count in ((2, 3), (3, 7), (4, 9), (5, 4), (6, 2 * NX)):

        @pl.when(hosted == level)
        def _(count=count):
            settle(count, b_send)

    @pl.when(hosted <= DEPTH)
    def _():
        size = jnp.int32(NQ)
        for level, count in ((1, 2), (2, 4), (3, 8), (5, 8), (6, 8)):
            size = jnp.where(hosted == level, count, size)
        for level in range(1, DEPTH + 1):

            @pl.when(hosted == level)
            def _(level=level):
                settle(2**level - 1 if level < 5 else NQ // 2 - 1, r_recv)

        def add(n, total):
            return total + z_recv[n].astype(F32)

        total = lax.fori_loop(0, size - 1, add, part[hosted])
        dk_out[1] = key_gradient(own[0], total[0], pl.multiple_of(place[1], T))
        dv_out[1] = total[1].astype(BF)

    @pl.when(hosted > DEPTH)
    def _():
        dk_out[1] = jnp.zeros((T, D), BF)
        dv_out[1] = jnp.zeros((T, D), BF)

    def total_of_lines(senders):
        lines = gain_p.at[pl.ds(0, senders)]
        pltpu.make_async_copy(lines, lines, gp_recv).wait()
        total = gain_p[0]
        for n in range(1, NX * NY):
            total = total + gain_p[n]
        gain_total[...] = total

    def pass_on(when, targets):
        @pl.when(when)
        def _():
            for qq in targets:
                remote(gain_total, gain_total, gt_send, gt_recv, at(x, qq)).start()

    @pl.when(is_relay)
    def _():
        total_of_lines(NX * NY - 1)

    @pl.when(is_extra)
    def _():
        total_of_lines(NX * NY)

    pass_on(jnp.logical_and(is_relay, plane > 0), (3, 5, 0))
    pass_on(is_extra, (5, 2, 0))

    @pl.when(is_relay)
    def _():
        pltpu.make_async_copy(gain_p, gain_p, gp_send).wait()

    @pl.when(sends_six)
    def _():
        settle(1, x_sem.at[0])

    @pl.when(sends_five)
    def _():
        settle(1, x_sem.at[1])

    @pl.when(hosted < 5)
    def _():
        settle(3, r_send)

    @pl.when(hosted >= 5)
    def _():
        settle(4, r_send)

    @pl.when(sums)
    def _():
        settle(1, s_send)

    @pl.when(jnp.logical_not(is_relay))
    def _():
        pltpu.make_async_copy(gain_total, gain_total, gz_send).wait()

        @pl.when(jnp.logical_not(is_extra))
        def _():
            pltpu.make_async_copy(gain_total, gain_total, gt_recv).wait()

    pass_one = jnp.logical_and(among((3, 7, 9, 11, 13, 15)), jnp.logical_not(is_extra))
    pass_on(q == 5, (7, 9, 11, 13, 15, 4))
    pass_on(pass_one, (q - 1,))
    dqg_out[...] = gain_total[0:1]
    dkg_out[...] = gain_total[1:2]

    def passed(when, count):
        @pl.when(when)
        def _():
            sent = gain_z.at[pl.ds(0, count)]
            pltpu.make_async_copy(sent, sent, gt_send).wait()

    passed(jnp.logical_or(is_extra, jnp.logical_and(is_relay, plane > 0)), 3)
    passed(q == 5, 6)
    passed(pass_one, 1)


def hand_over(*refs):
    copies = [pltpu.make_async_copy(refs[n], refs[5 + n], refs[10].at[n]) for n in range(5)]
    for copy in copies:
        copy.start()
    for copy in copies:
        copy.wait()


def on_device(queries, keys, values, output_gradient, q_gain, k_gain, leaf_len):
    dma = pltpu.SemaphoreType.DMA
    anywhere = pl.BlockSpec(memory_space=pl.ANY)
    in_hbm = pl.BlockSpec(memory_space=pltpu.HBM)
    results = pl.pallas_call(
        kernel,
        name="tree_backward",
        out_shape=[
            pltpu.VMEM(queries.shape, BF),
            pltpu.VMEM(keys.shape, BF),
            pltpu.VMEM(values.shape, BF),
            pltpu.VMEM((1, D), F32),
            pltpu.VMEM((1, D), F32),
        ],
        in_specs=[anywhere] * 7 + [pl.BlockSpec(memory_space=pltpu.SMEM)],
        out_specs=[pl.BlockSpec(memory_space=pltpu.VMEM)] * 5,
        scratch_shapes=[
            pltpu.VMEM((2, T, G * D), BF),
            pltpu.VMEM((2, T, G * D), BF),
            pltpu.VMEM((2, T, D), BF),
            pltpu.VMEM((SLOTS, 2, T, D), BF),
            pltpu.VMEM((1, D), F32),
            pltpu.VMEM((1, D), F32),
            pltpu.VMEM((KEYS, D), F32),
            pltpu.VMEM((2 * ROWS, D), BF),
            pltpu.VMEM((2 * ROWS, D), BF),
            pltpu.VMEM((KEYS, D), BF),
            pltpu.VMEM((KEYS, D), BF),
            pltpu.VMEM((D, 2 * ROWS), F32),
            pltpu.VMEM((D, 2 * ROWS), F32),
            pltpu.VMEM((KEYS, D), F32),
            pltpu.VMEM((KEYS, D), F32),
            pltpu.VMEM((NEAR * T, 2 * ROWS), F32),
            pltpu.VMEM((NEAR * T, 2 * ROWS), F32),
            pltpu.VMEM((8, 2 * ROWS), F32),
            pltpu.VMEM((KEYS, 2 * ROWS), BF),
            pltpu.VMEM((KEYS, 2 * ROWS), BF),
            pltpu.VMEM((SLOTS, 2, T, D), F32),
            pltpu.VMEM((2 * ROWS, D), F32),
            pltpu.VMEM((NQ, 2, T, D), BF),
            pltpu.VMEM((DEPTH, 2, T, D), BF),
            pltpu.VMEM((2, T, D), BF),
            pltpu.VMEM((2 * NX - 1, 2, T, D), BF),
            pltpu.VMEM((NQ, 2, T, D), BF),
            pltpu.VMEM((2, 2, D), F32),
            pltpu.VMEM((NQ, 2, D), F32),
            pltpu.VMEM((NX * NY, 2, D), F32),
            pltpu.VMEM((2, D), F32),
            dma((8,)),
            dma(()),
            dma((SLOTS,)),
            dma(()),
            dma(()),
            dma((2,)),
            dma(()),
            dma(()),
            dma(()),
            dma(()),
            dma(()),
            dma(()),
            dma(()),
            dma(()),
        ],
        compiler_params=pltpu.CompilerParams(
            collective_id=0, has_side_effects=True, vmem_limit_bytes=40 * 2**20
        ),
        cost_estimate=pl.CostEstimate(flops=10 * 2 * ROWS * KEYS * D, bytes_accessed=2**20, transcendentals=2 * ROWS * KEYS),
    )(
        *(
            pltpu.with_memory_space_constraint(array, pltpu.HBM)
            for array in (
                queries,
                keys,
                values,
                output_gradient,
                q_gain.reshape(1, D),
                k_gain.reshape(1, D),
                jnp.asarray(rope_table()),
            )
        ),
        leaf_len,
    )
    dq, dk, dv, dq_gain, dk_gain = pl.pallas_call(
        hand_over,
        name="hand_over",
        out_shape=[jax.ShapeDtypeStruct(r.shape, r.dtype) for r in results],
        in_specs=[anywhere] * 5,
        out_specs=[in_hbm] * 5,
        scratch_shapes=[dma((5,))],
        compiler_params=pltpu.CompilerParams(vmem_limit_bytes=8 * 2**20),
    )(*(pltpu.with_memory_space_constraint(r, pltpu.VMEM) for r in results))
    return dq, dk, dv, dq_gain.reshape(D), dk_gain.reshape(D)


def solution(mesh):
    shape = dict(mesh.shape)
    if shape != {"leaf": NX * NZ * NC, "head": NY}:
        raise ValueError("another mesh")
    split = P(None, "leaf", "head")
    return jax.shard_map(
        on_device,
        mesh=mesh,
        in_specs=(split, split, split, split, P(), P(), P("leaf")),
        out_specs=(split, split, split, P(), P()),
        check_vma=False,
    )
```

```python
import jax
import jax.numpy as jnp
import numpy as np
from jax import lax
from jax.experimental import pallas as pl
from jax.experimental.pallas import tpu as pltpu
from jax.sharding import PartitionSpec as P

NEG_BIG = -1000000000.0
NORM_EPS = 1e-06
ROPE_BASE = 1000000.0
DEPTH = 6
T = 64
D = 128
G = 8
SLOTS = DEPTH + 1
KEYS = SLOTS * T
NEAR = 4
MID = 5
ROWS = G * T
NX, NZ, NC, NY = 4, 8, 2, 8
NQ = NZ * NC
SCALE = D ** (-0.5)
BF = jnp.bfloat16
F32 = jnp.float32
MESH = pl.DeviceIdType.MESH
SERVED = ((1, (11, 13, 15, 3)), (5, (9, 7)))
AWAY = sorted(
    ((dx, dy) for dx in range(NX) for dy in range(NY) if dx or dy),
    key=lambda step: -min(step[0], NX - step[0]) - min(step[1], NY - step[1]),
)


def rope_table():
    frequency = (ROPE_BASE ** (-(np.arange(D // 2, dtype=np.float32) * 2.0 / D))).astype(np.float32)
    angles = np.arange(KEYS, dtype=np.float32)[:, None] * frequency
    return np.concatenate([np.cos(angles), np.sin(angles)], axis=1).astype(np.float32)


def spread(table):
    lane = lax.broadcasted_iota(jnp.int32, table.shape, 1)
    other = pltpu.roll(table, D // 2, axis=1)
    low = lane < D // 2
    return jnp.where(low, table, other), jnp.where(low, -other, table)


def turn(x, cosine, sine):
    return x * cosine + pltpu.roll(x, D // 2, axis=1) * sine


def unturn(x, cosine, sine):
    return x * cosine - pltpu.roll(x, D // 2, axis=1) * sine


def unit_of(x):
    factor = lax.rsqrt(jnp.mean(x * x, axis=-1, keepdims=True) + NORM_EPS)
    return x * factor, factor


def dot(a, b, contract):
    return lax.dot_general(a, b, (contract, ((), ())), preferred_element_type=F32)


def kernel(
    q_in, k_in, v_in, g_in, qg_in, kg_in, table_in, length,
    dq_out, dk_out, dv_out, dqg_out, dkg_out,
    q_raw, g_raw, own, kv, qg, kg, table,
    q_rot, g_rows, k_rot, v_all, wq_cos, wq_sin, wk_cos, wk_sin, near_e, near_d, near_s, probs, dscores, part, y_q, ballast,
    send_kv, send_sum, x_recv, z_recv, gain_send, gain_z, gain_p, gain_total,
    load_sem, b_send, b_recv, r_send, r_recv, x_sem, xr_sem, s_send,
    gz_send, gz_recv, gp_send, gp_recv, gt_send, gt_recv,
):
    leaf = lax.axis_index("leaf")
    y = lax.axis_index("head")
    x = leaf // NQ
    q = lax.rem(leaf, NQ)
    z = q // NC
    c = lax.rem(q, NC)

    def at(xx, qq, yy=None):
        return (xx * NQ + qq, y if yy is None else yy)

    hosted = jnp.int32(1)
    for level in range(1, DEPTH + 1):
        hosted = hosted + jnp.where(lax.rem(leaf, 2**level) == 0, 1, 0)

    def remote(src, dst, send, recv, device):
        return pltpu.make_async_remote_copy(
            src_ref=src, dst_ref=dst, send_sem=send, recv_sem=recv, device_id=device, device_id_type=MESH
        )

    def settle(count, sem):
        blocks = ballast.at[pl.ds(0, count)]
        pltpu.make_async_copy(blocks, blocks, sem).wait()

    holder = {level: q // 2**level * 2**level + 2 ** (level - 1) for level in range(1, 5)}
    is_relay = q == 1
    is_near = q == 5
    is_extra = jnp.logical_and(leaf == 3, y == 0)
    is_second = q == 9
    far_owner = jnp.logical_and(q == 0, x > 0)
    plane = x * NY + y
    mirror = (NZ - 1 - z) * NC + c
    low = jnp.where(z < 4, q, mirror)
    sends_six = jnp.logical_or(z >= 4, x != 2)
    sends_five = jnp.logical_or(z >= 4, lax.rem(x, 2) == 0)

    def among(places):
        here = q == places[0]
        for place in places[1:]:
            here = jnp.logical_or(here, q == place)
        return here

    barrier = pltpu.get_barrier_semaphore()

    def greet(device):
        pl.semaphore_signal(barrier, inc=1, device_id=device, device_id_type=MESH)

    @pl.when(jnp.logical_or(is_relay, is_near))
    def _():
        greet(at(2, 0))
        greet(at(x // 2 * 2 + 1, 0))

    for relay, served in SERVED:

        @pl.when(among(served))
        def _(relay=relay):
            greet(at(x, relay))

    @pl.when(among((10, 11, 12, 13)))
    def _():
        greet(at(x, 9))

    @pl.when(z == NZ - 1)
    def _():
        greet(at(x, 13))

    @pl.when(jnp.logical_or(z < 4, is_second))
    def _():
        greet(at(x, 8))

    for level in (3, 2, 1):

        @pl.when(jnp.logical_and(q != holder[level], jnp.logical_not(jnp.logical_and(z == NZ - 1, level == 3))))
        def _(level=level):
            greet(at(x, holder[level]))

    @pl.when(jnp.logical_and(z < 4, x == 2))
    def _():
        for xx in range(NX):
            greet(at(xx, mirror))
        for xx in (0, 1, 3):
            greet(at(xx, q))

    @pl.when(jnp.logical_and(z < 4, lax.rem(x, 2) == 1))
    def _():
        greet(at(x, mirror))
        greet(at(x - 1, mirror))
        greet(at(x - 1, q))

    early = jnp.where(c == 1, 1, 0)
    early = early + jnp.where(sends_six, 1, 0) + jnp.where(sends_five, 1, 0)
    early = early + jnp.where(is_relay, 4 + NX * NY, 0) + jnp.where(is_near, 2, 0)
    early = early + jnp.where(is_second, 4, 0) + jnp.where(q == 13, 2, 0) - jnp.where(q == 12, 2, 0)
    for level, count in ((2, 3), (3, 7), (4, 9), (5, 4), (6, 2 * NX)):
        early = early + jnp.where(hosted == level, count, 0)

    loads = [
        pltpu.make_async_copy(k_in.at[1], own.at[0], load_sem.at[0]),
        pltpu.make_async_copy(v_in.at[1], own.at[1], load_sem.at[0]),
        pltpu.make_async_copy(k_in.at[0], kv.at[0, 0], load_sem.at[1]),
        pltpu.make_async_copy(v_in.at[0], kv.at[0, 1], load_sem.at[1]),
        pltpu.make_async_copy(table_in, table, load_sem.at[2]),
        pltpu.make_async_copy(qg_in, qg, load_sem.at[3]),
        pltpu.make_async_copy(kg_in, kg, load_sem.at[4]),
        pltpu.make_async_copy(q_in, q_raw, load_sem.at[5]),
        pltpu.make_async_copy(g_in, g_raw, load_sem.at[6]),
    ]
    for load in loads:
        load.start()

    @pl.when(is_relay)
    def _():
        def greet_plane(n, carry):
            there = lax.rem(plane + n, NX * NY)
            greet(at(there // NY, 1, lax.rem(there, NY)))
            return carry

        lax.fori_loop(1, NX * NY, greet_plane, 0)

    @pl.when(is_extra)
    def _():
        def greet_all(n, carry):
            greet(at(n // NY, 1, lax.rem(n, NY)))
            return carry

        lax.fori_loop(0, NX * NY, greet_all, 0)

    settle(1, load_sem.at[0])

    pl.semaphore_wait(barrier, early)

    @pl.when(jnp.logical_and(far_owner, x == 2))
    def _():
        for relay in (5, 1):
            for xx in range(NX):
                remote(own, kv.at[6], b_send, b_recv.at[6], at(xx, relay)).start()

    @pl.when(jnp.logical_and(far_owner, x != 2))
    def _():
        for relay in (5, 1):
            for n in range(2):
                remote(own, kv.at[5], b_send, b_recv.at[5], at(x - n, relay)).start()

    for level in (4, 3, 2, 1):

        @pl.when(hosted == level)
        def _(level=level):
            half = 2 ** (level - 1)
            offsets = sorted((o for o in range(-half, half) if o), key=lambda o: -abs(o))
            if level == 4:
                offsets = [1] + [o for o in offsets if o < 0]
            for offset in offsets:
                if level == 3 and offset in (2, 3):

                    @pl.when(q != 12)
                    def _(offset=offset):
                        remote(own, kv.at[level], b_send, b_recv.at[level], at(x, q + offset)).start()

                else:
                    remote(own, kv.at[level], b_send, b_recv.at[level], at(x, q + offset)).start()
            for n in range(2):
                pltpu.make_async_copy((k_in, v_in)[n].at[1], kv.at[level, n], load_sem.at[7]).start()

    @pl.when(is_second)
    def _():
        remote(own, kv.at[4], b_send, b_recv.at[4], at(x, 8)).wait_recv()
        for qq in (13, 12, 10, 11):
            remote(kv.at[4], kv.at[4], b_send, b_recv.at[4], at(x, qq)).start()

    top_two = kv.at[pl.ds(5, 2)]

    for relay, served in SERVED:

        @pl.when(q == relay)
        def _(relay=relay, served=served):
            for level in (5, 6):
                remote(own, kv.at[level], b_send, b_recv.at[level], at(x, 0)).wait_recv()
            for qq in (*served, relay - 1):
                remote(top_two, top_two, b_send, b_recv.at[5], at(x, qq)).start()

    for load in loads[4:]:
        load.wait()
    q_gain, k_gain = qg[...], kg[...]
    leaf_len = length[0]
    place = [DEPTH * T, jnp.maximum(DEPTH - hosted, 0) * T]
    live = [
        lax.broadcasted_iota(jnp.int32, (T, D), 0) < leaf_len,
        jnp.broadcast_to(hosted <= DEPTH, (T, D)),
    ]
    for kind in range(2):
        cosine, sine = spread(table[pl.ds(pl.multiple_of(place[kind], T), T), :])
        w_cos, w_sin = [], []
        for head in range(G):
            rows = pl.ds(kind * ROWS + head * T, T)
            unit, _ = unit_of(q_raw[kind, :, head * D : (head + 1) * D].astype(F32))
            q_rot[rows, :] = turn(unit * q_gain, cosine, sine).astype(BF)
            w_cos.append(unit * cosine)
            w_sin.append(pltpu.roll(unit * sine, D // 2, axis=1))
            if head % 2:
                pair = slice(kind * ROWS + (head - 1) * T, kind * ROWS + (head + 1) * T)
                wq_cos[:, pair] = jnp.transpose(jnp.concatenate(w_cos[-2:], axis=0))
                wq_sin[:, pair] = jnp.transpose(jnp.concatenate(w_sin[-2:], axis=0))
            grad = g_raw[kind, :, head * D : (head + 1) * D]
            g_rows[rows, :] = jnp.where(live[kind], grad, jnp.zeros((), BF))

    settle(1, load_sem.at[1])

    def take(slot):
        rows = pl.ds(slot * T, T)
        cosine, sine = spread(table[(DEPTH - slot) * T : (DEPTH - slot + 1) * T, :])
        unit, _ = unit_of(kv[slot, 0].astype(F32))
        wk_cos[rows, :] = unit * cosine
        wk_sin[rows, :] = pltpu.roll(unit * sine, D // 2, axis=1)
        k_rot[rows, :] = turn(unit * k_gain, cosine, sine).astype(BF)
        v_all[rows, :] = kv[slot, 1]

    def from_holder(level):
        passed_on = {3: q == 13, 4: among((9, 13))}.get(level, False)

        @pl.when(jnp.logical_and(q != holder[level], jnp.logical_not(passed_on)))
        def _():
            remote(own, kv.at[level], b_send, b_recv.at[level], at(x, holder[level])).wait_recv()

        @pl.when(hosted == level)
        def _():
            settle(1, load_sem.at[7])

    @pl.when(q == 13)
    def _():
        remote(own, kv.at[3], b_send, b_recv.at[3], at(x, 12)).wait_recv()
        for qq in (14, 15):
            remote(kv.at[3], kv.at[3], b_send, b_recv.at[3], at(x, qq)).start()

    take(0)
    for level in (1, 2):
        from_holder(level)
        take(level)

    @pl.when(q == 13)
    def _():
        remote(own, kv.at[4], b_send, b_recv.at[4], at(x, 9)).wait_recv()
        for qq in (14, 15):
            remote(kv.at[4], kv.at[4], b_send, b_recv.at[4], at(x, qq)).start()

    @pl.when(jnp.logical_and(c == 1, jnp.logical_not(jnp.logical_or(is_relay, is_near))))
    def _():
        remote(top_two, top_two, b_send, b_recv.at[5], at(x, 1)).wait_recv()
        remote(top_two, top_two, b_send, b_recv.at[5], at(x, q - 1)).start()

    from_holder(3)
    take(3)

    key_at = lax.broadcasted_iota(jnp.int32, (T, ROWS), 0)
    row_at = lax.rem(lax.broadcasted_iota(jnp.int32, (T, ROWS), 1), T)
    ahead = key_at - row_at

    def partial(first, last, kind):
        rows = slice(kind * ROWS, (kind + 1) * ROWS)
        slots = slice(first * T, last * T)
        scores = dot(k_rot[slots, :], q_rot[rows, :], ((1,), (1,))) * SCALE
        pieces = []
        for slot in range(first, last):
            piece = scores[(slot - first) * T : (slot - first + 1) * T]
            if kind == 0:
                if slot == 0:
                    seen = jnp.logical_and(ahead <= 0, key_at < leaf_len)
                    piece = jnp.where(seen, piece, NEG_BIG)
            elif slot == 0:
                piece = jnp.full_like(piece, NEG_BIG)
            else:
                bound = jnp.where(hosted == slot, 0, jnp.where(hosted < slot, T, -T))
                piece = jnp.where(ahead <= bound, piece, NEG_BIG)
            pieces.append(piece)
        scores = jnp.concatenate(pieces, axis=0)
        top = jnp.max(scores, axis=0, keepdims=True)
        raised = jnp.exp(scores - top)
        dprobs = dot(v_all[slots, :], g_rows[rows, :], ((1,), (1,)))
        return (
            raised,
            dprobs,
            top,
            jnp.sum(raised, axis=0, keepdims=True),
            jnp.sum(raised * dprobs, axis=0, keepdims=True),
        )

    def keep(first, last, at_row, kind, rows):
        raised, products, *sums = partial(first, last, kind)
        near_e[first * T : last * T, rows] = raised
        near_d[first * T : last * T, rows] = products
        for n, line in enumerate(sums):
            near_s[at_row + n : at_row + n + 1, rows] = line

    for kind in range(2):
        rows = slice(kind * ROWS, (kind + 1) * ROWS)
        keep(0, NEAR, 0, kind, rows)

    from_holder(4)
    take(4)
    for kind in range(2):
        rows = slice(kind * ROWS, (kind + 1) * ROWS)
        keep(NEAR, MID, 3, kind, rows)

    @pl.when(c == 0)
    def _():
        remote(top_two, top_two, b_send, b_recv.at[5], at(x, 1)).wait_recv()

    take(5)
    take(6)
    for kind in range(2):
        rows = slice(kind * ROWS, (kind + 1) * ROWS)
        far_e, far_d, far_top, far_sum, far_delta = partial(MID, SLOTS, kind)
        near_top, mid_top = near_s[0:1, rows], near_s[3:4, rows]
        top = jnp.maximum(jnp.maximum(near_top, mid_top), far_top)
        near_f, mid_f, far_f = jnp.exp(near_top - top), jnp.exp(mid_top - top), jnp.exp(far_top - top)
        over = 1.0 / (near_s[1:2, rows] * near_f + near_s[4:5, rows] * mid_f + far_sum * far_f)
        near_f, mid_f, far_f = near_f * over, mid_f * over, far_f * over
        delta = near_s[2:3, rows] * near_f + near_s[5:6, rows] * mid_f + far_delta * far_f
        for first, last, factor, e, d in (
            (0, NEAR, near_f, near_e[: NEAR * T, rows], near_d[: NEAR * T, rows]),
            (NEAR, MID, mid_f, near_e[NEAR * T :, rows], near_d[NEAR * T :, rows]),
            (MID, SLOTS, far_f, far_e, far_d),
        ):
            prob = e * factor
            probs[first * T : last * T, rows] = prob.astype(BF)
            dscores[first * T : last * T, rows] = (prob * (d - delta)).astype(BF)
    dk_all = dot(dscores[...], q_rot[...], ((1,), (0,))) * SCALE
    dq_turned = dot(k_rot[...], dscores[...], ((0,), (0,))) * SCALE
    straight, crossed = dq_turned * wq_cos[...], dq_turned * wq_sin[...]
    both = straight - jnp.concatenate([crossed[D // 2 :], crossed[: D // 2]], axis=0)
    lanes = both[:, :D]
    for n in range(1, 2 * ROWS // D):
        lanes = lanes + both[:, n * D : (n + 1) * D]
    gain_q = jnp.sum(jnp.transpose(lanes), axis=0, keepdims=True)
    gain_k = jnp.sum(dk_all * wk_cos[...], axis=0, keepdims=True) - pltpu.roll(
        jnp.sum(dk_all * wk_sin[...], axis=0, keepdims=True), D // 2, axis=1
    )
    terms = jnp.concatenate([gain_q, gain_k], axis=0)
    gain_send[0] = terms

    @pl.when(jnp.logical_not(is_relay))
    def _():
        remote(gain_send.at[0], gain_z.at[lax.rem(q + NQ - 2, NQ)], gz_send, gz_recv, at(x, 1)).start()

    dv_all = dot(probs[...], g_rows[...], ((1,), (0,)))
    for slot in range(SLOTS):
        part[slot, 0] = dk_all[slot * T : (slot + 1) * T]
        part[slot, 1] = dv_all[slot * T : (slot + 1) * T]

    for slot in range(1, SLOTS):
        send_kv[slot - 1] = part[slot].astype(BF)

    @pl.when(sends_six)
    def _():
        n = jnp.where(z >= 4, x, NX + jnp.minimum(x, 2))
        remote(send_kv.at[5], x_recv.at[n], x_sem.at[0], xr_sem, at(2, low)).start()

    @pl.when(sends_five)
    def _():
        n = jnp.where(z >= 4, 1 + lax.rem(x, 2), 0)
        remote(send_kv.at[4], x_recv.at[n], x_sem.at[1], xr_sem, at(x // 2 * 2 + 1, low)).start()

    for level in range(1, 5):

        @pl.when(q != holder[level])
        def _(level=level):
            n = lax.rem(q, 2**level)
            n = jnp.where(n > 2 ** (level - 1), n - 1, n)
            remote(send_kv.at[level - 1], z_recv.at[n], r_send, r_recv, at(x, holder[level])).start()

    y_q[...] = jnp.transpose(dq_turned)
    for kind in range(2):
        cosine, sine = spread(table[pl.ds(pl.multiple_of(place[kind], T), T), :])
        for head in range(G):
            rows = pl.ds(kind * ROWS + head * T, T)
            columns = slice(head * D, (head + 1) * D)
            raw = q_raw[kind, :, columns].astype(F32)
            unit, factor = unit_of(raw)
            scaled = unturn(y_q[rows, :], cosine, sine) * q_gain
            inner = jnp.mean(scaled * unit, axis=-1, keepdims=True)
            dq_out[kind, :, columns] = (factor * (scaled - unit * inner)).astype(BF)

    def key_gradient(raw, turned, start):
        cosine, sine = spread(table[pl.ds(start, T), :])
        unit, factor = unit_of(raw.astype(F32))
        scaled = unturn(turned, cosine, sine) * k_gain
        inner = jnp.mean(scaled * unit, axis=-1, keepdims=True)
        return (factor * (scaled - unit * inner)).astype(BF)

    dk_out[0] = key_gradient(kv[0, 0], part[0, 0], DEPTH * T)
    dv_out[0] = part[0, 1].astype(BF)

    @pl.when(is_relay)
    def _():
        gain_z[NQ - 1] = terms
        lines = gain_z.at[pl.ds(0, NQ - 1)]
        pltpu.make_async_copy(lines, lines, gz_recv).wait()
        line = gain_z[0]
        for qq in range(1, NQ):
            line = line + gain_z[qq]
        gain_send[1] = line
        gain_p[plane] = line
        for dx, dy in AWAY:
            device = at(lax.rem(x + dx, NX), 1, lax.rem(y + dy, NY))
            remote(gain_send.at[1], gain_p.at[plane], gp_send, gp_recv, device).start()
        remote(gain_send.at[1], gain_p.at[plane], gp_send, gp_recv, at(0, 3, 0)).start()

    def gather(level, count):
        settle(count, xr_sem)
        total = part[level]
        for n in range(count):
            total = total + x_recv[n].astype(F32)
        part[level] = total
        send_sum[...] = total.astype(BF)

    @pl.when(jnp.logical_and(z < 4, x == 2))
    def _():
        gather(6, 2 * NX - 1)

    @pl.when(jnp.logical_and(z < 4, lax.rem(x, 2) == 1))
    def _():
        gather(5, 3)

    sums = jnp.logical_and(x > 0, jnp.logical_and(z < 4, q != 0))

    @pl.when(sums)
    def _():
        remote(send_sum, z_recv.at[q - 1], s_send, r_recv, at(x, 0)).start()

    for places, count in (((1,), 11), ((5, 9, 13), 7), ((4,), 7), ((12,), 5)):

        @pl.when(among(places))
        def _(count=count):
            settle(count, b_send)

    @pl.when(among((3, 7, 11, 15)))
    def _():
        settle(3, b_send)

    for level, count in ((2, 3), (4, 9), (5, 4), (6, 2 * NX)):

        @pl.when(hosted == level)
        def _(count=count):
            settle(count, b_send)

    @pl.when(hosted <= DEPTH)
    def _():
        size = jnp.int32(NQ)
        for level, count in ((1, 2), (2, 4), (3, 8), (5, 8), (6, 8)):
            size = jnp.where(hosted == level, count, size)
        for level in range(1, DEPTH + 1):

            @pl.when(hosted == level)
            def _(level=level):
                settle(2**level - 1 if level < 5 else NQ // 2 - 1, r_recv)

        def add(n, total):
            return total + z_recv[n].astype(F32)

        total = lax.fori_loop(0, size - 1, add, part[hosted])
        dk_out[1] = key_gradient(own[0], total[0], pl.multiple_of(place[1], T))
        dv_out[1] = total[1].astype(BF)

    @pl.when(hosted > DEPTH)
    def _():
        dk_out[1] = jnp.zeros((T, D), BF)
        dv_out[1] = jnp.zeros((T, D), BF)

    def total_of_lines(senders):
        lines = gain_p.at[pl.ds(0, senders)]
        pltpu.make_async_copy(lines, lines, gp_recv).wait()
        total = gain_p[0]
        for n in range(1, NX * NY):
            total = total + gain_p[n]
        gain_total[...] = total

    def pass_on(when, targets):
        @pl.when(when)
        def _():
            for qq in targets:
                remote(gain_total, gain_total, gt_send, gt_recv, at(x, qq)).start()

    @pl.when(is_relay)
    def _():
        total_of_lines(NX * NY - 1)

    @pl.when(is_extra)
    def _():
        total_of_lines(NX * NY)

    pass_on(jnp.logical_and(is_relay, plane > 0), (3, 5, 7, 0))
    pass_on(is_extra, (5, 7, 2, 0))

    @pl.when(is_relay)
    def _():
        pltpu.make_async_copy(gain_p, gain_p, gp_send).wait()

    @pl.when(sends_six)
    def _():
        settle(1, x_sem.at[0])

    @pl.when(sends_five)
    def _():
        settle(1, x_sem.at[1])

    @pl.when(hosted < 5)
    def _():
        settle(3, r_send)

    @pl.when(hosted >= 5)
    def _():
        settle(4, r_send)

    @pl.when(sums)
    def _():
        settle(1, s_send)

    @pl.when(jnp.logical_not(is_relay))
    def _():
        pltpu.make_async_copy(gain_total, gain_total, gz_send).wait()

        @pl.when(jnp.logical_not(is_extra))
        def _():
            pltpu.make_async_copy(gain_total, gain_total, gt_recv).wait()

    pass_one = jnp.logical_and(among((3, 7, 9, 11, 13, 15)), jnp.logical_not(is_extra))
    pass_on(q == 5, (9, 11, 13, 15, 4))
    pass_on(pass_one, (q - 1,))
    dqg_out[...] = gain_total[0:1]
    dkg_out[...] = gain_total[1:2]

    def passed(when, count):
        @pl.when(when)
        def _():
            sent = gain_z.at[pl.ds(0, count)]
            pltpu.make_async_copy(sent, sent, gt_send).wait()

    passed(jnp.logical_or(is_extra, jnp.logical_and(is_relay, plane > 0)), 4)
    passed(q == 5, 5)
    passed(pass_one, 1)


def hand_over(*refs):
    copies = [pltpu.make_async_copy(refs[n], refs[5 + n], refs[10].at[n]) for n in range(5)]
    for copy in copies:
        copy.start()
    for copy in copies:
        copy.wait()


def on_device(queries, keys, values, output_gradient, q_gain, k_gain, leaf_len):
    dma = pltpu.SemaphoreType.DMA
    anywhere = pl.BlockSpec(memory_space=pl.ANY)
    in_hbm = pl.BlockSpec(memory_space=pltpu.HBM)
    results = pl.pallas_call(
        kernel,
        name="tree_backward",
        out_shape=[
            pltpu.VMEM(queries.shape, BF),
            pltpu.VMEM(keys.shape, BF),
            pltpu.VMEM(values.shape, BF),
            pltpu.VMEM((1, D), F32),
            pltpu.VMEM((1, D), F32),
        ],
        in_specs=[anywhere] * 7 + [pl.BlockSpec(memory_space=pltpu.SMEM)],
        out_specs=[pl.BlockSpec(memory_space=pltpu.VMEM)] * 5,
        scratch_shapes=[
            pltpu.VMEM((2, T, G * D), BF),
            pltpu.VMEM((2, T, G * D), BF),
            pltpu.VMEM((2, T, D), BF),
            pltpu.VMEM((SLOTS, 2, T, D), BF),
            pltpu.VMEM((1, D), F32),
            pltpu.VMEM((1, D), F32),
            pltpu.VMEM((KEYS, D), F32),
            pltpu.VMEM((2 * ROWS, D), BF),
            pltpu.VMEM((2 * ROWS, D), BF),
            pltpu.VMEM((KEYS, D), BF),
            pltpu.VMEM((KEYS, D), BF),
            pltpu.VMEM((D, 2 * ROWS), F32),
            pltpu.VMEM((D, 2 * ROWS), F32),
            pltpu.VMEM((KEYS, D), F32),
            pltpu.VMEM((KEYS, D), F32),
            pltpu.VMEM((MID * T, 2 * ROWS), F32),
            pltpu.VMEM((MID * T, 2 * ROWS), F32),
            pltpu.VMEM((8, 2 * ROWS), F32),
            pltpu.VMEM((KEYS, 2 * ROWS), BF),
            pltpu.VMEM((KEYS, 2 * ROWS), BF),
            pltpu.VMEM((SLOTS, 2, T, D), F32),
            pltpu.VMEM((2 * ROWS, D), F32),
            pltpu.VMEM((NQ, 2, T, D), BF),
            pltpu.VMEM((DEPTH, 2, T, D), BF),
            pltpu.VMEM((2, T, D), BF),
            pltpu.VMEM((2 * NX - 1, 2, T, D), BF),
            pltpu.VMEM((NQ, 2, T, D), BF),
            pltpu.VMEM((2, 2, D), F32),
            pltpu.VMEM((NQ, 2, D), F32),
            pltpu.VMEM((NX * NY, 2, D), F32),
            pltpu.VMEM((2, D), F32),
            dma((8,)),
            dma(()),
            dma((SLOTS,)),
            dma(()),
            dma(()),
            dma((2,)),
            dma(()),
            dma(()),
            dma(()),
            dma(()),
            dma(()),
            dma(()),
            dma(()),
            dma(()),
        ],
        compiler_params=pltpu.CompilerParams(
            collective_id=0, has_side_effects=True, vmem_limit_bytes=40 * 2**20
        ),
        cost_estimate=pl.CostEstimate(flops=10 * 2 * ROWS * KEYS * D, bytes_accessed=2**20, transcendentals=2 * ROWS * KEYS),
    )(
        *(
            pltpu.with_memory_space_constraint(array, pltpu.HBM)
            for array in (
                queries,
                keys,
                values,
                output_gradient,
                q_gain.reshape(1, D),
                k_gain.reshape(1, D),
                jnp.asarray(rope_table()),
            )
        ),
        leaf_len,
    )
    dq, dk, dv, dq_gain, dk_gain = pl.pallas_call(
        hand_over,
        name="hand_over",
        out_shape=[jax.ShapeDtypeStruct(r.shape, r.dtype) for r in results],
        in_specs=[anywhere] * 5,
        out_specs=[in_hbm] * 5,
        scratch_shapes=[dma((5,))],
        compiler_params=pltpu.CompilerParams(vmem_limit_bytes=8 * 2**20),
    )(*(pltpu.with_memory_space_constraint(r, pltpu.VMEM) for r in results))
    return dq, dk, dv, dq_gain.reshape(D), dk_gain.reshape(D)


def solution(mesh):
    shape = dict(mesh.shape)
    if shape != {"leaf": NX * NZ * NC, "head": NY}:
        raise ValueError("another mesh")
    split = P(None, "leaf", "head")
    return jax.shard_map(
        on_device,
        mesh=mesh,
        in_specs=(split, split, split, split, P(), P(), P("leaf")),
        out_specs=(split, split, split, P(), P()),
        check_vma=False,
    )
```

```python
import jax
import jax.numpy as jnp
import numpy as np
from jax import lax
from jax.experimental import pallas as pl
from jax.experimental.pallas import tpu as pltpu
from jax.sharding import PartitionSpec as P

NEG_BIG = -1000000000.0
NORM_EPS = 1e-06
ROPE_BASE = 1000000.0
DEPTH = 6
T = 64
D = 128
G = 8
SLOTS = DEPTH + 1
KEYS = SLOTS * T
NEAR = 4
MID = 5
ROWS = G * T
NX, NZ, NC, NY = 4, 8, 2, 8
NQ = NZ * NC
SCALE = D ** (-0.5)
BF = jnp.bfloat16
F32 = jnp.float32
MESH = pl.DeviceIdType.MESH
FIRST = ((0, 1, 0), (0, 3, 0), (0, 1, 1), (1, 1, 0), (2, 1, 0), (3, 1, 0))
LAST_Y = (4, 5)
EARLY_Q = 6
SERVED = ((1, (11, 13, 15, 3)), (5, (9, 7)))
AWAY = sorted(
    ((dx, dy) for dx in range(NX) for dy in range(NY) if dx or dy),
    key=lambda step: -min(step[0], NX - step[0]) - min(step[1], NY - step[1]),
)


def rope_table():
    frequency = (ROPE_BASE ** (-(np.arange(D // 2, dtype=np.float32) * 2.0 / D))).astype(np.float32)
    angles = np.arange(KEYS, dtype=np.float32)[:, None] * frequency
    return np.concatenate([np.cos(angles), np.sin(angles)], axis=1).astype(np.float32)


def spread(table):
    lane = lax.broadcasted_iota(jnp.int32, table.shape, 1)
    other = pltpu.roll(table, D // 2, axis=1)
    low = lane < D // 2
    return jnp.where(low, table, other), jnp.where(low, -other, table)


def turn(x, cosine, sine):
    return x * cosine + pltpu.roll(x, D // 2, axis=1) * sine


def unturn(x, cosine, sine):
    return x * cosine - pltpu.roll(x, D // 2, axis=1) * sine


def unit_of(x):
    factor = lax.rsqrt(jnp.mean(x * x, axis=-1, keepdims=True) + NORM_EPS)
    return x * factor, factor


def dot(a, b, contract):
    return lax.dot_general(a, b, (contract, ((), ())), preferred_element_type=F32)


def kernel(
    q_in, k_in, v_in, g_in, qg_in, kg_in, table_in, length,
    dq_out, dk_out, dv_out, dqg_out, dkg_out,
    q_raw, g_raw, own, kv, qg, kg, table,
    q_rot, g_rows, k_rot, v_all, wq_cos, wq_sin, wk_cos, wk_sin, near_e, near_d, near_s, probs, dscores, part, y_q, ballast,
    send_kv, send_sum, x_recv, z_recv, gain_send, gain_z, gain_p, gain_d, gain_total,
    load_sem, b_send, b_recv, r_send, r_recv, x_sem, xr_sem, s_send,
    gz_send, gz_recv, gp_send, gp_recv, gd_send, gd_recv, gt_send, gt_recv,
):
    leaf = lax.axis_index("leaf")
    y = lax.axis_index("head")
    x = leaf // NQ
    q = lax.rem(leaf, NQ)
    z = q // NC
    c = lax.rem(q, NC)

    def at(xx, qq, yy=None):
        return (xx * NQ + qq, y if yy is None else yy)

    hosted = jnp.int32(1)
    for level in range(1, DEPTH + 1):
        hosted = hosted + jnp.where(lax.rem(leaf, 2**level) == 0, 1, 0)

    def remote(src, dst, send, recv, device):
        return pltpu.make_async_remote_copy(
            src_ref=src, dst_ref=dst, send_sem=send, recv_sem=recv, device_id=device, device_id_type=MESH
        )

    def settle(count, sem):
        blocks = ballast.at[pl.ds(0, count)]
        pltpu.make_async_copy(blocks, blocks, sem).wait()

    holder = {level: q // 2**level * 2**level + 2 ** (level - 1) for level in range(1, 5)}
    is_relay = q == 1
    is_near = q == 5
    is_extra = jnp.logical_and(leaf == 3, y == 0)
    is_first = jnp.logical_or(is_extra, jnp.logical_and(is_relay, jnp.logical_or(y == 0, jnp.logical_and(x == 0, y == 1))))
    is_second = q == 9
    far_owner = jnp.logical_and(q == 0, x > 0)
    plane = x * NY + y
    starts_last = jnp.logical_and(y >= LAST_Y[0], y <= LAST_Y[-1])
    direct = jnp.logical_and(starts_last, q >= EARLY_Q)
    mirror = (NZ - 1 - z) * NC + c
    low = jnp.where(z < 4, q, mirror)
    sends_six = jnp.logical_or(z >= 4, x != 2)
    sends_five = jnp.logical_or(z >= 4, lax.rem(x, 2) == 0)

    def among(places):
        here = q == places[0]
        for place in places[1:]:
            here = jnp.logical_or(here, q == place)
        return here

    barrier = pltpu.get_barrier_semaphore()

    def greet(device):
        pl.semaphore_signal(barrier, inc=1, device_id=device, device_id_type=MESH)

    @pl.when(jnp.logical_or(is_relay, is_near))
    def _():
        greet(at(2, 0))
        greet(at(x // 2 * 2 + 1, 0))

    for relay, served in SERVED:

        @pl.when(among(served))
        def _(relay=relay):
            greet(at(x, relay))

    @pl.when(among((10, 11, 12, 13)))
    def _():
        greet(at(x, 9))

    @pl.when(z == NZ - 1)
    def _():
        greet(at(x, 13))

    @pl.when(jnp.logical_or(z < 4, is_second))
    def _():
        greet(at(x, 8))

    for level in (3, 2, 1):

        @pl.when(jnp.logical_and(q != holder[level], jnp.logical_not(jnp.logical_and(z == NZ - 1, level == 3))))
        def _(level=level):
            greet(at(x, holder[level]))

    @pl.when(jnp.logical_and(z < 4, x == 2))
    def _():
        for xx in range(NX):
            greet(at(xx, mirror))
        for xx in (0, 1, 3):
            greet(at(xx, q))

    @pl.when(jnp.logical_and(z < 4, lax.rem(x, 2) == 1))
    def _():
        greet(at(x, mirror))
        greet(at(x - 1, mirror))
        greet(at(x - 1, q))

    early = jnp.where(c == 1, 1, 0)
    early = early + jnp.where(sends_six, 1, 0) + jnp.where(sends_five, 1, 0)
    early = early + jnp.where(is_relay, 4 + NX * NY, 0) + jnp.where(is_near, 2 + jnp.where(starts_last, len(FIRST), 0), 0)
    early = early + jnp.where(is_second, 4, 0) + jnp.where(q == 13, 2, 0) - jnp.where(q == 12, 2, 0)
    for level, count in ((2, 3), (3, 7), (4, 9), (5, 4), (6, 2 * NX)):
        early = early + jnp.where(hosted == level, count, 0)

    loads = [
        pltpu.make_async_copy(k_in.at[1], own.at[0], load_sem.at[0]),
        pltpu.make_async_copy(v_in.at[1], own.at[1], load_sem.at[0]),
        pltpu.make_async_copy(k_in.at[0], kv.at[0, 0], load_sem.at[1]),
        pltpu.make_async_copy(v_in.at[0], kv.at[0, 1], load_sem.at[1]),
        pltpu.make_async_copy(table_in, table, load_sem.at[2]),
        pltpu.make_async_copy(qg_in, qg, load_sem.at[3]),
        pltpu.make_async_copy(kg_in, kg, load_sem.at[4]),
        pltpu.make_async_copy(q_in, q_raw, load_sem.at[5]),
        pltpu.make_async_copy(g_in, g_raw, load_sem.at[6]),
    ]
    for load in loads:
        load.start()

    @pl.when(is_relay)
    def _():
        def greet_plane(n, carry):
            there = lax.rem(plane + n, NX * NY)
            greet(at(there // NY, 1, lax.rem(there, NY)))
            return carry

        lax.fori_loop(1, NX * NY, greet_plane, 0)

    @pl.when(is_extra)
    def _():
        def greet_all(n, carry):
            greet(at(n // NY, 1, lax.rem(n, NY)))
            return carry

        lax.fori_loop(0, NX * NY, greet_all, 0)

    @pl.when(is_first)
    def _():
        for xx in range(NX):
            for yy in LAST_Y:
                greet(at(xx, 5, yy))

    settle(1, load_sem.at[0])

    pl.semaphore_wait(barrier, early)

    @pl.when(jnp.logical_and(far_owner, x == 2))
    def _():
        for relay in (5, 1):
            for xx in range(NX):
                remote(own, kv.at[6], b_send, b_recv.at[6], at(xx, relay)).start()

    @pl.when(jnp.logical_and(far_owner, x != 2))
    def _():
        for relay in (5, 1):
            for n in range(2):
                remote(own, kv.at[5], b_send, b_recv.at[5], at(x - n, relay)).start()

    for level in (4, 3, 2, 1):

        @pl.when(hosted == level)
        def _(level=level):
            half = 2 ** (level - 1)
            offsets = sorted((o for o in range(-half, half) if o), key=lambda o: -abs(o))
            if level == 4:
                offsets = [1] + [o for o in offsets if o < 0]
            for offset in offsets:
                if level == 3 and offset in (2, 3):

                    @pl.when(q != 12)
                    def _(offset=offset):
                        remote(own, kv.at[level], b_send, b_recv.at[level], at(x, q + offset)).start()

                else:
                    remote(own, kv.at[level], b_send, b_recv.at[level], at(x, q + offset)).start()
            for n in range(2):
                pltpu.make_async_copy((k_in, v_in)[n].at[1], kv.at[level, n], load_sem.at[7]).start()

    @pl.when(is_second)
    def _():
        remote(own, kv.at[4], b_send, b_recv.at[4], at(x, 8)).wait_recv()
        for qq in (13, 12, 10, 11):
            remote(kv.at[4], kv.at[4], b_send, b_recv.at[4], at(x, qq)).start()

    top_two = kv.at[pl.ds(5, 2)]

    for relay, served in SERVED:

        @pl.when(q == relay)
        def _(relay=relay, served=served):
            for level in (5, 6):
                remote(own, kv.at[level], b_send, b_recv.at[level], at(x, 0)).wait_recv()
            for qq in (*served, relay - 1):
                remote(top_two, top_two, b_send, b_recv.at[5], at(x, qq)).start()

    for load in loads[4:]:
        load.wait()
    q_gain, k_gain = qg[...], kg[...]
    leaf_len = length[0]
    place = [DEPTH * T, jnp.maximum(DEPTH - hosted, 0) * T]
    live = [
        lax.broadcasted_iota(jnp.int32, (T, D), 0) < leaf_len,
        jnp.broadcast_to(hosted <= DEPTH, (T, D)),
    ]
    for kind in range(2):
        cosine, sine = spread(table[pl.ds(pl.multiple_of(place[kind], T), T), :])
        w_cos, w_sin = [], []
        for head in range(G):
            rows = pl.ds(kind * ROWS + head * T, T)
            unit, _ = unit_of(q_raw[kind, :, head * D : (head + 1) * D].astype(F32))
            q_rot[rows, :] = turn(unit * q_gain, cosine, sine).astype(BF)
            w_cos.append(unit * cosine)
            w_sin.append(pltpu.roll(unit * sine, D // 2, axis=1))
            if head % 2:
                pair = slice(kind * ROWS + (head - 1) * T, kind * ROWS + (head + 1) * T)
                wq_cos[:, pair] = jnp.transpose(jnp.concatenate(w_cos[-2:], axis=0))
                wq_sin[:, pair] = jnp.transpose(jnp.concatenate(w_sin[-2:], axis=0))
            grad = g_raw[kind, :, head * D : (head + 1) * D]
            g_rows[rows, :] = jnp.where(live[kind], grad, jnp.zeros((), BF))

    settle(1, load_sem.at[1])

    def take(slot):
        rows = pl.ds(slot * T, T)
        cosine, sine = spread(table[(DEPTH - slot) * T : (DEPTH - slot + 1) * T, :])
        unit, _ = unit_of(kv[slot, 0].astype(F32))
        wk_cos[rows, :] = unit * cosine
        wk_sin[rows, :] = pltpu.roll(unit * sine, D // 2, axis=1)
        k_rot[rows, :] = turn(unit * k_gain, cosine, sine).astype(BF)
        v_all[rows, :] = kv[slot, 1]

    def from_holder(level):
        passed_on = {3: q == 13, 4: among((9, 13))}.get(level, False)

        @pl.when(jnp.logical_and(q != holder[level], jnp.logical_not(passed_on)))
        def _():
            remote(own, kv.at[level], b_send, b_recv.at[level], at(x, holder[level])).wait_recv()

        @pl.when(hosted == level)
        def _():
            settle(1, load_sem.at[7])

    @pl.when(q == 13)
    def _():
        remote(own, kv.at[3], b_send, b_recv.at[3], at(x, 12)).wait_recv()
        for qq in (14, 15):
            remote(kv.at[3], kv.at[3], b_send, b_recv.at[3], at(x, qq)).start()

    take(0)
    for level in (1, 2):
        from_holder(level)
        take(level)

    @pl.when(q == 13)
    def _():
        remote(own, kv.at[4], b_send, b_recv.at[4], at(x, 9)).wait_recv()
        for qq in (14, 15):
            remote(kv.at[4], kv.at[4], b_send, b_recv.at[4], at(x, qq)).start()

    @pl.when(jnp.logical_and(c == 1, jnp.logical_not(jnp.logical_or(is_relay, is_near))))
    def _():
        remote(top_two, top_two, b_send, b_recv.at[5], at(x, 1)).wait_recv()
        remote(top_two, top_two, b_send, b_recv.at[5], at(x, q - 1)).start()

    from_holder(3)
    take(3)

    key_at = lax.broadcasted_iota(jnp.int32, (T, ROWS), 0)
    row_at = lax.rem(lax.broadcasted_iota(jnp.int32, (T, ROWS), 1), T)
    ahead = key_at - row_at

    def partial(first, last, kind):
        rows = slice(kind * ROWS, (kind + 1) * ROWS)
        slots = slice(first * T, last * T)
        scores = dot(k_rot[slots, :], q_rot[rows, :], ((1,), (1,))) * SCALE
        pieces = []
        for slot in range(first, last):
            piece = scores[(slot - first) * T : (slot - first + 1) * T]
            if kind == 0:
                if slot == 0:
                    seen = jnp.logical_and(ahead <= 0, key_at < leaf_len)
                    piece = jnp.where(seen, piece, NEG_BIG)
            elif slot == 0:
                piece = jnp.full_like(piece, NEG_BIG)
            else:
                bound = jnp.where(hosted == slot, 0, jnp.where(hosted < slot, T, -T))
                piece = jnp.where(ahead <= bound, piece, NEG_BIG)
            pieces.append(piece)
        scores = jnp.concatenate(pieces, axis=0)
        top = jnp.max(scores, axis=0, keepdims=True)
        raised = jnp.exp(scores - top)
        dprobs = dot(v_all[slots, :], g_rows[rows, :], ((1,), (1,)))
        return (
            raised,
            dprobs,
            top,
            jnp.sum(raised, axis=0, keepdims=True),
            jnp.sum(raised * dprobs, axis=0, keepdims=True),
        )

    def keep(first, last, at_row, kind, rows):
        raised, products, *sums = partial(first, last, kind)
        near_e[first * T : last * T, rows] = raised
        near_d[first * T : last * T, rows] = products
        for n, line in enumerate(sums):
            near_s[at_row + n : at_row + n + 1, rows] = line

    for kind in range(2):
        rows = slice(kind * ROWS, (kind + 1) * ROWS)
        keep(0, NEAR, 0, kind, rows)

    from_holder(4)
    take(4)
    for kind in range(2):
        rows = slice(kind * ROWS, (kind + 1) * ROWS)
        keep(NEAR, MID, 3, kind, rows)

    @pl.when(c == 0)
    def _():
        remote(top_two, top_two, b_send, b_recv.at[5], at(x, 1)).wait_recv()

    take(5)
    take(6)
    for kind in range(2):
        rows = slice(kind * ROWS, (kind + 1) * ROWS)
        far_e, far_d, far_top, far_sum, far_delta = partial(MID, SLOTS, kind)
        near_top, mid_top = near_s[0:1, rows], near_s[3:4, rows]
        top = jnp.maximum(jnp.maximum(near_top, mid_top), far_top)
        near_f, mid_f, far_f = jnp.exp(near_top - top), jnp.exp(mid_top - top), jnp.exp(far_top - top)
        over = 1.0 / (near_s[1:2, rows] * near_f + near_s[4:5, rows] * mid_f + far_sum * far_f)
        near_f, mid_f, far_f = near_f * over, mid_f * over, far_f * over
        delta = near_s[2:3, rows] * near_f + near_s[5:6, rows] * mid_f + far_delta * far_f
        for first, last, factor, e, d in (
            (0, NEAR, near_f, near_e[: NEAR * T, rows], near_d[: NEAR * T, rows]),
            (NEAR, MID, mid_f, near_e[NEAR * T :, rows], near_d[NEAR * T :, rows]),
            (MID, SLOTS, far_f, far_e, far_d),
        ):
            prob = e * factor
            probs[first * T : last * T, rows] = prob.astype(BF)
            dscores[first * T : last * T, rows] = (prob * (d - delta)).astype(BF)
    dk_all = dot(dscores[...], q_rot[...], ((1,), (0,))) * SCALE
    dq_turned = dot(k_rot[...], dscores[...], ((0,), (0,))) * SCALE
    straight, crossed = dq_turned * wq_cos[...], dq_turned * wq_sin[...]
    both = straight - jnp.concatenate([crossed[D // 2 :], crossed[: D // 2]], axis=0)
    lanes = both[:, :D]
    for n in range(1, 2 * ROWS // D):
        lanes = lanes + both[:, n * D : (n + 1) * D]
    gain_q = jnp.sum(jnp.transpose(lanes), axis=0, keepdims=True)
    gain_k = jnp.sum(dk_all * wk_cos[...], axis=0, keepdims=True) - pltpu.roll(
        jnp.sum(dk_all * wk_sin[...], axis=0, keepdims=True), D // 2, axis=1
    )
    terms = jnp.concatenate([gain_q, gain_k], axis=0)
    gain_send[0] = terms

    @pl.when(direct)
    def _():
        for xx, qq, yy in FIRST:
            slot = gain_d.at[x * len(LAST_Y) + y - LAST_Y[0], q - EARLY_Q]
            remote(gain_send.at[0], slot, gd_send, gd_recv, at(xx, qq, yy)).start()

    @pl.when(jnp.logical_not(is_relay))
    def _():
        recv = gz_recv.at[jnp.where(q < EARLY_Q, 0, 1)]
        remote(gain_send.at[0], gain_z.at[lax.rem(q + NQ - 2, NQ)], gz_send, recv, at(x, 1)).start()

    dv_all = dot(probs[...], g_rows[...], ((1,), (0,)))
    for slot in range(SLOTS):
        part[slot, 0] = dk_all[slot * T : (slot + 1) * T]
        part[slot, 1] = dv_all[slot * T : (slot + 1) * T]

    for slot in range(1, SLOTS):
        send_kv[slot - 1] = part[slot].astype(BF)

    @pl.when(sends_six)
    def _():
        n = jnp.where(z >= 4, x, NX + jnp.minimum(x, 2))
        remote(send_kv.at[5], x_recv.at[n], x_sem.at[0], xr_sem, at(2, low)).start()

    @pl.when(sends_five)
    def _():
        n = jnp.where(z >= 4, 1 + lax.rem(x, 2), 0)
        remote(send_kv.at[4], x_recv.at[n], x_sem.at[1], xr_sem, at(x // 2 * 2 + 1, low)).start()

    for level in range(1, 5):

        @pl.when(q != holder[level])
        def _(level=level):
            n = lax.rem(q, 2**level)
            n = jnp.where(n > 2 ** (level - 1), n - 1, n)
            remote(send_kv.at[level - 1], z_recv.at[n], r_send, r_recv, at(x, holder[level])).start()

    y_q[...] = jnp.transpose(dq_turned)
    for kind in range(2):
        cosine, sine = spread(table[pl.ds(pl.multiple_of(place[kind], T), T), :])
        for head in range(G):
            rows = pl.ds(kind * ROWS + head * T, T)
            columns = slice(head * D, (head + 1) * D)
            raw = q_raw[kind, :, columns].astype(F32)
            unit, factor = unit_of(raw)
            scaled = unturn(y_q[rows, :], cosine, sine) * q_gain
            inner = jnp.mean(scaled * unit, axis=-1, keepdims=True)
            dq_out[kind, :, columns] = (factor * (scaled - unit * inner)).astype(BF)

    def key_gradient(raw, turned, start):
        cosine, sine = spread(table[pl.ds(start, T), :])
        unit, factor = unit_of(raw.astype(F32))
        scaled = unturn(turned, cosine, sine) * k_gain
        inner = jnp.mean(scaled * unit, axis=-1, keepdims=True)
        return (factor * (scaled - unit * inner)).astype(BF)

    dk_out[0] = key_gradient(kv[0, 0], part[0, 0], DEPTH * T)
    dv_out[0] = part[0, 1].astype(BF)

    @pl.when(is_relay)
    def _():
        def wait_lines(count, sem):
            lines = gain_z.at[pl.ds(0, count)]
            pltpu.make_async_copy(lines, lines, sem).wait()

        wait_lines(EARLY_Q - 1, gz_recv.at[0])
        line = terms + gain_z[NQ - 2]
        for n in range(EARLY_Q - 2):
            line = line + gain_z[n]
        gain_send[2] = line

        @pl.when(starts_last)
        def _():
            for xx, qq, yy in FIRST:
                remote(gain_send.at[2], gain_p.at[plane], gp_send, gp_recv, at(xx, qq, yy)).start()

        wait_lines(NQ - EARLY_Q, gz_recv.at[1])
        for n in range(EARLY_Q - 2, NQ - 2):
            line = line + gain_z[n]
        gain_send[1] = line
        gain_p[plane] = line
        for dx, dy in AWAY:
            xx, yy = lax.rem(x + dx, NX), lax.rem(y + dy, NY)
            first = jnp.logical_or(yy == 0, jnp.logical_and(xx == 0, yy == 1))

            @pl.when(jnp.logical_not(jnp.logical_and(first, starts_last)))
            def _(xx=xx, yy=yy):
                remote(gain_send.at[1], gain_p.at[plane], gp_send, gp_recv, at(xx, 1, yy)).start()

        @pl.when(jnp.logical_not(starts_last))
        def _():
            remote(gain_send.at[1], gain_p.at[plane], gp_send, gp_recv, at(0, 3, 0)).start()

    def gather(level, count):
        settle(count, xr_sem)
        total = part[level]
        for n in range(count):
            total = total + x_recv[n].astype(F32)
        part[level] = total
        send_sum[...] = total.astype(BF)

    @pl.when(jnp.logical_and(z < 4, x == 2))
    def _():
        gather(6, 2 * NX - 1)

    @pl.when(jnp.logical_and(z < 4, lax.rem(x, 2) == 1))
    def _():
        gather(5, 3)

    sums = jnp.logical_and(x > 0, jnp.logical_and(z < 4, q != 0))

    @pl.when(sums)
    def _():
        remote(send_sum, z_recv.at[q - 1], s_send, r_recv, at(x, 0)).start()

    for places, count in (((1,), 11), ((5, 9, 13), 7), ((4,), 7), ((12,), 5)):

        @pl.when(among(places))
        def _(count=count):
            settle(count, b_send)

    @pl.when(among((3, 7, 11, 15)))
    def _():
        settle(3, b_send)

    for level, count in ((2, 3), (4, 9), (5, 4), (6, 2 * NX)):

        @pl.when(hosted == level)
        def _(count=count):
            settle(count, b_send)

    @pl.when(hosted <= DEPTH)
    def _():
        size = jnp.int32(NQ)
        for level, count in ((1, 2), (2, 4), (3, 8), (5, 8), (6, 8)):
            size = jnp.where(hosted == level, count, size)
        for level in range(1, DEPTH + 1):

            @pl.when(hosted == level)
            def _(level=level):
                settle(2**level - 1 if level < 5 else NQ // 2 - 1, r_recv)

        def add(n, total):
            return total + z_recv[n].astype(F32)

        total = lax.fori_loop(0, size - 1, add, part[hosted])
        dk_out[1] = key_gradient(own[0], total[0], pl.multiple_of(place[1], T))
        dv_out[1] = total[1].astype(BF)

    @pl.when(hosted > DEPTH)
    def _():
        dk_out[1] = jnp.zeros((T, D), BF)
        dv_out[1] = jnp.zeros((T, D), BF)

    def total_of_lines(senders):
        lines = gain_p.at[pl.ds(0, senders)]
        pltpu.make_async_copy(lines, lines, gp_recv).wait()

        @pl.when(is_first)
        def _():
            pltpu.make_async_copy(gain_d, gain_d, gd_recv).wait()
            for n in range(NX * len(LAST_Y)):
                there = n // len(LAST_Y) * NY + LAST_Y[0] + n % len(LAST_Y)
                line = gain_p[there]
                for k in range(NQ - EARLY_Q):
                    line = line + gain_d[n, k]
                gain_p[there] = line

        total = gain_p[0]
        for n in range(1, NX * NY):
            total = total + gain_p[n]
        gain_total[...] = total

    def pass_on(when, targets):
        @pl.when(when)
        def _():
            for qq in targets:
                remote(gain_total, gain_total, gt_send, gt_recv, at(x, qq)).start()

    @pl.when(is_relay)
    def _():
        total_of_lines(NX * NY - 1)

    @pl.when(is_extra)
    def _():
        total_of_lines(NX * NY)

    pass_on(jnp.logical_and(is_relay, plane > 0), (3, 5, 7, 0))
    pass_on(is_extra, (5, 7, 2, 0))

    @pl.when(is_relay)
    def _():
        pltpu.make_async_copy(gain_p, gain_p, gp_send).wait()

    @pl.when(sends_six)
    def _():
        settle(1, x_sem.at[0])

    @pl.when(sends_five)
    def _():
        settle(1, x_sem.at[1])

    @pl.when(hosted < 5)
    def _():
        settle(3, r_send)

    @pl.when(hosted >= 5)
    def _():
        settle(4, r_send)

    @pl.when(sums)
    def _():
        settle(1, s_send)

    @pl.when(jnp.logical_not(is_relay))
    def _():
        pltpu.make_async_copy(gain_total, gain_total, gz_send).wait()

        @pl.when(direct)
        def _():
            sent = gain_z.at[pl.ds(0, len(FIRST))]
            pltpu.make_async_copy(sent, sent, gd_send).wait()


        @pl.when(jnp.logical_not(is_extra))
        def _():
            pltpu.make_async_copy(gain_total, gain_total, gt_recv).wait()

    pass_one = jnp.logical_and(among((3, 7, 9, 11, 13, 15)), jnp.logical_not(is_extra))
    pass_on(q == 5, (9, 11, 13, 15, 4))
    pass_on(pass_one, (q - 1,))
    dqg_out[...] = gain_total[0:1]
    dkg_out[...] = gain_total[1:2]

    def passed(when, count):
        @pl.when(when)
        def _():
            sent = gain_z.at[pl.ds(0, count)]
            pltpu.make_async_copy(sent, sent, gt_send).wait()

    passed(jnp.logical_or(is_extra, jnp.logical_and(is_relay, plane > 0)), 4)
    passed(q == 5, 5)
    passed(pass_one, 1)


def hand_over(*refs):
    copies = [pltpu.make_async_copy(refs[n], refs[5 + n], refs[10].at[n]) for n in range(5)]
    for copy in copies:
        copy.start()
    for copy in copies:
        copy.wait()


def on_device(queries, keys, values, output_gradient, q_gain, k_gain, leaf_len):
    dma = pltpu.SemaphoreType.DMA
    anywhere = pl.BlockSpec(memory_space=pl.ANY)
    in_hbm = pl.BlockSpec(memory_space=pltpu.HBM)
    results = pl.pallas_call(
        kernel,
        name="tree_backward",
        out_shape=[
            pltpu.VMEM(queries.shape, BF),
            pltpu.VMEM(keys.shape, BF),
            pltpu.VMEM(values.shape, BF),
            pltpu.VMEM((1, D), F32),
            pltpu.VMEM((1, D), F32),
        ],
        in_specs=[anywhere] * 7 + [pl.BlockSpec(memory_space=pltpu.SMEM)],
        out_specs=[pl.BlockSpec(memory_space=pltpu.VMEM)] * 5,
        scratch_shapes=[
            pltpu.VMEM((2, T, G * D), BF),
            pltpu.VMEM((2, T, G * D), BF),
            pltpu.VMEM((2, T, D), BF),
            pltpu.VMEM((SLOTS, 2, T, D), BF),
            pltpu.VMEM((1, D), F32),
            pltpu.VMEM((1, D), F32),
            pltpu.VMEM((KEYS, D), F32),
            pltpu.VMEM((2 * ROWS, D), BF),
            pltpu.VMEM((2 * ROWS, D), BF),
            pltpu.VMEM((KEYS, D), BF),
            pltpu.VMEM((KEYS, D), BF),
            pltpu.VMEM((D, 2 * ROWS), F32),
            pltpu.VMEM((D, 2 * ROWS), F32),
            pltpu.VMEM((KEYS, D), F32),
            pltpu.VMEM((KEYS, D), F32),
            pltpu.VMEM((MID * T, 2 * ROWS), F32),
            pltpu.VMEM((MID * T, 2 * ROWS), F32),
            pltpu.VMEM((8, 2 * ROWS), F32),
            pltpu.VMEM((KEYS, 2 * ROWS), BF),
            pltpu.VMEM((KEYS, 2 * ROWS), BF),
            pltpu.VMEM((SLOTS, 2, T, D), F32),
            pltpu.VMEM((2 * ROWS, D), F32),
            pltpu.VMEM((NQ, 2, T, D), BF),
            pltpu.VMEM((DEPTH, 2, T, D), BF),
            pltpu.VMEM((2, T, D), BF),
            pltpu.VMEM((2 * NX - 1, 2, T, D), BF),
            pltpu.VMEM((NQ, 2, T, D), BF),
            pltpu.VMEM((3, 2, D), F32),
            pltpu.VMEM((NQ, 2, D), F32),
            pltpu.VMEM((NX * NY, 2, D), F32),
            pltpu.VMEM((NX * len(LAST_Y), NQ - EARLY_Q, 2, D), F32),
            pltpu.VMEM((2, D), F32),
            dma((8,)),
            dma(()),
            dma((SLOTS,)),
            dma(()),
            dma(()),
            dma((2,)),
            dma(()),
            dma(()),
            dma(()),
            dma((2,)),
            dma(()),
            dma(()),
            dma(()),
            dma(()),
            dma(()),
            dma(()),
        ],
        compiler_params=pltpu.CompilerParams(
            collective_id=0, has_side_effects=True, vmem_limit_bytes=40 * 2**20
        ),
        cost_estimate=pl.CostEstimate(flops=10 * 2 * ROWS * KEYS * D, bytes_accessed=2**20, transcendentals=2 * ROWS * KEYS),
    )(
        *(
            pltpu.with_memory_space_constraint(array, pltpu.HBM)
            for array in (
                queries,
                keys,
                values,
                output_gradient,
                q_gain.reshape(1, D),
                k_gain.reshape(1, D),
                jnp.asarray(rope_table()),
            )
        ),
        leaf_len,
    )
    dq, dk, dv, dq_gain, dk_gain = pl.pallas_call(
        hand_over,
        name="hand_over",
        out_shape=[jax.ShapeDtypeStruct(r.shape, r.dtype) for r in results],
        in_specs=[anywhere] * 5,
        out_specs=[in_hbm] * 5,
        scratch_shapes=[dma((5,))],
        compiler_params=pltpu.CompilerParams(vmem_limit_bytes=8 * 2**20),
    )(*(pltpu.with_memory_space_constraint(r, pltpu.VMEM) for r in results))
    return dq, dk, dv, dq_gain.reshape(D), dk_gain.reshape(D)


def solution(mesh):
    shape = dict(mesh.shape)
    if shape != {"leaf": NX * NZ * NC, "head": NY}:
        raise ValueError("another mesh")
    split = P(None, "leaf", "head")
    return jax.shard_map(
        on_device,
        mesh=mesh,
        in_specs=(split, split, split, split, P(), P(), P("leaf")),
        out_specs=(split, split, split, P(), P()),
        check_vma=False,
    )
```

```python
import jax
import jax.numpy as jnp
import numpy as np
from jax import lax
from jax.experimental import pallas as pl
from jax.experimental.pallas import tpu as pltpu
from jax.sharding import PartitionSpec as P

NEG_BIG = -1000000000.0
NORM_EPS = 1e-06
ROPE_BASE = 1000000.0
DEPTH = 6
T = 64
D = 128
G = 8
SLOTS = DEPTH + 1
KEYS = SLOTS * T
NEAR = 4
MID = 5
ROWS = G * T
NX, NZ, NC, NY = 4, 8, 2, 8
NQ = NZ * NC
SCALE = D ** (-0.5)
BF = jnp.bfloat16
F32 = jnp.float32
MESH = pl.DeviceIdType.MESH
FIRST = ((0, 1, 0), (0, 3, 0), (0, 1, 1), (1, 1, 0), (0, 1, 2), (1, 1, 1), (2, 1, 0), (3, 1, 0))
LAST_Y = (4,5,6)
EARLY_Q = 4
SERVED = ((1, (11, 13, 15, 3)), (5, (9, 7)))
AWAY = sorted(
    ((dx, dy) for dx in range(NX) for dy in range(NY) if dx or dy),
    key=lambda step: -min(step[0], NX - step[0]) - min(step[1], NY - step[1]),
)


def rope_table():
    frequency = (ROPE_BASE ** (-(np.arange(D // 2, dtype=np.float32) * 2.0 / D))).astype(np.float32)
    angles = np.arange(KEYS, dtype=np.float32)[:, None] * frequency
    return np.concatenate([np.cos(angles), np.sin(angles)], axis=1).astype(np.float32)


def spread(table):
    lane = lax.broadcasted_iota(jnp.int32, table.shape, 1)
    other = pltpu.roll(table, D // 2, axis=1)
    low = lane < D // 2
    return jnp.where(low, table, other), jnp.where(low, -other, table)


def turn(x, cosine, sine):
    return x * cosine + pltpu.roll(x, D // 2, axis=1) * sine


def unturn(x, cosine, sine):
    return x * cosine - pltpu.roll(x, D // 2, axis=1) * sine


def unit_of(x):
    factor = lax.rsqrt(jnp.mean(x * x, axis=-1, keepdims=True) + NORM_EPS)
    return x * factor, factor


def dot(a, b, contract):
    return lax.dot_general(a, b, (contract, ((), ())), preferred_element_type=F32)


def kernel(
    q_in, k_in, v_in, g_in, qg_in, kg_in, table_in, length,
    dq_out, dk_out, dv_out, dqg_out, dkg_out,
    q_raw, g_raw, own, kv, qg, kg, table,
    q_rot, g_rows, k_rot, v_all, wq_cos, wq_sin, wk_cos, wk_sin, near_e, near_d, near_s, probs, dscores, part, y_q, ballast,
    send_kv, send_sum, x_recv, z_recv, gain_send, gain_z, gain_p, gain_d, gain_total,
    load_sem, b_send, b_recv, r_send, r_recv, x_sem, xr_sem, s_send,
    gz_send, gz_recv, gp_send, gp_recv, gd_send, gd_recv, gt_send, gt_recv,
):
    leaf = lax.axis_index("leaf")
    y = lax.axis_index("head")
    x = leaf // NQ
    q = lax.rem(leaf, NQ)
    z = q // NC
    c = lax.rem(q, NC)

    def at(xx, qq, yy=None):
        return (xx * NQ + qq, y if yy is None else yy)

    hosted = jnp.int32(1)
    for level in range(1, DEPTH + 1):
        hosted = hosted + jnp.where(lax.rem(leaf, 2**level) == 0, 1, 0)

    def remote(src, dst, send, recv, device):
        return pltpu.make_async_remote_copy(
            src_ref=src, dst_ref=dst, send_sem=send, recv_sem=recv, device_id=device, device_id_type=MESH
        )

    def settle(count, sem):
        blocks = ballast.at[pl.ds(0, count)]
        pltpu.make_async_copy(blocks, blocks, sem).wait()

    holder = {level: q // 2**level * 2**level + 2 ** (level - 1) for level in range(1, 5)}
    is_relay = q == 1
    is_near = q == 5
    is_extra = jnp.logical_and(leaf == 3, y == 0)

    def first_relay(xx, yy):
        near_zero = jnp.logical_and(yy > 0, xx + yy < 3)
        return jnp.logical_or(yy == 0, near_zero)

    is_first = jnp.logical_or(is_extra, jnp.logical_and(is_relay, first_relay(x, y)))
    is_second = q == 9
    far_owner = jnp.logical_and(q == 0, x > 0)
    plane = x * NY + y
    starts_last = jnp.logical_and(y >= LAST_Y[0], y <= LAST_Y[-1])
    direct = jnp.logical_and(starts_last, q >= EARLY_Q)
    mirror = (NZ - 1 - z) * NC + c
    low = jnp.where(z < 4, q, mirror)
    sends_six = jnp.logical_or(z >= 4, x != 2)
    sends_five = jnp.logical_or(z >= 4, lax.rem(x, 2) == 0)

    def among(places):
        here = q == places[0]
        for place in places[1:]:
            here = jnp.logical_or(here, q == place)
        return here

    barrier = pltpu.get_barrier_semaphore()

    def greet(device):
        pl.semaphore_signal(barrier, inc=1, device_id=device, device_id_type=MESH)

    @pl.when(jnp.logical_or(is_relay, is_near))
    def _():
        greet(at(2, 0))
        greet(at(x // 2 * 2 + 1, 0))

    for relay, served in SERVED:

        @pl.when(among(served))
        def _(relay=relay):
            greet(at(x, relay))

    @pl.when(among((10, 11, 12, 13)))
    def _():
        greet(at(x, 9))

    @pl.when(z == NZ - 1)
    def _():
        greet(at(x, 13))

    @pl.when(jnp.logical_or(z < 4, is_second))
    def _():
        greet(at(x, 8))

    for level in (3, 2, 1):

        @pl.when(jnp.logical_and(q != holder[level], jnp.logical_not(jnp.logical_and(z == NZ - 1, level == 3))))
        def _(level=level):
            greet(at(x, holder[level]))

    @pl.when(jnp.logical_and(z < 4, x == 2))
    def _():
        for xx in range(NX):
            greet(at(xx, mirror))
        for xx in (0, 1, 3):
            greet(at(xx, q))

    @pl.when(jnp.logical_and(z < 4, lax.rem(x, 2) == 1))
    def _():
        greet(at(x, mirror))
        greet(at(x - 1, mirror))
        greet(at(x - 1, q))

    early = jnp.where(c == 1, 1, 0)
    early = early + jnp.where(sends_six, 1, 0) + jnp.where(sends_five, 1, 0)
    early = early + jnp.where(is_relay, 4 + NX * NY, 0) + jnp.where(is_near, 2 + jnp.where(starts_last, len(FIRST), 0), 0)
    early = early + jnp.where(is_second, 4, 0) + jnp.where(q == 13, 2, 0) - jnp.where(q == 12, 2, 0)
    for level, count in ((2, 3), (3, 7), (4, 9), (5, 4), (6, 2 * NX)):
        early = early + jnp.where(hosted == level, count, 0)

    loads = [
        pltpu.make_async_copy(k_in.at[1], own.at[0], load_sem.at[0]),
        pltpu.make_async_copy(v_in.at[1], own.at[1], load_sem.at[0]),
        pltpu.make_async_copy(k_in.at[0], kv.at[0, 0], load_sem.at[1]),
        pltpu.make_async_copy(v_in.at[0], kv.at[0, 1], load_sem.at[1]),
        pltpu.make_async_copy(table_in, table, load_sem.at[2]),
        pltpu.make_async_copy(qg_in, qg, load_sem.at[3]),
        pltpu.make_async_copy(kg_in, kg, load_sem.at[4]),
        pltpu.make_async_copy(q_in, q_raw, load_sem.at[5]),
        pltpu.make_async_copy(g_in, g_raw, load_sem.at[6]),
    ]
    for load in loads:
        load.start()

    @pl.when(is_relay)
    def _():
        def greet_plane(n, carry):
            there = lax.rem(plane + n, NX * NY)
            greet(at(there // NY, 1, lax.rem(there, NY)))
            return carry

        lax.fori_loop(1, NX * NY, greet_plane, 0)

    @pl.when(is_extra)
    def _():
        def greet_all(n, carry):
            greet(at(n // NY, 1, lax.rem(n, NY)))
            return carry

        lax.fori_loop(0, NX * NY, greet_all, 0)

    @pl.when(is_first)
    def _():
        for xx in range(NX):
            for yy in LAST_Y:
                greet(at(xx, 5, yy))

    settle(1, load_sem.at[0])

    pl.semaphore_wait(barrier, early)

    @pl.when(jnp.logical_and(far_owner, x == 2))
    def _():
        for relay in (5, 1):
            for xx in range(NX):
                remote(own, kv.at[6], b_send, b_recv.at[6], at(xx, relay)).start()

    @pl.when(jnp.logical_and(far_owner, x != 2))
    def _():
        for relay in (5, 1):
            for n in range(2):
                remote(own, kv.at[5], b_send, b_recv.at[5], at(x - n, relay)).start()

    for level in (4, 3, 2, 1):

        @pl.when(hosted == level)
        def _(level=level):
            half = 2 ** (level - 1)
            offsets = sorted((o for o in range(-half, half) if o), key=lambda o: -abs(o))
            if level == 4:
                offsets = [1] + [o for o in offsets if o < 0]
            for offset in offsets:
                if level == 3 and offset in (2, 3):

                    @pl.when(q != 12)
                    def _(offset=offset):
                        remote(own, kv.at[level], b_send, b_recv.at[level], at(x, q + offset)).start()

                else:
                    remote(own, kv.at[level], b_send, b_recv.at[level], at(x, q + offset)).start()
            for n in range(2):
                pltpu.make_async_copy((k_in, v_in)[n].at[1], kv.at[level, n], load_sem.at[7]).start()

    @pl.when(is_second)
    def _():
        remote(own, kv.at[4], b_send, b_recv.at[4], at(x, 8)).wait_recv()
        for qq in (13, 12, 10, 11):
            remote(kv.at[4], kv.at[4], b_send, b_recv.at[4], at(x, qq)).start()

    top_two = kv.at[pl.ds(5, 2)]

    for relay, served in SERVED:

        @pl.when(q == relay)
        def _(relay=relay, served=served):
            for level in (5, 6):
                remote(own, kv.at[level], b_send, b_recv.at[level], at(x, 0)).wait_recv()
            for qq in (*served, relay - 1):
                remote(top_two, top_two, b_send, b_recv.at[5], at(x, qq)).start()

    @pl.when(q == 13)
    def _():
        remote(own, kv.at[3], b_send, b_recv.at[3], at(x, 12)).wait_recv()
        for qq in (14, 15):
            remote(kv.at[3], kv.at[3], b_send, b_recv.at[3], at(x, qq)).start()

    for load in loads[4:]:
        load.wait()
    q_gain, k_gain = qg[...], kg[...]
    leaf_len = length[0]
    place = [DEPTH * T, jnp.maximum(DEPTH - hosted, 0) * T]
    live = [
        lax.broadcasted_iota(jnp.int32, (T, D), 0) < leaf_len,
        jnp.broadcast_to(hosted <= DEPTH, (T, D)),
    ]
    for kind in range(2):
        cosine, sine = spread(table[pl.ds(pl.multiple_of(place[kind], T), T), :])
        w_cos, w_sin = [], []
        for head in range(G):
            rows = pl.ds(kind * ROWS + head * T, T)
            unit, _ = unit_of(q_raw[kind, :, head * D : (head + 1) * D].astype(F32))
            q_rot[rows, :] = turn(unit * q_gain, cosine, sine).astype(BF)
            w_cos.append(unit * cosine)
            w_sin.append(pltpu.roll(unit * sine, D // 2, axis=1))
            if head % 2:
                pair = slice(kind * ROWS + (head - 1) * T, kind * ROWS + (head + 1) * T)
                wq_cos[:, pair] = jnp.transpose(jnp.concatenate(w_cos[-2:], axis=0))
                wq_sin[:, pair] = jnp.transpose(jnp.concatenate(w_sin[-2:], axis=0))
            grad = g_raw[kind, :, head * D : (head + 1) * D]
            g_rows[rows, :] = jnp.where(live[kind], grad, jnp.zeros((), BF))

    settle(1, load_sem.at[1])

    def take(slot):
        rows = pl.ds(slot * T, T)
        cosine, sine = spread(table[(DEPTH - slot) * T : (DEPTH - slot + 1) * T, :])
        unit, _ = unit_of(kv[slot, 0].astype(F32))
        wk_cos[rows, :] = unit * cosine
        wk_sin[rows, :] = pltpu.roll(unit * sine, D // 2, axis=1)
        k_rot[rows, :] = turn(unit * k_gain, cosine, sine).astype(BF)
        v_all[rows, :] = kv[slot, 1]

    def from_holder(level):
        passed_on = {3: q == 13, 4: among((9, 13))}.get(level, False)

        @pl.when(jnp.logical_and(q != holder[level], jnp.logical_not(passed_on)))
        def _():
            remote(own, kv.at[level], b_send, b_recv.at[level], at(x, holder[level])).wait_recv()

        @pl.when(hosted == level)
        def _():
            settle(1, load_sem.at[7])

    @pl.when(q == 13)
    def _():
        remote(own, kv.at[4], b_send, b_recv.at[4], at(x, 9)).wait_recv()
        for qq in (14, 15):
            remote(kv.at[4], kv.at[4], b_send, b_recv.at[4], at(x, qq)).start()

    take(0)
    for level in (1, 2):
        from_holder(level)
        take(level)

    @pl.when(jnp.logical_and(c == 1, jnp.logical_not(jnp.logical_or(is_relay, is_near))))
    def _():
        remote(top_two, top_two, b_send, b_recv.at[5], at(x, 1)).wait_recv()
        remote(top_two, top_two, b_send, b_recv.at[5], at(x, q - 1)).start()

    from_holder(3)
    take(3)

    key_at = lax.broadcasted_iota(jnp.int32, (T, ROWS), 0)
    row_at = lax.rem(lax.broadcasted_iota(jnp.int32, (T, ROWS), 1), T)
    ahead = key_at - row_at

    def partial(first, last, kind):
        rows = slice(kind * ROWS, (kind + 1) * ROWS)
        slots = slice(first * T, last * T)
        scores = dot(k_rot[slots, :], q_rot[rows, :], ((1,), (1,))) * SCALE
        pieces = []
        for slot in range(first, last):
            piece = scores[(slot - first) * T : (slot - first + 1) * T]
            if kind == 0:
                if slot == 0:
                    seen = jnp.logical_and(ahead <= 0, key_at < leaf_len)
                    piece = jnp.where(seen, piece, NEG_BIG)
            elif slot == 0:
                piece = jnp.full_like(piece, NEG_BIG)
            else:
                bound = jnp.where(hosted == slot, 0, jnp.where(hosted < slot, T, -T))
                piece = jnp.where(ahead <= bound, piece, NEG_BIG)
            pieces.append(piece)
        scores = jnp.concatenate(pieces, axis=0)
        top = jnp.max(scores, axis=0, keepdims=True)
        raised = jnp.exp(scores - top)
        dprobs = dot(v_all[slots, :], g_rows[rows, :], ((1,), (1,)))
        return (
            raised,
            dprobs,
            top,
            jnp.sum(raised, axis=0, keepdims=True),
            jnp.sum(raised * dprobs, axis=0, keepdims=True),
        )

    def keep(first, last, at_row, kind, rows):
        raised, products, *sums = partial(first, last, kind)
        near_e[first * T : last * T, rows] = raised
        near_d[first * T : last * T, rows] = products
        for n, line in enumerate(sums):
            near_s[at_row + n : at_row + n + 1, rows] = line

    for kind in range(2):
        rows = slice(kind * ROWS, (kind + 1) * ROWS)
        keep(0, NEAR, 0, kind, rows)

    from_holder(4)
    take(4)
    for kind in range(2):
        rows = slice(kind * ROWS, (kind + 1) * ROWS)
        keep(NEAR, MID, 3, kind, rows)

    @pl.when(c == 0)
    def _():
        remote(top_two, top_two, b_send, b_recv.at[5], at(x, 1)).wait_recv()

    take(5)
    take(6)
    for kind in range(2):
        rows = slice(kind * ROWS, (kind + 1) * ROWS)
        far_e, far_d, far_top, far_sum, far_delta = partial(MID, SLOTS, kind)
        near_top, mid_top = near_s[0:1, rows], near_s[3:4, rows]
        top = jnp.maximum(jnp.maximum(near_top, mid_top), far_top)
        near_f, mid_f, far_f = jnp.exp(near_top - top), jnp.exp(mid_top - top), jnp.exp(far_top - top)
        over = 1.0 / (near_s[1:2, rows] * near_f + near_s[4:5, rows] * mid_f + far_sum * far_f)
        near_f, mid_f, far_f = near_f * over, mid_f * over, far_f * over
        delta = near_s[2:3, rows] * near_f + near_s[5:6, rows] * mid_f + far_delta * far_f
        for first, last, factor, e, d in (
            (0, NEAR, near_f, near_e[: NEAR * T, rows], near_d[: NEAR * T, rows]),
            (NEAR, MID, mid_f, near_e[NEAR * T :, rows], near_d[NEAR * T :, rows]),
            (MID, SLOTS, far_f, far_e, far_d),
        ):
            prob = e * factor
            probs[first * T : last * T, rows] = prob.astype(BF)
            dscores[first * T : last * T, rows] = (prob * (d - delta)).astype(BF)
    dk_all = dot(dscores[...], q_rot[...], ((1,), (0,))) * SCALE
    dq_turned = dot(k_rot[...], dscores[...], ((0,), (0,))) * SCALE
    straight, crossed = dq_turned * wq_cos[...], dq_turned * wq_sin[...]
    both = straight - jnp.concatenate([crossed[D // 2 :], crossed[: D // 2]], axis=0)
    lanes = both[:, :D]
    for n in range(1, 2 * ROWS // D):
        lanes = lanes + both[:, n * D : (n + 1) * D]
    gain_q = jnp.sum(jnp.transpose(lanes), axis=0, keepdims=True)
    gain_k = jnp.sum(dk_all * wk_cos[...], axis=0, keepdims=True) - pltpu.roll(
        jnp.sum(dk_all * wk_sin[...], axis=0, keepdims=True), D // 2, axis=1
    )
    terms = jnp.concatenate([gain_q, gain_k], axis=0)
    gain_send[0] = terms

    @pl.when(direct)
    def _():
        for xx, qq, yy in FIRST:
            slot = gain_d.at[x * len(LAST_Y) + y - LAST_Y[0], q - EARLY_Q]
            remote(gain_send.at[0], slot, gd_send, gd_recv, at(xx, qq, yy)).start()

    @pl.when(jnp.logical_not(is_relay))
    def _():
        recv = gz_recv.at[jnp.where(q < EARLY_Q, 0, 1)]
        remote(gain_send.at[0], gain_z.at[lax.rem(q + NQ - 2, NQ)], gz_send, recv, at(x, 1)).start()

    dv_all = dot(probs[...], g_rows[...], ((1,), (0,)))
    for slot in range(SLOTS):
        part[slot, 0] = dk_all[slot * T : (slot + 1) * T]
        part[slot, 1] = dv_all[slot * T : (slot + 1) * T]

    for slot in range(1, SLOTS):
        send_kv[slot - 1] = part[slot].astype(BF)

    @pl.when(sends_six)
    def _():
        n = jnp.where(z >= 4, x, NX + jnp.minimum(x, 2))
        remote(send_kv.at[5], x_recv.at[n], x_sem.at[0], xr_sem, at(2, low)).start()

    @pl.when(sends_five)
    def _():
        n = jnp.where(z >= 4, 1 + lax.rem(x, 2), 0)
        remote(send_kv.at[4], x_recv.at[n], x_sem.at[1], xr_sem, at(x // 2 * 2 + 1, low)).start()

    for level in range(1, 5):

        @pl.when(q != holder[level])
        def _(level=level):
            n = lax.rem(q, 2**level)
            n = jnp.where(n > 2 ** (level - 1), n - 1, n)
            remote(send_kv.at[level - 1], z_recv.at[n], r_send, r_recv, at(x, holder[level])).start()

    y_q[...] = jnp.transpose(dq_turned)
    for kind in range(2):
        cosine, sine = spread(table[pl.ds(pl.multiple_of(place[kind], T), T), :])
        for head in range(G):
            rows = pl.ds(kind * ROWS + head * T, T)
            columns = slice(head * D, (head + 1) * D)
            raw = q_raw[kind, :, columns].astype(F32)
            unit, factor = unit_of(raw)
            scaled = unturn(y_q[rows, :], cosine, sine) * q_gain
            inner = jnp.mean(scaled * unit, axis=-1, keepdims=True)
            dq_out[kind, :, columns] = (factor * (scaled - unit * inner)).astype(BF)

    def key_gradient(raw, turned, start):
        cosine, sine = spread(table[pl.ds(start, T), :])
        unit, factor = unit_of(raw.astype(F32))
        scaled = unturn(turned, cosine, sine) * k_gain
        inner = jnp.mean(scaled * unit, axis=-1, keepdims=True)
        return (factor * (scaled - unit * inner)).astype(BF)

    dk_out[0] = key_gradient(kv[0, 0], part[0, 0], DEPTH * T)
    dv_out[0] = part[0, 1].astype(BF)

    @pl.when(is_relay)
    def _():
        def wait_lines(count, sem):
            lines = gain_z.at[pl.ds(0, count)]
            pltpu.make_async_copy(lines, lines, sem).wait()

        wait_lines(EARLY_Q - 1, gz_recv.at[0])
        line = terms + gain_z[NQ - 2]
        for n in range(EARLY_Q - 2):
            line = line + gain_z[n]
        gain_send[2] = line

        @pl.when(starts_last)
        def _():
            for xx, qq, yy in FIRST:
                remote(gain_send.at[2], gain_p.at[plane], gp_send, gp_recv, at(xx, qq, yy)).start()

        wait_lines(NQ - EARLY_Q, gz_recv.at[1])
        for n in range(EARLY_Q - 2, NQ - 2):
            line = line + gain_z[n]
        gain_send[1] = line
        gain_p[plane] = line
        for dx, dy in AWAY:
            xx, yy = lax.rem(x + dx, NX), lax.rem(y + dy, NY)
            first = first_relay(xx, yy)

            @pl.when(jnp.logical_not(jnp.logical_and(first, starts_last)))
            def _(xx=xx, yy=yy):
                remote(gain_send.at[1], gain_p.at[plane], gp_send, gp_recv, at(xx, 1, yy)).start()

        @pl.when(jnp.logical_not(starts_last))
        def _():
            remote(gain_send.at[1], gain_p.at[plane], gp_send, gp_recv, at(0, 3, 0)).start()

    def gather(level, count):
        settle(count, xr_sem)
        total = part[level]
        for n in range(count):
            total = total + x_recv[n].astype(F32)
        part[level] = total
        send_sum[...] = total.astype(BF)

    @pl.when(jnp.logical_and(z < 4, x == 2))
    def _():
        gather(6, 2 * NX - 1)

    @pl.when(jnp.logical_and(z < 4, lax.rem(x, 2) == 1))
    def _():
        gather(5, 3)

    sums = jnp.logical_and(x > 0, jnp.logical_and(z < 4, q != 0))

    @pl.when(sums)
    def _():
        remote(send_sum, z_recv.at[q - 1], s_send, r_recv, at(x, 0)).start()

    for places, count in (((1,), 11), ((5, 9, 13), 7), ((4,), 7), ((12,), 5)):

        @pl.when(among(places))
        def _(count=count):
            settle(count, b_send)

    @pl.when(among((3, 7, 11, 15)))
    def _():
        settle(3, b_send)

    for level, count in ((2, 3), (4, 9), (5, 4), (6, 2 * NX)):

        @pl.when(hosted == level)
        def _(count=count):
            settle(count, b_send)

    @pl.when(hosted <= DEPTH)
    def _():
        size = jnp.int32(NQ)
        for level, count in ((1, 2), (2, 4), (3, 8), (5, 8), (6, 8)):
            size = jnp.where(hosted == level, count, size)
        for level in range(1, DEPTH + 1):

            @pl.when(hosted == level)
            def _(level=level):
                settle(2**level - 1 if level < 5 else NQ // 2 - 1, r_recv)

        def add(n, total):
            return total + z_recv[n].astype(F32)

        total = lax.fori_loop(0, size - 1, add, part[hosted])
        dk_out[1] = key_gradient(own[0], total[0], pl.multiple_of(place[1], T))
        dv_out[1] = total[1].astype(BF)

    @pl.when(hosted > DEPTH)
    def _():
        dk_out[1] = jnp.zeros((T, D), BF)
        dv_out[1] = jnp.zeros((T, D), BF)

    def total_of_lines(senders):
        lines = gain_p.at[pl.ds(0, senders)]
        pltpu.make_async_copy(lines, lines, gp_recv).wait()

        @pl.when(is_first)
        def _():
            pltpu.make_async_copy(gain_d, gain_d, gd_recv).wait()
            for n in range(NX * len(LAST_Y)):
                there = n // len(LAST_Y) * NY + LAST_Y[0] + n % len(LAST_Y)
                line = gain_p[there]
                for k in range(NQ - EARLY_Q):
                    line = line + gain_d[n, k]
                gain_p[there] = line

        total = gain_p[0]
        for n in range(1, NX * NY):
            total = total + gain_p[n]
        gain_total[...] = total

    def pass_on(when, targets):
        @pl.when(when)
        def _():
            for qq in targets:
                remote(gain_total, gain_total, gt_send, gt_recv, at(x, qq)).start()

    @pl.when(is_relay)
    def _():
        total_of_lines(NX * NY - 1)

    @pl.when(is_extra)
    def _():
        total_of_lines(NX * NY)

    pass_on(jnp.logical_and(is_relay, plane > 0), (3, 5, 7, 0))
    pass_on(is_extra, (5, 7, 2, 0))

    @pl.when(is_relay)
    def _():
        pltpu.make_async_copy(gain_p, gain_p, gp_send).wait()

    @pl.when(sends_six)
    def _():
        settle(1, x_sem.at[0])

    @pl.when(sends_five)
    def _():
        settle(1, x_sem.at[1])

    @pl.when(hosted < 5)
    def _():
        settle(3, r_send)

    @pl.when(hosted >= 5)
    def _():
        settle(4, r_send)

    @pl.when(sums)
    def _():
        settle(1, s_send)

    @pl.when(jnp.logical_not(is_relay))
    def _():
        pltpu.make_async_copy(gain_total, gain_total, gz_send).wait()

        @pl.when(direct)
        def _():
            sent = gain_z.at[pl.ds(0, len(FIRST))]
            pltpu.make_async_copy(sent, sent, gd_send).wait()


        @pl.when(jnp.logical_not(is_extra))
        def _():
            pltpu.make_async_copy(gain_total, gain_total, gt_recv).wait()

    pass_one = jnp.logical_and(among((3, 7, 9, 11, 13, 15)), jnp.logical_not(is_extra))
    pass_on(q == 5, (9, 11, 13, 15, 4))
    pass_on(pass_one, (q - 1,))
    dqg_out[...] = gain_total[0:1]
    dkg_out[...] = gain_total[1:2]

    def passed(when, count):
        @pl.when(when)
        def _():
            sent = gain_z.at[pl.ds(0, count)]
            pltpu.make_async_copy(sent, sent, gt_send).wait()

    passed(jnp.logical_or(is_extra, jnp.logical_and(is_relay, plane > 0)), 4)
    passed(q == 5, 5)
    passed(pass_one, 1)


def hand_over(*refs):
    copies = [pltpu.make_async_copy(refs[n], refs[5 + n], refs[10].at[n]) for n in range(5)]
    for copy in copies:
        copy.start()
    for copy in copies:
        copy.wait()


def on_device(queries, keys, values, output_gradient, q_gain, k_gain, leaf_len):
    dma = pltpu.SemaphoreType.DMA
    anywhere = pl.BlockSpec(memory_space=pl.ANY)
    in_hbm = pl.BlockSpec(memory_space=pltpu.HBM)
    results = pl.pallas_call(
        kernel,
        name="tree_backward",
        out_shape=[
            pltpu.VMEM(queries.shape, BF),
            pltpu.VMEM(keys.shape, BF),
            pltpu.VMEM(values.shape, BF),
            pltpu.VMEM((1, D), F32),
            pltpu.VMEM((1, D), F32),
        ],
        in_specs=[anywhere] * 7 + [pl.BlockSpec(memory_space=pltpu.SMEM)],
        out_specs=[pl.BlockSpec(memory_space=pltpu.VMEM)] * 5,
        scratch_shapes=[
            pltpu.VMEM((2, T, G * D), BF),
            pltpu.VMEM((2, T, G * D), BF),
            pltpu.VMEM((2, T, D), BF),
            pltpu.VMEM((SLOTS, 2, T, D), BF),
            pltpu.VMEM((1, D), F32),
            pltpu.VMEM((1, D), F32),
            pltpu.VMEM((KEYS, D), F32),
            pltpu.VMEM((2 * ROWS, D), BF),
            pltpu.VMEM((2 * ROWS, D), BF),
            pltpu.VMEM((KEYS, D), BF),
            pltpu.VMEM((KEYS, D), BF),
            pltpu.VMEM((D, 2 * ROWS), F32),
            pltpu.VMEM((D, 2 * ROWS), F32),
            pltpu.VMEM((KEYS, D), F32),
            pltpu.VMEM((KEYS, D), F32),
            pltpu.VMEM((MID * T, 2 * ROWS), F32),
            pltpu.VMEM((MID * T, 2 * ROWS), F32),
            pltpu.VMEM((8, 2 * ROWS), F32),
            pltpu.VMEM((KEYS, 2 * ROWS), BF),
            pltpu.VMEM((KEYS, 2 * ROWS), BF),
            pltpu.VMEM((SLOTS, 2, T, D), F32),
            pltpu.VMEM((2 * ROWS, D), F32),
            pltpu.VMEM((NQ, 2, T, D), BF),
            pltpu.VMEM((DEPTH, 2, T, D), BF),
            pltpu.VMEM((2, T, D), BF),
            pltpu.VMEM((2 * NX - 1, 2, T, D), BF),
            pltpu.VMEM((NQ, 2, T, D), BF),
            pltpu.VMEM((3, 2, D), F32),
            pltpu.VMEM((NQ, 2, D), F32),
            pltpu.VMEM((NX * NY, 2, D), F32),
            pltpu.VMEM((NX * len(LAST_Y), NQ - EARLY_Q, 2, D), F32),
            pltpu.VMEM((2, D), F32),
            dma((8,)),
            dma(()),
            dma((SLOTS,)),
            dma(()),
            dma(()),
            dma((2,)),
            dma(()),
            dma(()),
            dma(()),
            dma((2,)),
            dma(()),
            dma(()),
            dma(()),
            dma(()),
            dma(()),
            dma(()),
        ],
        compiler_params=pltpu.CompilerParams(
            collective_id=0, has_side_effects=True, vmem_limit_bytes=40 * 2**20
        ),
        cost_estimate=pl.CostEstimate(flops=10 * 2 * ROWS * KEYS * D, bytes_accessed=2**20, transcendentals=2 * ROWS * KEYS),
    )(
        *(
            pltpu.with_memory_space_constraint(array, pltpu.HBM)
            for array in (
                queries,
                keys,
                values,
                output_gradient,
                q_gain.reshape(1, D),
                k_gain.reshape(1, D),
                jnp.asarray(rope_table()),
            )
        ),
        leaf_len,
    )
    dq, dk, dv, dq_gain, dk_gain = pl.pallas_call(
        hand_over,
        name="hand_over",
        out_shape=[jax.ShapeDtypeStruct(r.shape, r.dtype) for r in results],
        in_specs=[anywhere] * 5,
        out_specs=[in_hbm] * 5,
        scratch_shapes=[dma((5,))],
        compiler_params=pltpu.CompilerParams(vmem_limit_bytes=8 * 2**20),
    )(*(pltpu.with_memory_space_constraint(r, pltpu.VMEM) for r in results))
    return dq, dk, dv, dq_gain.reshape(D), dk_gain.reshape(D)


def solution(mesh):
    shape = dict(mesh.shape)
    if shape != {"leaf": NX * NZ * NC, "head": NY}:
        raise ValueError("another mesh")
    split = P(None, "leaf", "head")
    return jax.shard_map(
        on_device,
        mesh=mesh,
        in_specs=(split, split, split, split, P(), P(), P("leaf")),
        out_specs=(split, split, split, P(), P()),
        check_vma=False,
    )
```

```python
import jax
import jax.numpy as jnp
import numpy as np
from jax import lax
from jax.experimental import pallas as pl
from jax.experimental.pallas import tpu as pltpu
from jax.sharding import PartitionSpec as P

NEG_BIG = -1000000000.0
NORM_EPS = 1e-06
ROPE_BASE = 1000000.0
DEPTH = 6
T = 64
D = 128
G = 8
SLOTS = DEPTH + 1
KEYS = SLOTS * T
GROUPS = ((0, 3), (3, 5), (5, 6), (6, 7))

ROWS = G * T
NX, NZ, NC, NY = 4, 8, 2, 8
NQ = NZ * NC
SCALE = D ** (-0.5)
BF = jnp.bfloat16
F32 = jnp.float32
MESH = pl.DeviceIdType.MESH
FIRST = ((0, 1, 0), (0, 3, 0), (0, 1, 1), (1, 1, 0), (0, 1, 2), (1, 1, 1), (2, 1, 0), (3, 1, 0))
LAST_Y = (4,5,6)
EARLY_Q = 4
SERVED = ((1, (11, 13, 15, 3)), (5, (8, 9, 7)))
AWAY = sorted(
    ((dx, dy) for dx in range(NX) for dy in range(NY) if dx or dy),
    key=lambda step: -min(step[0], NX - step[0]) - min(step[1], NY - step[1]),
)


def rope_table():
    frequency = (ROPE_BASE ** (-(np.arange(D // 2, dtype=np.float32) * 2.0 / D))).astype(np.float32)
    angles = np.arange(KEYS, dtype=np.float32)[:, None] * frequency
    return np.concatenate([np.cos(angles), np.sin(angles)], axis=1).astype(np.float32)


def spread(table):
    lane = lax.broadcasted_iota(jnp.int32, table.shape, 1)
    other = pltpu.roll(table, D // 2, axis=1)
    low = lane < D // 2
    return jnp.where(low, table, other), jnp.where(low, -other, table)


def turn(x, cosine, sine):
    return x * cosine + pltpu.roll(x, D // 2, axis=1) * sine


def unturn(x, cosine, sine):
    return x * cosine - pltpu.roll(x, D // 2, axis=1) * sine


def unit_of(x):
    factor = lax.rsqrt(jnp.mean(x * x, axis=-1, keepdims=True) + NORM_EPS)
    return x * factor, factor


def tree_sum(terms):
    while len(terms) > 1:
        terms = [sum(terms[n + 1 : n + 2], terms[n]) for n in range(0, len(terms), 2)]
    return terms[0]


def dot(a, b, contract):
    return lax.dot_general(a, b, (contract, ((), ())), preferred_element_type=F32)


def kernel(
    q_in, k_in, v_in, g_in, qg_in, kg_in, table_in, length,
    dq_out, dk_out, dv_out, dqg_out, dkg_out,
    q_raw, g_raw, own, kv, qg, kg, table,
    q_rot, g_rows, k_rot, v_all, wq_cos, wq_sin, wk_cos, wk_sin, near_e, near_d, near_s, probs, dscores, part, y_q, ballast,
    send_kv, send_sum, x_recv, z_recv, gain_send, gain_z, gain_p, gain_d, gain_total,
    load_sem, b_send, b_recv, r_send, r_recv, x_sem, xr_sem, s_send,
    gz_send, gz_recv, gp_send, gp_recv, gd_send, gd_recv, gt_send, gt_recv,
):
    leaf = lax.axis_index("leaf")
    y = lax.axis_index("head")
    x = leaf // NQ
    q = lax.rem(leaf, NQ)
    z = q // NC
    c = lax.rem(q, NC)

    def at(xx, qq, yy=None):
        return (xx * NQ + qq, y if yy is None else yy)

    hosted = jnp.int32(1)
    for level in range(1, DEPTH + 1):
        hosted = hosted + jnp.where(lax.rem(leaf, 2**level) == 0, 1, 0)

    def remote(src, dst, send, recv, device):
        return pltpu.make_async_remote_copy(
            src_ref=src, dst_ref=dst, send_sem=send, recv_sem=recv, device_id=device, device_id_type=MESH
        )

    def settle(count, sem):
        blocks = ballast.at[pl.ds(0, count)]
        pltpu.make_async_copy(blocks, blocks, sem).wait()

    holder = {level: q // 2**level * 2**level + 2 ** (level - 1) for level in range(1, 5)}
    is_relay = q == 1
    is_near = q == 5
    is_extra = jnp.logical_and(leaf == 3, y == 0)

    def first_relay(xx, yy):
        near_zero = jnp.logical_and(yy > 0, xx + yy < 3)
        return jnp.logical_or(yy == 0, near_zero)

    is_first = jnp.logical_or(is_extra, jnp.logical_and(is_relay, first_relay(x, y)))
    is_second = q == 9
    far_owner = jnp.logical_and(q == 0, x > 0)
    plane = x * NY + y
    starts_last = jnp.logical_and(y >= LAST_Y[0], y <= LAST_Y[-1])
    direct = jnp.logical_and(starts_last, q >= EARLY_Q)
    mirror = (NZ - 1 - z) * NC + c
    low = jnp.where(z < 4, q, mirror)
    sends_six = jnp.logical_or(z >= 4, x != 2)
    sends_five = jnp.logical_or(z >= 4, lax.rem(x, 2) == 0)

    def among(places):
        here = q == places[0]
        for place in places[1:]:
            here = jnp.logical_or(here, q == place)
        return here

    barrier = pltpu.get_barrier_semaphore()

    def greet(device):
        pl.semaphore_signal(barrier, inc=1, device_id=device, device_id_type=MESH)

    @pl.when(jnp.logical_or(is_relay, is_near))
    def _():
        greet(at(2, 0))
        greet(at(x // 2 * 2 + 1, 0))

    for relay, served in SERVED:

        @pl.when(among(served))
        def _(relay=relay):
            greet(at(x, relay))

    @pl.when(among((10, 11, 12, 13)))
    def _():
        greet(at(x, 9))

    @pl.when(z == NZ - 1)
    def _():
        greet(at(x, 13))

    @pl.when(jnp.logical_or(z < 4, is_second))
    def _():
        greet(at(x, 8))

    for level in (3, 2, 1):

        @pl.when(jnp.logical_and(q != holder[level], jnp.logical_not(jnp.logical_and(z == NZ - 1, level == 3))))
        def _(level=level):
            greet(at(x, holder[level]))

    @pl.when(jnp.logical_and(z < 4, x == 2))
    def _():
        for xx in range(NX):
            greet(at(xx, mirror))
        for xx in (0, 1, 3):
            greet(at(xx, q))

    @pl.when(jnp.logical_and(z < 4, lax.rem(x, 2) == 1))
    def _():
        greet(at(x, mirror))
        greet(at(x - 1, mirror))
        greet(at(x - 1, q))

    early = jnp.where(c == 1, 1, 0)
    early = early + jnp.where(sends_six, 1, 0) + jnp.where(sends_five, 1, 0)
    early = early + jnp.where(is_relay, 4 + NX * NY, 0) + jnp.where(is_near, 3 + jnp.where(starts_last, len(FIRST), 0), 0)
    early = early + jnp.where(is_second, 4, 0) + jnp.where(q == 13, 2, 0) - jnp.where(q == 12, 2, 0)
    for level, count in ((2, 3), (3, 7), (4, 9), (5, 4), (6, 2 * NX)):
        early = early + jnp.where(hosted == level, count, 0)

    loads = [
        pltpu.make_async_copy(k_in.at[1], own.at[0], load_sem.at[0]),
        pltpu.make_async_copy(v_in.at[1], own.at[1], load_sem.at[0]),
        pltpu.make_async_copy(k_in.at[0], kv.at[0, 0], load_sem.at[1]),
        pltpu.make_async_copy(v_in.at[0], kv.at[0, 1], load_sem.at[1]),
        pltpu.make_async_copy(table_in, table, load_sem.at[2]),
        pltpu.make_async_copy(qg_in, qg, load_sem.at[3]),
        pltpu.make_async_copy(kg_in, kg, load_sem.at[4]),
        pltpu.make_async_copy(q_in, q_raw, load_sem.at[5]),
        pltpu.make_async_copy(g_in, g_raw, load_sem.at[6]),
    ]
    for load in loads:
        load.start()

    @pl.when(is_relay)
    def _():
        def greet_plane(n, carry):
            there = lax.rem(plane + n, NX * NY)
            greet(at(there // NY, 1, lax.rem(there, NY)))
            return carry

        lax.fori_loop(1, NX * NY, greet_plane, 0)

    @pl.when(is_extra)
    def _():
        def greet_all(n, carry):
            greet(at(n // NY, 1, lax.rem(n, NY)))
            return carry

        lax.fori_loop(0, NX * NY, greet_all, 0)

    @pl.when(is_first)
    def _():
        for xx in range(NX):
            for yy in LAST_Y:
                greet(at(xx, 5, yy))

    settle(1, load_sem.at[0])

    pl.semaphore_wait(barrier, early)

    @pl.when(jnp.logical_and(far_owner, x == 2))
    def _():
        for relay in (5, 1):
            for xx in range(NX):
                remote(own, kv.at[6], b_send, b_recv.at[6], at(xx, relay)).start()

    @pl.when(jnp.logical_and(far_owner, x != 2))
    def _():
        for relay in (5, 1):
            for n in range(2):
                remote(own, kv.at[5], b_send, b_recv.at[5], at(x - n, relay)).start()

    for level in (4, 3, 2, 1):

        @pl.when(hosted == level)
        def _(level=level):
            half = 2 ** (level - 1)
            offsets = sorted((o for o in range(-half, half) if o), key=lambda o: -abs(o))
            if level == 4:
                offsets = [1] + [o for o in offsets if o < 0]
            for offset in offsets:
                if level == 3 and offset in (2, 3):

                    @pl.when(q != 12)
                    def _(offset=offset):
                        remote(own, kv.at[level], b_send, b_recv.at[level], at(x, q + offset)).start()

                else:
                    remote(own, kv.at[level], b_send, b_recv.at[level], at(x, q + offset)).start()
            for n in range(2):
                pltpu.make_async_copy((k_in, v_in)[n].at[1], kv.at[level, n], load_sem.at[7]).start()

    @pl.when(is_second)
    def _():
        remote(own, kv.at[4], b_send, b_recv.at[4], at(x, 8)).wait_recv()
        for qq in (13, 12, 10, 11):
            remote(kv.at[4], kv.at[4], b_send, b_recv.at[4], at(x, qq)).start()

    for relay, served in SERVED:

        @pl.when(q == relay)
        def _(relay=relay, served=served):
            for level in (5, 6):
                remote(own, kv.at[level], b_send, b_recv.at[level], at(x, 0)).wait_recv()
            for qq in (*served, relay - 1):
                for level in (5, 6):
                    remote(kv.at[level], kv.at[level], b_send, b_recv.at[level], at(x, qq)).start()

    @pl.when(q == 13)
    def _():
        remote(own, kv.at[3], b_send, b_recv.at[3], at(x, 12)).wait_recv()
        for qq in (14, 15):
            remote(kv.at[3], kv.at[3], b_send, b_recv.at[3], at(x, qq)).start()

    for load in loads[4:]:
        load.wait()
    q_gain, k_gain = qg[...], kg[...]
    leaf_len = length[0]
    place = [DEPTH * T, jnp.maximum(DEPTH - hosted, 0) * T]
    live = [
        lax.broadcasted_iota(jnp.int32, (T, D), 0) < leaf_len,
        jnp.broadcast_to(hosted <= DEPTH, (T, D)),
    ]
    for kind in range(2):
        cosine, sine = spread(table[pl.ds(pl.multiple_of(place[kind], T), T), :])
        w_cos, w_sin = [], []
        for head in range(G):
            rows = pl.ds(kind * ROWS + head * T, T)
            unit, _ = unit_of(q_raw[kind, :, head * D : (head + 1) * D].astype(F32))
            q_rot[rows, :] = turn(unit * q_gain, cosine, sine).astype(BF)
            w_cos.append(unit * cosine)
            w_sin.append(pltpu.roll(unit * sine, D // 2, axis=1))
            if head % 2:
                pair = slice(kind * ROWS + (head - 1) * T, kind * ROWS + (head + 1) * T)
                wq_cos[:, pair] = jnp.transpose(jnp.concatenate(w_cos[-2:], axis=0))
                wq_sin[:, pair] = jnp.transpose(jnp.concatenate(w_sin[-2:], axis=0))
            grad = g_raw[kind, :, head * D : (head + 1) * D]
            g_rows[rows, :] = jnp.where(live[kind], grad, jnp.zeros((), BF))

    settle(1, load_sem.at[1])

    def take(slot):
        rows = pl.ds(slot * T, T)
        cosine, sine = spread(table[(DEPTH - slot) * T : (DEPTH - slot + 1) * T, :])
        unit, _ = unit_of(kv[slot, 0].astype(F32))
        wk_cos[rows, :] = unit * cosine
        wk_sin[rows, :] = pltpu.roll(unit * sine, D // 2, axis=1)
        k_rot[rows, :] = turn(unit * k_gain, cosine, sine).astype(BF)
        v_all[rows, :] = kv[slot, 1]

    def from_holder(level):
        passed_on = {3: q == 13, 4: among((9, 13))}.get(level, False)

        @pl.when(jnp.logical_and(q != holder[level], jnp.logical_not(passed_on)))
        def _():
            remote(own, kv.at[level], b_send, b_recv.at[level], at(x, holder[level])).wait_recv()

        @pl.when(hosted == level)
        def _():
            settle(1, load_sem.at[7])

    @pl.when(q == 13)
    def _():
        remote(own, kv.at[4], b_send, b_recv.at[4], at(x, 9)).wait_recv()
        for qq in (14, 15):
            remote(kv.at[4], kv.at[4], b_send, b_recv.at[4], at(x, qq)).start()

    take(0)
    for level in (1, 2):
        from_holder(level)
        take(level)

    key_at = lax.broadcasted_iota(jnp.int32, (T, ROWS), 0)
    row_at = lax.rem(lax.broadcasted_iota(jnp.int32, (T, ROWS), 1), T)
    ahead = key_at - row_at

    def partial(first, last, kind):
        rows = slice(kind * ROWS, (kind + 1) * ROWS)
        slots = slice(first * T, last * T)
        scores = dot(k_rot[slots, :], q_rot[rows, :], ((1,), (1,))) * SCALE
        pieces = []
        for slot in range(first, last):
            piece = scores[(slot - first) * T : (slot - first + 1) * T]
            if kind == 0:
                if slot == 0:
                    seen = jnp.logical_and(ahead <= 0, key_at < leaf_len)
                    piece = jnp.where(seen, piece, NEG_BIG)
            elif slot == 0:
                piece = jnp.full_like(piece, NEG_BIG)
            else:
                bound = jnp.where(hosted == slot, 0, jnp.where(hosted < slot, T, -T))
                piece = jnp.where(ahead <= bound, piece, NEG_BIG)
            pieces.append(piece)
        scores = jnp.concatenate(pieces, axis=0)
        top = jnp.max(scores, axis=0, keepdims=True)
        raised = jnp.exp(scores - top)
        dprobs = dot(v_all[slots, :], g_rows[rows, :], ((1,), (1,)))
        products = raised * dprobs
        return (
            raised,
            products,
            top,
            jnp.sum(raised, axis=0, keepdims=True),
            jnp.sum(products, axis=0, keepdims=True),
        )

    def keep(first, last, at_row, kind, rows):
        raised, products, *sums = partial(first, last, kind)
        near_e[first * T : last * T, rows] = raised
        near_d[first * T : last * T, rows] = products
        for n, line in enumerate(sums):
            near_s[at_row + n : at_row + n + 1, rows] = line

    for kind in range(2):
        rows = slice(kind * ROWS, (kind + 1) * ROWS)
        keep(0, 3, 0, kind, rows)

    @pl.when(jnp.logical_and(c == 1, jnp.logical_not(among((1, 5, 9)))))
    def _():
        for level in (5, 6):
            remote(own, kv.at[level], b_send, b_recv.at[level], at(x, 1)).wait_recv()
            remote(kv.at[level], kv.at[level], b_send, b_recv.at[level], at(x, q - 1)).start()

    from_holder(3)
    take(3)
    from_holder(4)
    take(4)
    for kind in range(2):
        rows = slice(kind * ROWS, (kind + 1) * ROWS)
        keep(3, 5, 3, kind, rows)

    def from_relay(level):
        @pl.when(jnp.logical_or(c == 0, is_second))
        def _():
            remote(own, kv.at[level], b_send, b_recv.at[level], at(x, 1)).wait_recv()

    from_relay(5)
    take(5)
    for kind in range(2):
        rows = slice(kind * ROWS, (kind + 1) * ROWS)
        keep(5, 6, 6, kind, rows)
    from_relay(6)
    take(6)

    for kind in range(2):
        rows = slice(kind * ROWS, (kind + 1) * ROWS)
        last_e, last_d, *last = partial(SLOTS - 1, SLOTS, kind)
        sums = [[near_s[3 * n + line : 3 * n + line + 1, rows] for line in range(3)] for n in range(len(GROUPS) - 1)]
        sums.append(last)
        top = sums[0][0]
        for group in sums[1:]:
            top = jnp.maximum(top, group[0])
        factors = [jnp.exp(group[0] - top) for group in sums]
        total = sums[0][1] * factors[0]
        delta = sums[0][2] * factors[0]
        for group, factor in zip(sums[1:], factors[1:]):
            total = total + group[1] * factor
            delta = delta + group[2] * factor
        over = 1.0 / total
        delta = delta * over
        for n, (first, after) in enumerate(GROUPS):
            here = slice(first * T, after * T)
            e, d = (last_e, last_d) if n == len(GROUPS) - 1 else (near_e[here, rows], near_d[here, rows])
            factor = factors[n] * over
            dscores[here, rows] = (d * factor - e * (factor * delta)).astype(BF)
            near_s[n : n + 1, rows] = factor
        near_e[(SLOTS - 1) * T :, rows] = last_e
    dk_all = dot(dscores[...], q_rot[...], ((1,), (0,))) * SCALE
    dq_turned = dot(k_rot[...], dscores[...], ((0,), (0,))) * SCALE
    lanes, crossed = None, None
    for n in range(2 * ROWS // D):
        tile = slice(n * D, (n + 1) * D)
        one, other = dq_turned[:, tile] * wq_cos[:, tile], dq_turned[:, tile] * wq_sin[:, tile]
        lanes = one if lanes is None else lanes + one
        crossed = other if crossed is None else crossed + other
    lanes = lanes - jnp.concatenate([crossed[D // 2 :], crossed[: D // 2]], axis=0)
    gain_q = jnp.sum(jnp.transpose(lanes), axis=0, keepdims=True)
    gain_k = jnp.sum(dk_all * wk_cos[...], axis=0, keepdims=True) - pltpu.roll(
        jnp.sum(dk_all * wk_sin[...], axis=0, keepdims=True), D // 2, axis=1
    )
    terms = jnp.concatenate([gain_q, gain_k], axis=0)
    gain_send[0] = terms

    @pl.when(direct)
    def _():
        for xx, qq, yy in FIRST:
            slot = gain_d.at[x * len(LAST_Y) + y - LAST_Y[0], q - EARLY_Q]
            remote(gain_send.at[0], slot, gd_send, gd_recv, at(xx, qq, yy)).start()

    @pl.when(jnp.logical_not(is_relay))
    def _():
        recv = gz_recv.at[jnp.where(q < EARLY_Q, 0, 1)]
        remote(gain_send.at[0], gain_z.at[lax.rem(q + NQ - 2, NQ)], gz_send, recv, at(x, 1)).start()

    for n, (first, after) in enumerate(GROUPS):
        here = slice(first * T, after * T)
        probs[here, :] = (near_e[here, :] * near_s[n : n + 1, :]).astype(BF)
    dv_all = dot(probs[...], g_rows[...], ((1,), (0,)))
    for slot in range(SLOTS):
        part[slot, 0] = dk_all[slot * T : (slot + 1) * T]
        part[slot, 1] = dv_all[slot * T : (slot + 1) * T]

    for slot in range(1, SLOTS):
        send_kv[slot - 1] = part[slot].astype(BF)

    @pl.when(sends_six)
    def _():
        n = jnp.where(z >= 4, x, NX + jnp.minimum(x, 2))
        remote(send_kv.at[5], x_recv.at[n], x_sem.at[0], xr_sem, at(2, low)).start()

    @pl.when(sends_five)
    def _():
        n = jnp.where(z >= 4, 1 + lax.rem(x, 2), 0)
        remote(send_kv.at[4], x_recv.at[n], x_sem.at[1], xr_sem, at(x // 2 * 2 + 1, low)).start()

    for level in range(1, 5):

        @pl.when(q != holder[level])
        def _(level=level):
            n = lax.rem(q, 2**level)
            n = jnp.where(n > 2 ** (level - 1), n - 1, n)
            remote(send_kv.at[level - 1], z_recv.at[n], r_send, r_recv, at(x, holder[level])).start()

    def wait_lines(count, sem):
        lines = gain_z.at[pl.ds(0, count)]
        pltpu.make_async_copy(lines, lines, sem).wait()

    @pl.when(is_relay)
    def _():
        wait_lines(EARLY_Q - 1, gz_recv.at[0])
        line = terms + gain_z[NQ - 2]
        for n in range(EARLY_Q - 2):
            line = line + gain_z[n]
        gain_send[2] = line

        @pl.when(starts_last)
        def _():
            for xx, qq, yy in FIRST:
                remote(gain_send.at[2], gain_p.at[plane], gp_send, gp_recv, at(xx, qq, yy)).start()

    y_q[...] = jnp.transpose(dq_turned)
    for kind in range(2):
        cosine, sine = spread(table[pl.ds(pl.multiple_of(place[kind], T), T), :])
        for head in range(G):
            rows = pl.ds(kind * ROWS + head * T, T)
            columns = slice(head * D, (head + 1) * D)
            raw = q_raw[kind, :, columns].astype(F32)
            unit, factor = unit_of(raw)
            scaled = unturn(y_q[rows, :], cosine, sine) * q_gain
            inner = jnp.mean(scaled * unit, axis=-1, keepdims=True)
            dq_out[kind, :, columns] = (factor * (scaled - unit * inner)).astype(BF)

    def key_gradient(raw, turned, start):
        cosine, sine = spread(table[pl.ds(start, T), :])
        unit, factor = unit_of(raw.astype(F32))
        scaled = unturn(turned, cosine, sine) * k_gain
        inner = jnp.mean(scaled * unit, axis=-1, keepdims=True)
        return (factor * (scaled - unit * inner)).astype(BF)

    dk_out[0] = key_gradient(kv[0, 0], part[0, 0], DEPTH * T)
    dv_out[0] = part[0, 1].astype(BF)

    @pl.when(is_relay)
    def _():
        line = gain_send[2]
        wait_lines(NQ - EARLY_Q, gz_recv.at[1])
        line = line + tree_sum([gain_z[n] for n in range(EARLY_Q - 2, NQ - 2)])
        gain_send[1] = line
        gain_p[plane] = line
        for dx, dy in AWAY:
            xx, yy = lax.rem(x + dx, NX), lax.rem(y + dy, NY)
            first = first_relay(xx, yy)

            @pl.when(jnp.logical_not(jnp.logical_and(first, starts_last)))
            def _(xx=xx, yy=yy):
                remote(gain_send.at[1], gain_p.at[plane], gp_send, gp_recv, at(xx, 1, yy)).start()

        @pl.when(jnp.logical_not(starts_last))
        def _():
            remote(gain_send.at[1], gain_p.at[plane], gp_send, gp_recv, at(0, 3, 0)).start()

    def gather(level, count):
        settle(count, xr_sem)
        total = part[level]
        for n in range(count):
            total = total + x_recv[n].astype(F32)
        part[level] = total
        send_sum[...] = total.astype(BF)

    @pl.when(jnp.logical_and(z < 4, x == 2))
    def _():
        gather(6, 2 * NX - 1)

    @pl.when(jnp.logical_and(z < 4, lax.rem(x, 2) == 1))
    def _():
        gather(5, 3)

    sums = jnp.logical_and(x > 0, jnp.logical_and(z < 4, q != 0))

    @pl.when(sums)
    def _():
        remote(send_sum, z_recv.at[q - 1], s_send, r_recv, at(x, 0)).start()

    for places, count in (((1,), 11), ((5,), 9), ((9,), 5), ((13,), 7), ((4,), 7), ((12,), 5)):

        @pl.when(among(places))
        def _(count=count):
            settle(count, b_send)

    @pl.when(among((3, 7, 11, 15)))
    def _():
        settle(3, b_send)

    for level, count in ((2, 3), (4, 9), (5, 4), (6, 2 * NX)):

        @pl.when(hosted == level)
        def _(count=count):
            settle(count, b_send)

    @pl.when(hosted <= DEPTH)
    def _():
        size = jnp.int32(NQ)
        for level, count in ((1, 2), (2, 4), (3, 8), (5, 8), (6, 8)):
            size = jnp.where(hosted == level, count, size)
        for level in range(1, DEPTH + 1):

            @pl.when(hosted == level)
            def _(level=level):
                settle(2**level - 1 if level < 5 else NQ // 2 - 1, r_recv)

        def add(n, total):
            return total + z_recv[n].astype(F32)

        total = lax.fori_loop(0, size - 1, add, part[hosted])
        dk_out[1] = key_gradient(own[0], total[0], pl.multiple_of(place[1], T))
        dv_out[1] = total[1].astype(BF)

    @pl.when(hosted > DEPTH)
    def _():
        dk_out[1] = jnp.zeros((T, D), BF)
        dv_out[1] = jnp.zeros((T, D), BF)

    last_lines = [xx * NY + yy for xx in range(NX) for yy in LAST_Y]

    def total_of_lines(senders, straight):
        lines = gain_p.at[pl.ds(0, senders)]
        pltpu.make_async_copy(lines, lines, gp_recv).wait()
        others = tree_sum([gain_p[n] for n in range(NX * NY) if n not in last_lines])
        if straight:
            pltpu.make_async_copy(gain_d, gain_d, gd_recv).wait()
        late = []
        for n, there in enumerate(last_lines):
            line = gain_p[there]
            if straight:
                line = line + tree_sum([gain_d[n, k] for k in range(NQ - EARLY_Q)])
            late.append(line)
        gain_total[...] = others + tree_sum(late)

    def pass_on(when, targets):
        @pl.when(when)
        def _():
            for qq in targets:
                remote(gain_total, gain_total, gt_send, gt_recv, at(x, qq)).start()

    @pl.when(jnp.logical_and(is_relay, is_first))
    def _():
        total_of_lines(NX * NY - 1, True)

    @pl.when(jnp.logical_and(is_relay, jnp.logical_not(is_first)))
    def _():
        total_of_lines(NX * NY - 1, False)

    @pl.when(is_extra)
    def _():
        total_of_lines(NX * NY, True)

    pass_on(jnp.logical_and(is_relay, plane > 0), (3, 5, 7, 0))
    pass_on(is_extra, (5, 7, 2, 0))

    @pl.when(is_relay)
    def _():
        pltpu.make_async_copy(gain_p, gain_p, gp_send).wait()

    @pl.when(sends_six)
    def _():
        settle(1, x_sem.at[0])

    @pl.when(sends_five)
    def _():
        settle(1, x_sem.at[1])

    @pl.when(hosted < 5)
    def _():
        settle(3, r_send)

    @pl.when(hosted >= 5)
    def _():
        settle(4, r_send)

    @pl.when(sums)
    def _():
        settle(1, s_send)

    @pl.when(jnp.logical_not(is_relay))
    def _():
        pltpu.make_async_copy(gain_total, gain_total, gz_send).wait()

        @pl.when(direct)
        def _():
            sent = gain_z.at[pl.ds(0, len(FIRST))]
            pltpu.make_async_copy(sent, sent, gd_send).wait()


        @pl.when(jnp.logical_not(is_extra))
        def _():
            pltpu.make_async_copy(gain_total, gain_total, gt_recv).wait()

    pass_one = jnp.logical_and(among((3, 7, 9, 11, 13, 15)), jnp.logical_not(is_extra))
    pass_on(q == 5, (9, 11, 13, 15, 4))
    pass_on(pass_one, (q - 1,))
    dqg_out[...] = gain_total[0:1]
    dkg_out[...] = gain_total[1:2]

    def passed(when, count):
        @pl.when(when)
        def _():
            sent = gain_z.at[pl.ds(0, count)]
            pltpu.make_async_copy(sent, sent, gt_send).wait()

    passed(jnp.logical_or(is_extra, jnp.logical_and(is_relay, plane > 0)), 4)
    passed(q == 5, 5)
    passed(pass_one, 1)


def hand_over(*refs):
    copies = [pltpu.make_async_copy(refs[n], refs[5 + n], refs[10].at[n]) for n in range(5)]
    for copy in copies:
        copy.start()
    for copy in copies:
        copy.wait()


def on_device(queries, keys, values, output_gradient, q_gain, k_gain, leaf_len):
    dma = pltpu.SemaphoreType.DMA
    anywhere = pl.BlockSpec(memory_space=pl.ANY)
    in_hbm = pl.BlockSpec(memory_space=pltpu.HBM)
    results = pl.pallas_call(
        kernel,
        name="tree_backward",
        out_shape=[
            pltpu.VMEM(queries.shape, BF),
            pltpu.VMEM(keys.shape, BF),
            pltpu.VMEM(values.shape, BF),
            pltpu.VMEM((1, D), F32),
            pltpu.VMEM((1, D), F32),
        ],
        in_specs=[anywhere] * 7 + [pl.BlockSpec(memory_space=pltpu.SMEM)],
        out_specs=[pl.BlockSpec(memory_space=pltpu.VMEM)] * 5,
        scratch_shapes=[
            pltpu.VMEM((2, T, G * D), BF),
            pltpu.VMEM((2, T, G * D), BF),
            pltpu.VMEM((2, T, D), BF),
            pltpu.VMEM((SLOTS, 2, T, D), BF),
            pltpu.VMEM((1, D), F32),
            pltpu.VMEM((1, D), F32),
            pltpu.VMEM((KEYS, D), F32),
            pltpu.VMEM((2 * ROWS, D), BF),
            pltpu.VMEM((2 * ROWS, D), BF),
            pltpu.VMEM((KEYS, D), BF),
            pltpu.VMEM((KEYS, D), BF),
            pltpu.VMEM((D, 2 * ROWS), F32),
            pltpu.VMEM((D, 2 * ROWS), F32),
            pltpu.VMEM((KEYS, D), F32),
            pltpu.VMEM((KEYS, D), F32),
            pltpu.VMEM((KEYS, 2 * ROWS), F32),
            pltpu.VMEM(((SLOTS - 1) * T, 2 * ROWS), F32),
            pltpu.VMEM((16, 2 * ROWS), F32),
            pltpu.VMEM((KEYS, 2 * ROWS), BF),
            pltpu.VMEM((KEYS, 2 * ROWS), BF),
            pltpu.VMEM((SLOTS, 2, T, D), F32),
            pltpu.VMEM((2 * ROWS, D), F32),
            pltpu.VMEM((NQ, 2, T, D), BF),
            pltpu.VMEM((DEPTH, 2, T, D), BF),
            pltpu.VMEM((2, T, D), BF),
            pltpu.VMEM((2 * NX - 1, 2, T, D), BF),
            pltpu.VMEM((NQ, 2, T, D), BF),
            pltpu.VMEM((3, 2, D), F32),
            pltpu.VMEM((NQ, 2, D), F32),
            pltpu.VMEM((NX * NY, 2, D), F32),
            pltpu.VMEM((NX * len(LAST_Y), NQ - EARLY_Q, 2, D), F32),
            pltpu.VMEM((2, D), F32),
            dma((8,)),
            dma(()),
            dma((SLOTS,)),
            dma(()),
            dma(()),
            dma((2,)),
            dma(()),
            dma(()),
            dma(()),
            dma((2,)),
            dma(()),
            dma(()),
            dma(()),
            dma(()),
            dma(()),
            dma(()),
        ],
        compiler_params=pltpu.CompilerParams(
            collective_id=0, has_side_effects=True, vmem_limit_bytes=40 * 2**20
        ),
        cost_estimate=pl.CostEstimate(flops=10 * 2 * ROWS * KEYS * D, bytes_accessed=2**20, transcendentals=2 * ROWS * KEYS),
    )(
        *(
            pltpu.with_memory_space_constraint(array, pltpu.HBM)
            for array in (
                queries,
                keys,
                values,
                output_gradient,
                q_gain.reshape(1, D),
                k_gain.reshape(1, D),
                jnp.asarray(rope_table()),
            )
        ),
        leaf_len,
    )
    dq, dk, dv, dq_gain, dk_gain = pl.pallas_call(
        hand_over,
        name="hand_over",
        out_shape=[jax.ShapeDtypeStruct(r.shape, r.dtype) for r in results],
        in_specs=[anywhere] * 5,
        out_specs=[in_hbm] * 5,
        scratch_shapes=[dma((5,))],
        compiler_params=pltpu.CompilerParams(vmem_limit_bytes=8 * 2**20),
    )(*(pltpu.with_memory_space_constraint(r, pltpu.VMEM) for r in results))
    return dq, dk, dv, dq_gain.reshape(D), dk_gain.reshape(D)


def solution(mesh):
    shape = dict(mesh.shape)
    if shape != {"leaf": NX * NZ * NC, "head": NY}:
        raise ValueError("another mesh")
    split = P(None, "leaf", "head")
    return jax.shard_map(
        on_device,
        mesh=mesh,
        in_specs=(split, split, split, split, P(), P(), P("leaf")),
        out_specs=(split, split, split, P(), P()),
        check_vma=False,
    )
```

```python
import jax
import jax.numpy as jnp
import numpy as np
from jax import lax
from jax.experimental import pallas as pl
from jax.experimental.pallas import tpu as pltpu
from jax.sharding import PartitionSpec as P

NEG_BIG = -1000000000.0
NORM_EPS = 1e-06
ROPE_BASE = 1000000.0
DEPTH = 6
T = 64
D = 128
G = 8
SLOTS = DEPTH + 1
KEYS = SLOTS * T
GROUPS = ((0, 3), (3, 5), (5, 7))

ROWS = G * T
NX, NZ, NC, NY = 4, 8, 2, 8
NQ = NZ * NC
SCALE = D ** (-0.5)
BF = jnp.bfloat16
F32 = jnp.float32
MESH = pl.DeviceIdType.MESH
FIRST = ((0, 1, 0), (0, 3, 0), (0, 1, 1), (1, 1, 0), (0, 1, 2), (1, 1, 1), (2, 1, 0), (3, 1, 0))
LAST_Y = (4,5,6)
EARLY_Q = 4
SERVED = ((1, (11, 13, 15, 3)), (5, (8, 9, 7)))
AWAY = sorted(
    ((dx, dy) for dx in range(NX) for dy in range(NY) if dx or dy),
    key=lambda step: -min(step[0], NX - step[0]) - min(step[1], NY - step[1]),
)


def rope_table():
    frequency = (ROPE_BASE ** (-(np.arange(D // 2, dtype=np.float32) * 2.0 / D))).astype(np.float32)
    angles = np.arange(KEYS, dtype=np.float32)[:, None] * frequency
    return np.concatenate([np.cos(angles), np.sin(angles)], axis=1).astype(np.float32)


def spread(table):
    lane = lax.broadcasted_iota(jnp.int32, table.shape, 1)
    other = pltpu.roll(table, D // 2, axis=1)
    low = lane < D // 2
    return jnp.where(low, table, other), jnp.where(low, -other, table)


def turn(x, cosine, sine):
    return x * cosine + pltpu.roll(x, D // 2, axis=1) * sine


def unturn(x, cosine, sine):
    return x * cosine - pltpu.roll(x, D // 2, axis=1) * sine


def unit_of(x):
    factor = lax.rsqrt(jnp.mean(x * x, axis=-1, keepdims=True) + NORM_EPS)
    return x * factor, factor


def tree_sum(terms):
    while len(terms) > 1:
        terms = [sum(terms[n + 1 : n + 2], terms[n]) for n in range(0, len(terms), 2)]
    return terms[0]


def dot(a, b, contract):
    return lax.dot_general(a, b, (contract, ((), ())), preferred_element_type=F32)


def kernel(
    q_in, k_in, v_in, g_in, qg_in, kg_in, table_in, length,
    dq_out, dk_out, dv_out, dqg_out, dkg_out,
    q_raw, g_raw, own, kv, qg, kg, table,
    q_rot, g_rows, k_rot, v_all, wq_cos, wq_sin, wk_cos, wk_sin, near_e, near_d, near_s, probs, dscores, part, y_q, ballast,
    send_kv, send_sum, x_recv, z_recv, gain_send, gain_z, gain_p, gain_d, gain_total,
    load_sem, b_send, b_recv, r_send, r_recv, x_sem, xr_sem, s_send,
    gz_send, gz_recv, gp_send, gp_recv, gd_send, gd_recv, gt_send, gt_recv,
):
    leaf = lax.axis_index("leaf")
    y = lax.axis_index("head")
    x = leaf // NQ
    q = lax.rem(leaf, NQ)
    z = q // NC
    c = lax.rem(q, NC)

    def at(xx, qq, yy=None):
        return (xx * NQ + qq, y if yy is None else yy)

    hosted = jnp.int32(1)
    for level in range(1, DEPTH + 1):
        hosted = hosted + jnp.where(lax.rem(leaf, 2**level) == 0, 1, 0)

    def remote(src, dst, send, recv, device):
        return pltpu.make_async_remote_copy(
            src_ref=src, dst_ref=dst, send_sem=send, recv_sem=recv, device_id=device, device_id_type=MESH
        )

    def settle(count, sem):
        blocks = ballast.at[pl.ds(0, count)]
        pltpu.make_async_copy(blocks, blocks, sem).wait()

    holder = {level: q // 2**level * 2**level + 2 ** (level - 1) for level in range(1, 5)}
    is_relay = q == 1
    is_near = q == 5
    is_extra = jnp.logical_and(leaf == 3, y == 0)

    def first_relay(xx, yy):
        near_zero = jnp.logical_and(yy > 0, xx + yy < 3)
        return jnp.logical_or(yy == 0, near_zero)

    is_first = jnp.logical_or(is_extra, jnp.logical_and(is_relay, first_relay(x, y)))
    is_second = q == 9
    far_owner = jnp.logical_and(q == 0, x > 0)
    plane = x * NY + y
    starts_last = jnp.logical_and(y >= LAST_Y[0], y <= LAST_Y[-1])
    direct = jnp.logical_and(starts_last, q >= EARLY_Q)
    mirror = (NZ - 1 - z) * NC + c
    low = jnp.where(z < 4, q, mirror)
    sends_six = jnp.logical_or(z >= 4, x != 2)
    sends_five = jnp.logical_or(z >= 4, lax.rem(x, 2) == 0)

    def among(places):
        here = q == places[0]
        for place in places[1:]:
            here = jnp.logical_or(here, q == place)
        return here

    barrier = pltpu.get_barrier_semaphore()

    def greet(device):
        pl.semaphore_signal(barrier, inc=1, device_id=device, device_id_type=MESH)

    @pl.when(jnp.logical_or(is_relay, is_near))
    def _():
        greet(at(2, 0))
        greet(at(x // 2 * 2 + 1, 0))

    for relay, served in SERVED:

        @pl.when(among(served))
        def _(relay=relay):
            greet(at(x, relay))

    @pl.when(among((10, 11, 12, 13)))
    def _():
        greet(at(x, 9))

    @pl.when(z == NZ - 1)
    def _():
        greet(at(x, 13))

    @pl.when(jnp.logical_or(z < 4, is_second))
    def _():
        greet(at(x, 8))

    for level in (3, 2, 1):

        @pl.when(jnp.logical_and(q != holder[level], jnp.logical_not(jnp.logical_and(z == NZ - 1, level == 3))))
        def _(level=level):
            greet(at(x, holder[level]))

    @pl.when(jnp.logical_and(z < 4, x == 2))
    def _():
        for xx in range(NX):
            greet(at(xx, mirror))
        for xx in (0, 1, 3):
            greet(at(xx, q))

    @pl.when(jnp.logical_and(z < 4, lax.rem(x, 2) == 1))
    def _():
        greet(at(x, mirror))
        greet(at(x - 1, mirror))
        greet(at(x - 1, q))

    early = jnp.where(c == 1, 1, 0)
    early = early + jnp.where(sends_six, 1, 0) + jnp.where(sends_five, 1, 0)
    early = early + jnp.where(is_relay, 4 + NX * NY, 0) + jnp.where(is_near, 3 + jnp.where(starts_last, len(FIRST), 0), 0)
    early = early + jnp.where(is_second, 4, 0) + jnp.where(q == 13, 2, 0) - jnp.where(q == 12, 2, 0)
    for level, count in ((2, 3), (3, 7), (4, 9), (5, 4), (6, 2 * NX)):
        early = early + jnp.where(hosted == level, count, 0)

    loads = [
        pltpu.make_async_copy(k_in.at[1], own.at[0], load_sem.at[0]),
        pltpu.make_async_copy(v_in.at[1], own.at[1], load_sem.at[0]),
        pltpu.make_async_copy(k_in.at[0], kv.at[0, 0], load_sem.at[1]),
        pltpu.make_async_copy(v_in.at[0], kv.at[0, 1], load_sem.at[1]),
        pltpu.make_async_copy(table_in, table, load_sem.at[2]),
        pltpu.make_async_copy(qg_in, qg, load_sem.at[3]),
        pltpu.make_async_copy(kg_in, kg, load_sem.at[4]),
        pltpu.make_async_copy(q_in, q_raw, load_sem.at[5]),
        pltpu.make_async_copy(g_in, g_raw, load_sem.at[6]),
    ]
    for load in loads:
        load.start()

    @pl.when(is_relay)
    def _():
        def greet_plane(n, carry):
            there = lax.rem(plane + n, NX * NY)
            greet(at(there // NY, 1, lax.rem(there, NY)))
            return carry

        lax.fori_loop(1, NX * NY, greet_plane, 0)

    @pl.when(is_extra)
    def _():
        def greet_all(n, carry):
            greet(at(n // NY, 1, lax.rem(n, NY)))
            return carry

        lax.fori_loop(0, NX * NY, greet_all, 0)

    @pl.when(is_first)
    def _():
        for xx in range(NX):
            for yy in LAST_Y:
                greet(at(xx, 5, yy))

    settle(1, load_sem.at[0])

    pl.semaphore_wait(barrier, early)

    @pl.when(jnp.logical_and(far_owner, x == 2))
    def _():
        for relay in (5, 1):
            for xx in range(NX):
                remote(own, kv.at[6], b_send, b_recv.at[6], at(xx, relay)).start()

    @pl.when(jnp.logical_and(far_owner, x != 2))
    def _():
        for relay in (5, 1):
            for n in range(2):
                remote(own, kv.at[5], b_send, b_recv.at[5], at(x - n, relay)).start()

    for level in (4, 3, 2, 1):

        @pl.when(hosted == level)
        def _(level=level):
            half = 2 ** (level - 1)
            offsets = sorted((o for o in range(-half, half) if o), key=lambda o: -abs(o))
            if level == 4:
                offsets = [1] + [o for o in offsets if o < 0]
            for offset in offsets:
                if level == 3 and offset in (2, 3):

                    @pl.when(q != 12)
                    def _(offset=offset):
                        remote(own, kv.at[level], b_send, b_recv.at[level], at(x, q + offset)).start()

                else:
                    remote(own, kv.at[level], b_send, b_recv.at[level], at(x, q + offset)).start()
            for n in range(2):
                pltpu.make_async_copy((k_in, v_in)[n].at[1], kv.at[level, n], load_sem.at[7]).start()

    @pl.when(is_second)
    def _():
        remote(own, kv.at[4], b_send, b_recv.at[4], at(x, 8)).wait_recv()
        for qq in (13, 12, 10, 11):
            remote(kv.at[4], kv.at[4], b_send, b_recv.at[4], at(x, qq)).start()

    for relay, served in SERVED:

        @pl.when(q == relay)
        def _(relay=relay, served=served):
            for level in (5, 6):
                remote(own, kv.at[level], b_send, b_recv.at[level], at(x, 0)).wait_recv()
            for qq in (*served, relay - 1):
                for level in (5, 6):
                    remote(kv.at[level], kv.at[level], b_send, b_recv.at[level], at(x, qq)).start()

    @pl.when(q == 13)
    def _():
        remote(own, kv.at[3], b_send, b_recv.at[3], at(x, 12)).wait_recv()
        for qq in (14, 15):
            remote(kv.at[3], kv.at[3], b_send, b_recv.at[3], at(x, qq)).start()

    for load in loads[4:]:
        load.wait()
    q_gain, k_gain = qg[...], kg[...]
    leaf_len = length[0]
    place = [DEPTH * T, jnp.maximum(DEPTH - hosted, 0) * T]
    live = [
        lax.broadcasted_iota(jnp.int32, (T, D), 0) < leaf_len,
        jnp.broadcast_to(hosted <= DEPTH, (T, D)),
    ]
    for kind in range(2):
        cosine, sine = spread(table[pl.ds(pl.multiple_of(place[kind], T), T), :])
        w_cos, w_sin = [], []
        for head in range(G):
            rows = pl.ds(kind * ROWS + head * T, T)
            unit, _ = unit_of(q_raw[kind, :, head * D : (head + 1) * D].astype(F32))
            q_rot[rows, :] = turn(unit * q_gain, cosine, sine).astype(BF)
            w_cos.append(unit * cosine)
            w_sin.append(pltpu.roll(unit * sine, D // 2, axis=1))
            if head % 2:
                pair = slice(kind * ROWS + (head - 1) * T, kind * ROWS + (head + 1) * T)
                wq_cos[:, pair] = jnp.transpose(jnp.concatenate(w_cos[-2:], axis=0))
                wq_sin[:, pair] = jnp.transpose(jnp.concatenate(w_sin[-2:], axis=0))
            grad = g_raw[kind, :, head * D : (head + 1) * D]
            g_rows[rows, :] = jnp.where(live[kind], grad, jnp.zeros((), BF))

    settle(1, load_sem.at[1])

    def take(slot):
        rows = pl.ds(slot * T, T)
        cosine, sine = spread(table[(DEPTH - slot) * T : (DEPTH - slot + 1) * T, :])
        unit, _ = unit_of(kv[slot, 0].astype(F32))
        wk_cos[rows, :] = unit * cosine
        wk_sin[rows, :] = pltpu.roll(unit * sine, D // 2, axis=1)
        k_rot[rows, :] = turn(unit * k_gain, cosine, sine).astype(BF)
        v_all[rows, :] = kv[slot, 1]

    def from_holder(level):
        passed_on = {3: q == 13, 4: among((9, 13))}.get(level, False)

        @pl.when(jnp.logical_and(q != holder[level], jnp.logical_not(passed_on)))
        def _():
            remote(own, kv.at[level], b_send, b_recv.at[level], at(x, holder[level])).wait_recv()

        @pl.when(hosted == level)
        def _():
            settle(1, load_sem.at[7])

    @pl.when(q == 13)
    def _():
        remote(own, kv.at[4], b_send, b_recv.at[4], at(x, 9)).wait_recv()
        for qq in (14, 15):
            remote(kv.at[4], kv.at[4], b_send, b_recv.at[4], at(x, qq)).start()

    take(0)
    for level in (1, 2):
        from_holder(level)
        take(level)

    key_at = lax.broadcasted_iota(jnp.int32, (T, ROWS), 0)
    row_at = lax.rem(lax.broadcasted_iota(jnp.int32, (T, ROWS), 1), T)
    ahead = key_at - row_at

    def partial(first, last, kind):
        rows = slice(kind * ROWS, (kind + 1) * ROWS)
        slots = slice(first * T, last * T)
        scores = dot(k_rot[slots, :], q_rot[rows, :], ((1,), (1,))) * SCALE
        pieces = []
        for slot in range(first, last):
            piece = scores[(slot - first) * T : (slot - first + 1) * T]
            if kind == 0:
                if slot == 0:
                    seen = jnp.logical_and(ahead <= 0, key_at < leaf_len)
                    piece = jnp.where(seen, piece, NEG_BIG)
            elif slot == 0:
                piece = jnp.full_like(piece, NEG_BIG)
            else:
                bound = jnp.where(hosted == slot, 0, jnp.where(hosted < slot, T, -T))
                piece = jnp.where(ahead <= bound, piece, NEG_BIG)
            pieces.append(piece)
        scores = jnp.concatenate(pieces, axis=0)
        top = jnp.max(scores, axis=0, keepdims=True)
        raised = jnp.exp(scores - top)
        dprobs = dot(v_all[slots, :], g_rows[rows, :], ((1,), (1,)))
        products = raised * dprobs
        return (
            raised,
            products,
            top,
            jnp.sum(raised, axis=0, keepdims=True),
            jnp.sum(products, axis=0, keepdims=True),
        )

    def keep(first, last, at_row, kind, rows):
        raised, products, *sums = partial(first, last, kind)
        near_e[first * T : last * T, rows] = raised
        near_d[first * T : last * T, rows] = products
        for n, line in enumerate(sums):
            near_s[at_row + n : at_row + n + 1, rows] = line

    for kind in range(2):
        rows = slice(kind * ROWS, (kind + 1) * ROWS)
        keep(0, 3, 0, kind, rows)

    @pl.when(jnp.logical_and(c == 1, jnp.logical_not(among((1, 5, 9)))))
    def _():
        for level in (5, 6):
            remote(own, kv.at[level], b_send, b_recv.at[level], at(x, 1)).wait_recv()
            remote(kv.at[level], kv.at[level], b_send, b_recv.at[level], at(x, q - 1)).start()

    from_holder(3)
    take(3)
    from_holder(4)
    take(4)
    for kind in range(2):
        rows = slice(kind * ROWS, (kind + 1) * ROWS)
        keep(3, 5, 3, kind, rows)

    def from_relay(level):
        @pl.when(jnp.logical_or(c == 0, is_second))
        def _():
            remote(own, kv.at[level], b_send, b_recv.at[level], at(x, 1)).wait_recv()

    from_relay(5)
    take(5)
    from_relay(6)
    take(6)

    for kind in range(2):
        rows = slice(kind * ROWS, (kind + 1) * ROWS)
        last_e, last_d, *last = partial(GROUPS[-1][0], SLOTS, kind)
        sums = [[near_s[3 * n + line : 3 * n + line + 1, rows] for line in range(3)] for n in range(len(GROUPS) - 1)]
        sums.append(last)
        top = sums[0][0]
        for group in sums[1:]:
            top = jnp.maximum(top, group[0])
        factors = [jnp.exp(group[0] - top) for group in sums]
        total = sums[0][1] * factors[0]
        delta = sums[0][2] * factors[0]
        for group, factor in zip(sums[1:], factors[1:]):
            total = total + group[1] * factor
            delta = delta + group[2] * factor
        over = 1.0 / total
        delta = delta * over
        for n, (first, after) in enumerate(GROUPS):
            here = slice(first * T, after * T)
            e, d = (last_e, last_d) if n == len(GROUPS) - 1 else (near_e[here, rows], near_d[here, rows])
            factor = factors[n] * over
            dscores[here, rows] = (d * factor - e * (factor * delta)).astype(BF)
            near_s[n : n + 1, rows] = factor
        near_e[GROUPS[-1][0] * T :, rows] = last_e
    dk_all = dot(dscores[...], q_rot[...], ((1,), (0,))) * SCALE
    dq_turned = dot(k_rot[...], dscores[...], ((0,), (0,))) * SCALE
    lanes, crossed = None, None
    for n in range(2 * ROWS // D):
        tile = slice(n * D, (n + 1) * D)
        one, other = dq_turned[:, tile] * wq_cos[:, tile], dq_turned[:, tile] * wq_sin[:, tile]
        lanes = one if lanes is None else lanes + one
        crossed = other if crossed is None else crossed + other
    lanes = lanes - jnp.concatenate([crossed[D // 2 :], crossed[: D // 2]], axis=0)
    gain_q = jnp.sum(jnp.transpose(lanes), axis=0, keepdims=True)
    gain_k = jnp.sum(dk_all * wk_cos[...], axis=0, keepdims=True) - pltpu.roll(
        jnp.sum(dk_all * wk_sin[...], axis=0, keepdims=True), D // 2, axis=1
    )
    terms = jnp.concatenate([gain_q, gain_k], axis=0)
    gain_send[0] = terms

    @pl.when(direct)
    def _():
        for xx, qq, yy in FIRST:
            slot = gain_d.at[x * len(LAST_Y) + y - LAST_Y[0], q - EARLY_Q]
            remote(gain_send.at[0], slot, gd_send, gd_recv, at(xx, qq, yy)).start()

    @pl.when(jnp.logical_not(is_relay))
    def _():
        recv = gz_recv.at[jnp.where(q < EARLY_Q, 0, 1)]
        remote(gain_send.at[0], gain_z.at[lax.rem(q + NQ - 2, NQ)], gz_send, recv, at(x, 1)).start()

    for n, (first, after) in enumerate(GROUPS):
        here = slice(first * T, after * T)
        probs[here, :] = (near_e[here, :] * near_s[n : n + 1, :]).astype(BF)
    dv_all = dot(probs[...], g_rows[...], ((1,), (0,)))
    for slot in range(SLOTS):
        part[slot, 0] = dk_all[slot * T : (slot + 1) * T]
        part[slot, 1] = dv_all[slot * T : (slot + 1) * T]

    for slot in range(1, SLOTS):
        send_kv[slot - 1] = part[slot].astype(BF)

    @pl.when(sends_six)
    def _():
        n = jnp.where(z >= 4, x, NX + jnp.minimum(x, 2))
        remote(send_kv.at[5], x_recv.at[n], x_sem.at[0], xr_sem, at(2, low)).start()

    @pl.when(sends_five)
    def _():
        n = jnp.where(z >= 4, 1 + lax.rem(x, 2), 0)
        remote(send_kv.at[4], x_recv.at[n], x_sem.at[1], xr_sem, at(x // 2 * 2 + 1, low)).start()

    for level in range(1, 5):

        @pl.when(q != holder[level])
        def _(level=level):
            n = lax.rem(q, 2**level)
            n = jnp.where(n > 2 ** (level - 1), n - 1, n)
            remote(send_kv.at[level - 1], z_recv.at[n], r_send, r_recv, at(x, holder[level])).start()

    def wait_lines(count, sem):
        lines = gain_z.at[pl.ds(0, count)]
        pltpu.make_async_copy(lines, lines, sem).wait()

    @pl.when(is_relay)
    def _():
        wait_lines(EARLY_Q - 1, gz_recv.at[0])
        line = terms + gain_z[NQ - 2]
        for n in range(EARLY_Q - 2):
            line = line + gain_z[n]
        gain_send[2] = line

        @pl.when(starts_last)
        def _():
            for xx, qq, yy in FIRST:
                remote(gain_send.at[2], gain_p.at[plane], gp_send, gp_recv, at(xx, qq, yy)).start()

    y_q[...] = jnp.transpose(dq_turned)
    for kind in range(2):
        cosine, sine = spread(table[pl.ds(pl.multiple_of(place[kind], T), T), :])
        for head in range(G):
            rows = pl.ds(kind * ROWS + head * T, T)
            columns = slice(head * D, (head + 1) * D)
            raw = q_raw[kind, :, columns].astype(F32)
            unit, factor = unit_of(raw)
            scaled = unturn(y_q[rows, :], cosine, sine) * q_gain
            inner = jnp.mean(scaled * unit, axis=-1, keepdims=True)
            dq_out[kind, :, columns] = (factor * (scaled - unit * inner)).astype(BF)

    def key_gradient(raw, turned, start):
        cosine, sine = spread(table[pl.ds(start, T), :])
        unit, factor = unit_of(raw.astype(F32))
        scaled = unturn(turned, cosine, sine) * k_gain
        inner = jnp.mean(scaled * unit, axis=-1, keepdims=True)
        return (factor * (scaled - unit * inner)).astype(BF)

    dk_out[0] = key_gradient(kv[0, 0], part[0, 0], DEPTH * T)
    dv_out[0] = part[0, 1].astype(BF)

    @pl.when(is_relay)
    def _():
        line = gain_send[2]
        wait_lines(NQ - EARLY_Q, gz_recv.at[1])
        line = line + tree_sum([gain_z[n] for n in range(EARLY_Q - 2, NQ - 2)])
        gain_send[1] = line
        gain_p[plane] = line
        for dx, dy in AWAY:
            xx, yy = lax.rem(x + dx, NX), lax.rem(y + dy, NY)
            first = first_relay(xx, yy)

            @pl.when(jnp.logical_not(jnp.logical_and(first, starts_last)))
            def _(xx=xx, yy=yy):
                remote(gain_send.at[1], gain_p.at[plane], gp_send, gp_recv, at(xx, 1, yy)).start()

        @pl.when(jnp.logical_not(starts_last))
        def _():
            remote(gain_send.at[1], gain_p.at[plane], gp_send, gp_recv, at(0, 3, 0)).start()

    def gather(level, count):
        settle(count, xr_sem)
        total = part[level]
        for n in range(count):
            total = total + x_recv[n].astype(F32)
        part[level] = total
        send_sum[...] = total.astype(BF)

    @pl.when(jnp.logical_and(z < 4, x == 2))
    def _():
        gather(6, 2 * NX - 1)

    @pl.when(jnp.logical_and(z < 4, lax.rem(x, 2) == 1))
    def _():
        gather(5, 3)

    sums = jnp.logical_and(x > 0, jnp.logical_and(z < 4, q != 0))

    @pl.when(sums)
    def _():
        remote(send_sum, z_recv.at[q - 1], s_send, r_recv, at(x, 0)).start()

    for places, count in (((1,), 11), ((5,), 9), ((9,), 5), ((13,), 7), ((4,), 7), ((12,), 5)):

        @pl.when(among(places))
        def _(count=count):
            settle(count, b_send)

    @pl.when(among((3, 7, 11, 15)))
    def _():
        settle(3, b_send)

    for level, count in ((2, 3), (4, 9), (5, 4), (6, 2 * NX)):

        @pl.when(hosted == level)
        def _(count=count):
            settle(count, b_send)

    @pl.when(hosted <= DEPTH)
    def _():
        size = jnp.int32(NQ)
        for level, count in ((1, 2), (2, 4), (3, 8), (5, 8), (6, 8)):
            size = jnp.where(hosted == level, count, size)
        for level in range(1, DEPTH + 1):

            @pl.when(hosted == level)
            def _(level=level):
                settle(2**level - 1 if level < 5 else NQ // 2 - 1, r_recv)

        def add(n, total):
            return total + z_recv[n].astype(F32)

        total = lax.fori_loop(0, size - 1, add, part[hosted])
        dk_out[1] = key_gradient(own[0], total[0], pl.multiple_of(place[1], T))
        dv_out[1] = total[1].astype(BF)

    @pl.when(hosted > DEPTH)
    def _():
        dk_out[1] = jnp.zeros((T, D), BF)
        dv_out[1] = jnp.zeros((T, D), BF)

    last_lines = [xx * NY + yy for xx in range(NX) for yy in LAST_Y]

    def total_of_lines(senders, straight):
        lines = gain_p.at[pl.ds(0, senders)]
        pltpu.make_async_copy(lines, lines, gp_recv).wait()
        others = tree_sum([gain_p[n] for n in range(NX * NY) if n not in last_lines])
        if straight:
            pltpu.make_async_copy(gain_d, gain_d, gd_recv).wait()
        late = []
        for n, there in enumerate(last_lines):
            line = gain_p[there]
            if straight:
                line = line + tree_sum([gain_d[n, k] for k in range(NQ - EARLY_Q)])
            late.append(line)
        gain_total[...] = others + tree_sum(late)

    def pass_on(when, targets):
        @pl.when(when)
        def _():
            for qq in targets:
                remote(gain_total, gain_total, gt_send, gt_recv, at(x, qq)).start()

    @pl.when(jnp.logical_and(is_relay, is_first))
    def _():
        total_of_lines(NX * NY - 1, True)

    @pl.when(jnp.logical_and(is_relay, jnp.logical_not(is_first)))
    def _():
        total_of_lines(NX * NY - 1, False)

    @pl.when(is_extra)
    def _():
        total_of_lines(NX * NY, True)

    pass_on(jnp.logical_and(is_relay, plane > 0), (3, 5, 7, 0))
    pass_on(is_extra, (5, 7, 2, 0))

    @pl.when(is_relay)
    def _():
        pltpu.make_async_copy(gain_p, gain_p, gp_send).wait()

    @pl.when(sends_six)
    def _():
        settle(1, x_sem.at[0])

    @pl.when(sends_five)
    def _():
        settle(1, x_sem.at[1])

    @pl.when(hosted < 5)
    def _():
        settle(3, r_send)

    @pl.when(hosted >= 5)
    def _():
        settle(4, r_send)

    @pl.when(sums)
    def _():
        settle(1, s_send)

    @pl.when(jnp.logical_not(is_relay))
    def _():
        pltpu.make_async_copy(gain_total, gain_total, gz_send).wait()

        @pl.when(direct)
        def _():
            sent = gain_z.at[pl.ds(0, len(FIRST))]
            pltpu.make_async_copy(sent, sent, gd_send).wait()


        @pl.when(jnp.logical_not(is_extra))
        def _():
            pltpu.make_async_copy(gain_total, gain_total, gt_recv).wait()

    pass_one = jnp.logical_and(among((3, 7, 9, 11, 13, 15)), jnp.logical_not(is_extra))
    pass_on(q == 5, (9, 11, 13, 15, 4))
    pass_on(pass_one, (q - 1,))
    dqg_out[...] = gain_total[0:1]
    dkg_out[...] = gain_total[1:2]

    def passed(when, count):
        @pl.when(when)
        def _():
            sent = gain_z.at[pl.ds(0, count)]
            pltpu.make_async_copy(sent, sent, gt_send).wait()

    passed(jnp.logical_or(is_extra, jnp.logical_and(is_relay, plane > 0)), 4)
    passed(q == 5, 5)
    passed(pass_one, 1)


def hand_over(*refs):
    copies = [pltpu.make_async_copy(refs[n], refs[5 + n], refs[10].at[n]) for n in range(5)]
    for copy in copies:
        copy.start()
    for copy in copies:
        copy.wait()


def on_device(queries, keys, values, output_gradient, q_gain, k_gain, leaf_len):
    dma = pltpu.SemaphoreType.DMA
    anywhere = pl.BlockSpec(memory_space=pl.ANY)
    in_hbm = pl.BlockSpec(memory_space=pltpu.HBM)
    results = pl.pallas_call(
        kernel,
        name="tree_backward",
        out_shape=[
            pltpu.VMEM(queries.shape, BF),
            pltpu.VMEM(keys.shape, BF),
            pltpu.VMEM(values.shape, BF),
            pltpu.VMEM((1, D), F32),
            pltpu.VMEM((1, D), F32),
        ],
        in_specs=[anywhere] * 7 + [pl.BlockSpec(memory_space=pltpu.SMEM)],
        out_specs=[pl.BlockSpec(memory_space=pltpu.VMEM)] * 5,
        scratch_shapes=[
            pltpu.VMEM((2, T, G * D), BF),
            pltpu.VMEM((2, T, G * D), BF),
            pltpu.VMEM((2, T, D), BF),
            pltpu.VMEM((SLOTS, 2, T, D), BF),
            pltpu.VMEM((1, D), F32),
            pltpu.VMEM((1, D), F32),
            pltpu.VMEM((KEYS, D), F32),
            pltpu.VMEM((2 * ROWS, D), BF),
            pltpu.VMEM((2 * ROWS, D), BF),
            pltpu.VMEM((KEYS, D), BF),
            pltpu.VMEM((KEYS, D), BF),
            pltpu.VMEM((D, 2 * ROWS), F32),
            pltpu.VMEM((D, 2 * ROWS), F32),
            pltpu.VMEM((KEYS, D), F32),
            pltpu.VMEM((KEYS, D), F32),
            pltpu.VMEM((KEYS, 2 * ROWS), F32),
            pltpu.VMEM(((SLOTS - 1) * T, 2 * ROWS), F32),
            pltpu.VMEM((16, 2 * ROWS), F32),
            pltpu.VMEM((KEYS, 2 * ROWS), BF),
            pltpu.VMEM((KEYS, 2 * ROWS), BF),
            pltpu.VMEM((SLOTS, 2, T, D), F32),
            pltpu.VMEM((2 * ROWS, D), F32),
            pltpu.VMEM((NQ, 2, T, D), BF),
            pltpu.VMEM((DEPTH, 2, T, D), BF),
            pltpu.VMEM((2, T, D), BF),
            pltpu.VMEM((2 * NX - 1, 2, T, D), BF),
            pltpu.VMEM((NQ, 2, T, D), BF),
            pltpu.VMEM((3, 2, D), F32),
            pltpu.VMEM((NQ, 2, D), F32),
            pltpu.VMEM((NX * NY, 2, D), F32),
            pltpu.VMEM((NX * len(LAST_Y), NQ - EARLY_Q, 2, D), F32),
            pltpu.VMEM((2, D), F32),
            dma((8,)),
            dma(()),
            dma((SLOTS,)),
            dma(()),
            dma(()),
            dma((2,)),
            dma(()),
            dma(()),
            dma(()),
            dma((2,)),
            dma(()),
            dma(()),
            dma(()),
            dma(()),
            dma(()),
            dma(()),
        ],
        compiler_params=pltpu.CompilerParams(
            collective_id=0, has_side_effects=True, vmem_limit_bytes=40 * 2**20
        ),
        cost_estimate=pl.CostEstimate(flops=10 * 2 * ROWS * KEYS * D, bytes_accessed=2**20, transcendentals=2 * ROWS * KEYS),
    )(
        *(
            pltpu.with_memory_space_constraint(array, pltpu.HBM)
            for array in (
                queries,
                keys,
                values,
                output_gradient,
                q_gain.reshape(1, D),
                k_gain.reshape(1, D),
                jnp.asarray(rope_table()),
            )
        ),
        leaf_len,
    )
    dq, dk, dv, dq_gain, dk_gain = pl.pallas_call(
        hand_over,
        name="hand_over",
        out_shape=[jax.ShapeDtypeStruct(r.shape, r.dtype) for r in results],
        in_specs=[anywhere] * 5,
        out_specs=[in_hbm] * 5,
        scratch_shapes=[dma((5,))],
        compiler_params=pltpu.CompilerParams(vmem_limit_bytes=8 * 2**20),
    )(*(pltpu.with_memory_space_constraint(r, pltpu.VMEM) for r in results))
    return dq, dk, dv, dq_gain.reshape(D), dk_gain.reshape(D)


def solution(mesh):
    shape = dict(mesh.shape)
    if shape != {"leaf": NX * NZ * NC, "head": NY}:
        raise ValueError("another mesh")
    split = P(None, "leaf", "head")
    return jax.shard_map(
        on_device,
        mesh=mesh,
        in_specs=(split, split, split, split, P(), P(), P("leaf")),
        out_specs=(split, split, split, P(), P()),
        check_vma=False,
    )
```

```python
import jax
import jax.numpy as jnp
import numpy as np
from jax import lax
from jax.experimental import pallas as pl
from jax.experimental.pallas import tpu as pltpu
from jax.sharding import PartitionSpec as P

NEG_BIG = -1000000000.0
NORM_EPS = 1e-06
ROPE_BASE = 1000000.0
DEPTH = 6
T = 64
D = 128
G = 8
SLOTS = DEPTH + 1
KEYS = SLOTS * T
GROUPS = ((0, 3), (3, 5), (5, 7))

ROWS = G * T
NX, NZ, NC, NY = 4, 8, 2, 8
NQ = NZ * NC
SCALE = D ** (-0.5)
BF = jnp.bfloat16
F32 = jnp.float32
MESH = pl.DeviceIdType.MESH
FIRST = ((0, 1, 0), (0, 3, 0), (0, 1, 1), (1, 1, 0), (0, 1, 2), (1, 1, 1), (2, 1, 0), (3, 1, 0))
LAST_Y = (3,4,5,6)
EARLY_Q = 4
SERVED = ((1, (11, 13, 15, 3)), (5, (8, 9, 7)))
AWAY = sorted(
    ((dx, dy) for dx in range(NX) for dy in range(NY) if dx or dy),
    key=lambda step: -min(step[0], NX - step[0]) - min(step[1], NY - step[1]),
)


def rope_table():
    frequency = (ROPE_BASE ** (-(np.arange(D // 2, dtype=np.float32) * 2.0 / D))).astype(np.float32)
    angles = np.arange(KEYS, dtype=np.float32)[:, None] * frequency
    return np.concatenate([np.cos(angles), np.sin(angles)], axis=1).astype(np.float32)


def spread(table):
    lane = lax.broadcasted_iota(jnp.int32, table.shape, 1)
    other = pltpu.roll(table, D // 2, axis=1)
    low = lane < D // 2
    return jnp.where(low, table, other), jnp.where(low, -other, table)


def turn(x, cosine, sine):
    return x * cosine + pltpu.roll(x, D // 2, axis=1) * sine


def unturn(x, cosine, sine):
    return x * cosine - pltpu.roll(x, D // 2, axis=1) * sine


def unit_of(x):
    factor = lax.rsqrt(jnp.mean(x * x, axis=-1, keepdims=True) + NORM_EPS)
    return x * factor, factor


def tree_sum(terms):
    while len(terms) > 1:
        terms = [sum(terms[n + 1 : n + 2], terms[n]) for n in range(0, len(terms), 2)]
    return terms[0]


def dot(a, b, contract):
    return lax.dot_general(a, b, (contract, ((), ())), preferred_element_type=F32)


def kernel(
    q_in, k_in, v_in, g_in, qg_in, kg_in, table_in, length,
    dq_out, dk_out, dv_out, dqg_out, dkg_out,
    q_raw, g_raw, own, kv, qg, kg, table,
    q_rot, g_rows, k_rot, v_all, wq_cos, wq_sin, wk_cos, wk_sin, near_e, near_d, near_s, probs, dscores, part, y_q, ballast,
    send_kv, send_sum, x_recv, z_recv, gain_send, gain_z, gain_p, gain_d, gain_total,
    load_sem, b_send, b_recv, r_send, r_recv, x_sem, xr_sem, s_send,
    gz_send, gz_recv, gp_send, gp_recv, gd_send, gd_recv, gt_send, gt_recv,
):
    leaf = lax.axis_index("leaf")
    y = lax.axis_index("head")
    x = leaf // NQ
    q = lax.rem(leaf, NQ)
    z = q // NC
    c = lax.rem(q, NC)

    def at(xx, qq, yy=None):
        return (xx * NQ + qq, y if yy is None else yy)

    hosted = jnp.int32(1)
    for level in range(1, DEPTH + 1):
        hosted = hosted + jnp.where(lax.rem(leaf, 2**level) == 0, 1, 0)

    def remote(src, dst, send, recv, device):
        return pltpu.make_async_remote_copy(
            src_ref=src, dst_ref=dst, send_sem=send, recv_sem=recv, device_id=device, device_id_type=MESH
        )

    def settle(count, sem):
        blocks = ballast.at[pl.ds(0, count)]
        pltpu.make_async_copy(blocks, blocks, sem).wait()

    holder = {level: q // 2**level * 2**level + 2 ** (level - 1) for level in range(1, 5)}
    is_relay = q == 1
    is_near = q == 5
    is_extra = jnp.logical_and(leaf == 3, y == 0)

    def first_relay(xx, yy):
        near_zero = jnp.logical_and(yy > 0, xx + yy < 3)
        return jnp.logical_or(yy == 0, near_zero)

    is_first = jnp.logical_or(is_extra, jnp.logical_and(is_relay, first_relay(x, y)))
    is_second = q == 9
    far_owner = jnp.logical_and(q == 0, x > 0)
    plane = x * NY + y
    starts_last = jnp.logical_and(y >= LAST_Y[0], y <= LAST_Y[-1])
    direct = jnp.logical_and(starts_last, q >= EARLY_Q)
    mirror = (NZ - 1 - z) * NC + c
    low = jnp.where(z < 4, q, mirror)
    sends_six = jnp.logical_or(z >= 4, x != 2)
    sends_five = jnp.logical_or(z >= 4, lax.rem(x, 2) == 0)

    def among(places):
        here = q == places[0]
        for place in places[1:]:
            here = jnp.logical_or(here, q == place)
        return here

    barrier = pltpu.get_barrier_semaphore()

    def greet(device):
        pl.semaphore_signal(barrier, inc=1, device_id=device, device_id_type=MESH)

    @pl.when(jnp.logical_or(is_relay, is_near))
    def _():
        greet(at(2, 0))
        greet(at(x // 2 * 2 + 1, 0))

    for relay, served in SERVED:

        @pl.when(among(served))
        def _(relay=relay):
            greet(at(x, relay))

    @pl.when(among((10, 11, 12, 13)))
    def _():
        greet(at(x, 9))

    @pl.when(z == NZ - 1)
    def _():
        greet(at(x, 13))

    @pl.when(jnp.logical_or(z < 4, is_second))
    def _():
        greet(at(x, 8))

    for level in (3, 2, 1):

        @pl.when(jnp.logical_and(q != holder[level], jnp.logical_not(jnp.logical_and(z == NZ - 1, level == 3))))
        def _(level=level):
            greet(at(x, holder[level]))

    @pl.when(jnp.logical_and(z < 4, x == 2))
    def _():
        for xx in range(NX):
            greet(at(xx, mirror))
        for xx in (0, 1, 3):
            greet(at(xx, q))

    @pl.when(jnp.logical_and(z < 4, lax.rem(x, 2) == 1))
    def _():
        greet(at(x, mirror))
        greet(at(x - 1, mirror))
        greet(at(x - 1, q))

    early = jnp.where(c == 1, 1, 0)
    early = early + jnp.where(sends_six, 1, 0) + jnp.where(sends_five, 1, 0)
    early = early + jnp.where(is_relay, 4 + NX * NY, 0) + jnp.where(is_near, 3 + jnp.where(starts_last, len(FIRST), 0), 0)
    early = early + jnp.where(is_second, 4, 0) + jnp.where(q == 13, 2, 0) - jnp.where(q == 12, 2, 0)
    for level, count in ((2, 3), (3, 7), (4, 9), (5, 4), (6, 2 * NX)):
        early = early + jnp.where(hosted == level, count, 0)

    loads = [
        pltpu.make_async_copy(k_in.at[1], own.at[0], load_sem.at[0]),
        pltpu.make_async_copy(v_in.at[1], own.at[1], load_sem.at[0]),
        pltpu.make_async_copy(k_in.at[0], kv.at[0, 0], load_sem.at[1]),
        pltpu.make_async_copy(v_in.at[0], kv.at[0, 1], load_sem.at[1]),
        pltpu.make_async_copy(table_in, table, load_sem.at[2]),
        pltpu.make_async_copy(qg_in, qg, load_sem.at[3]),
        pltpu.make_async_copy(kg_in, kg, load_sem.at[4]),
        pltpu.make_async_copy(q_in, q_raw, load_sem.at[5]),
        pltpu.make_async_copy(g_in, g_raw, load_sem.at[6]),
    ]
    for load in loads:
        load.start()

    @pl.when(is_relay)
    def _():
        def greet_plane(n, carry):
            there = lax.rem(plane + n, NX * NY)
            greet(at(there // NY, 1, lax.rem(there, NY)))
            return carry

        lax.fori_loop(1, NX * NY, greet_plane, 0)

    @pl.when(is_extra)
    def _():
        def greet_all(n, carry):
            greet(at(n // NY, 1, lax.rem(n, NY)))
            return carry

        lax.fori_loop(0, NX * NY, greet_all, 0)

    @pl.when(is_first)
    def _():
        for xx in range(NX):
            for yy in LAST_Y:
                greet(at(xx, 5, yy))

    settle(1, load_sem.at[0])

    pl.semaphore_wait(barrier, early)

    @pl.when(jnp.logical_and(far_owner, x == 2))
    def _():
        for relay in (5, 1):
            for xx in range(NX):
                remote(own, kv.at[6], b_send, b_recv.at[6], at(xx, relay)).start()

    @pl.when(jnp.logical_and(far_owner, x != 2))
    def _():
        for relay in (5, 1):
            for n in range(2):
                remote(own, kv.at[5], b_send, b_recv.at[5], at(x - n, relay)).start()

    for level in (4, 3, 2, 1):

        @pl.when(hosted == level)
        def _(level=level):
            half = 2 ** (level - 1)
            offsets = sorted((o for o in range(-half, half) if o), key=lambda o: -abs(o))
            if level == 4:
                offsets = [1] + [o for o in offsets if o < 0]
            for offset in offsets:
                if level == 3 and offset in (2, 3):

                    @pl.when(q != 12)
                    def _(offset=offset):
                        remote(own, kv.at[level], b_send, b_recv.at[level], at(x, q + offset)).start()

                else:
                    remote(own, kv.at[level], b_send, b_recv.at[level], at(x, q + offset)).start()
            for n in range(2):
                pltpu.make_async_copy((k_in, v_in)[n].at[1], kv.at[level, n], load_sem.at[7]).start()

    @pl.when(is_second)
    def _():
        remote(own, kv.at[4], b_send, b_recv.at[4], at(x, 8)).wait_recv()
        for qq in (13, 12, 10, 11):
            remote(kv.at[4], kv.at[4], b_send, b_recv.at[4], at(x, qq)).start()

    for relay, served in SERVED:

        @pl.when(q == relay)
        def _(relay=relay, served=served):
            for level in (5, 6):
                remote(own, kv.at[level], b_send, b_recv.at[level], at(x, 0)).wait_recv()
            for qq in (*served, relay - 1):
                for level in (5, 6):
                    remote(kv.at[level], kv.at[level], b_send, b_recv.at[level], at(x, qq)).start()

    @pl.when(q == 13)
    def _():
        remote(own, kv.at[3], b_send, b_recv.at[3], at(x, 12)).wait_recv()
        for qq in (14, 15):
            remote(kv.at[3], kv.at[3], b_send, b_recv.at[3], at(x, qq)).start()

    for load in loads[4:]:
        load.wait()
    q_gain, k_gain = qg[...], kg[...]
    leaf_len = length[0]
    place = [DEPTH * T, jnp.maximum(DEPTH - hosted, 0) * T]
    live = [
        lax.broadcasted_iota(jnp.int32, (T, D), 0) < leaf_len,
        jnp.broadcast_to(hosted <= DEPTH, (T, D)),
    ]
    for kind in range(2):
        cosine, sine = spread(table[pl.ds(pl.multiple_of(place[kind], T), T), :])
        w_cos, w_sin = [], []
        for head in range(G):
            rows = pl.ds(kind * ROWS + head * T, T)
            unit, _ = unit_of(q_raw[kind, :, head * D : (head + 1) * D].astype(F32))
            q_rot[rows, :] = turn(unit * q_gain, cosine, sine).astype(BF)
            w_cos.append(unit * cosine)
            w_sin.append(pltpu.roll(unit * sine, D // 2, axis=1))
            if head % 2:
                pair = slice(kind * ROWS + (head - 1) * T, kind * ROWS + (head + 1) * T)
                wq_cos[:, pair] = jnp.transpose(jnp.concatenate(w_cos[-2:], axis=0))
                wq_sin[:, pair] = jnp.transpose(jnp.concatenate(w_sin[-2:], axis=0))
            grad = g_raw[kind, :, head * D : (head + 1) * D]
            g_rows[rows, :] = jnp.where(live[kind], grad, jnp.zeros((), BF))

    settle(1, load_sem.at[1])

    def take(slot):
        rows = pl.ds(slot * T, T)
        cosine, sine = spread(table[(DEPTH - slot) * T : (DEPTH - slot + 1) * T, :])
        unit, _ = unit_of(kv[slot, 0].astype(F32))
        wk_cos[rows, :] = unit * cosine
        wk_sin[rows, :] = pltpu.roll(unit * sine, D // 2, axis=1)
        k_rot[rows, :] = turn(unit * k_gain, cosine, sine).astype(BF)
        v_all[rows, :] = kv[slot, 1]

    def from_holder(level):
        passed_on = {3: q == 13, 4: among((9, 13))}.get(level, False)

        @pl.when(jnp.logical_and(q != holder[level], jnp.logical_not(passed_on)))
        def _():
            remote(own, kv.at[level], b_send, b_recv.at[level], at(x, holder[level])).wait_recv()

        @pl.when(hosted == level)
        def _():
            settle(1, load_sem.at[7])

    @pl.when(q == 13)
    def _():
        remote(own, kv.at[4], b_send, b_recv.at[4], at(x, 9)).wait_recv()
        for qq in (14, 15):
            remote(kv.at[4], kv.at[4], b_send, b_recv.at[4], at(x, qq)).start()

    take(0)
    for level in (1, 2):
        from_holder(level)
        take(level)

    key_at = lax.broadcasted_iota(jnp.int32, (T, ROWS), 0)
    row_at = lax.rem(lax.broadcasted_iota(jnp.int32, (T, ROWS), 1), T)
    ahead = key_at - row_at

    def partial(first, last, kind):
        rows = slice(kind * ROWS, (kind + 1) * ROWS)
        slots = slice(first * T, last * T)
        scores = dot(k_rot[slots, :], q_rot[rows, :], ((1,), (1,))) * SCALE
        pieces = []
        for slot in range(first, last):
            piece = scores[(slot - first) * T : (slot - first + 1) * T]
            if kind == 0:
                if slot == 0:
                    seen = jnp.logical_and(ahead <= 0, key_at < leaf_len)
                    piece = jnp.where(seen, piece, NEG_BIG)
            elif slot == 0:
                piece = jnp.full_like(piece, NEG_BIG)
            else:
                bound = jnp.where(hosted == slot, 0, jnp.where(hosted < slot, T, -T))
                piece = jnp.where(ahead <= bound, piece, NEG_BIG)
            pieces.append(piece)
        scores = jnp.concatenate(pieces, axis=0)
        top = jnp.max(scores, axis=0, keepdims=True)
        raised = jnp.exp(scores - top)
        dprobs = dot(v_all[slots, :], g_rows[rows, :], ((1,), (1,)))
        products = raised * dprobs
        return (
            raised,
            products,
            top,
            jnp.sum(raised, axis=0, keepdims=True),
            jnp.sum(products, axis=0, keepdims=True),
        )

    def keep(first, last, at_row, kind, rows):
        raised, products, *sums = partial(first, last, kind)
        near_e[first * T : last * T, rows] = raised
        near_d[first * T : last * T, rows] = products
        for n, line in enumerate(sums):
            near_s[at_row + n : at_row + n + 1, rows] = line

    for kind in range(2):
        rows = slice(kind * ROWS, (kind + 1) * ROWS)
        keep(0, 3, 0, kind, rows)

    @pl.when(jnp.logical_and(c == 1, jnp.logical_not(among((1, 5, 9)))))
    def _():
        for level in (5, 6):
            remote(own, kv.at[level], b_send, b_recv.at[level], at(x, 1)).wait_recv()
            remote(kv.at[level], kv.at[level], b_send, b_recv.at[level], at(x, q - 1)).start()

    from_holder(3)
    take(3)
    from_holder(4)
    take(4)
    for kind in range(2):
        rows = slice(kind * ROWS, (kind + 1) * ROWS)
        keep(3, 5, 3, kind, rows)

    def from_relay(level):
        @pl.when(jnp.logical_or(c == 0, is_second))
        def _():
            remote(own, kv.at[level], b_send, b_recv.at[level], at(x, 1)).wait_recv()

    from_relay(5)
    take(5)
    from_relay(6)
    take(6)

    for kind in range(2):
        rows = slice(kind * ROWS, (kind + 1) * ROWS)
        last_e, last_d, *last = partial(GROUPS[-1][0], SLOTS, kind)
        sums = [[near_s[3 * n + line : 3 * n + line + 1, rows] for line in range(3)] for n in range(len(GROUPS) - 1)]
        sums.append(last)
        top = sums[0][0]
        for group in sums[1:]:
            top = jnp.maximum(top, group[0])
        factors = [jnp.exp(group[0] - top) for group in sums]
        total = sums[0][1] * factors[0]
        delta = sums[0][2] * factors[0]
        for group, factor in zip(sums[1:], factors[1:]):
            total = total + group[1] * factor
            delta = delta + group[2] * factor
        over = 1.0 / total
        delta = delta * over
        for n, (first, after) in enumerate(GROUPS):
            here = slice(first * T, after * T)
            e, d = (last_e, last_d) if n == len(GROUPS) - 1 else (near_e[here, rows], near_d[here, rows])
            factor = factors[n] * over
            dscores[here, rows] = (d * factor - e * (factor * delta)).astype(BF)
            near_s[n : n + 1, rows] = factor
        near_e[GROUPS[-1][0] * T :, rows] = last_e
    dk_all = dot(dscores[...], q_rot[...], ((1,), (0,))) * SCALE
    dq_turned = dot(k_rot[...], dscores[...], ((0,), (0,))) * SCALE
    lanes, crossed = None, None
    for n in range(2 * ROWS // D):
        tile = slice(n * D, (n + 1) * D)
        one, other = dq_turned[:, tile] * wq_cos[:, tile], dq_turned[:, tile] * wq_sin[:, tile]
        lanes = one if lanes is None else lanes + one
        crossed = other if crossed is None else crossed + other
    lanes = lanes - jnp.concatenate([crossed[D // 2 :], crossed[: D // 2]], axis=0)
    gain_q = jnp.sum(jnp.transpose(lanes), axis=0, keepdims=True)
    gain_k = jnp.sum(dk_all * wk_cos[...], axis=0, keepdims=True) - pltpu.roll(
        jnp.sum(dk_all * wk_sin[...], axis=0, keepdims=True), D // 2, axis=1
    )
    terms = jnp.concatenate([gain_q, gain_k], axis=0)
    gain_send[0] = terms

    @pl.when(direct)
    def _():
        for xx, qq, yy in FIRST:
            slot = gain_d.at[x * len(LAST_Y) + y - LAST_Y[0], q - EARLY_Q]
            remote(gain_send.at[0], slot, gd_send, gd_recv, at(xx, qq, yy)).start()

    @pl.when(jnp.logical_not(is_relay))
    def _():
        recv = gz_recv.at[jnp.where(q < EARLY_Q, 0, 1)]
        remote(gain_send.at[0], gain_z.at[lax.rem(q + NQ - 2, NQ)], gz_send, recv, at(x, 1)).start()

    for n, (first, after) in enumerate(GROUPS):
        here = slice(first * T, after * T)
        probs[here, :] = (near_e[here, :] * near_s[n : n + 1, :]).astype(BF)
    dv_all = dot(probs[...], g_rows[...], ((1,), (0,)))
    for slot in range(SLOTS):
        part[slot, 0] = dk_all[slot * T : (slot + 1) * T]
        part[slot, 1] = dv_all[slot * T : (slot + 1) * T]

    for slot in range(1, SLOTS):
        send_kv[slot - 1] = part[slot].astype(BF)

    @pl.when(sends_six)
    def _():
        n = jnp.where(z >= 4, x, NX + jnp.minimum(x, 2))
        remote(send_kv.at[5], x_recv.at[n], x_sem.at[0], xr_sem, at(2, low)).start()

    @pl.when(sends_five)
    def _():
        n = jnp.where(z >= 4, 1 + lax.rem(x, 2), 0)
        remote(send_kv.at[4], x_recv.at[n], x_sem.at[1], xr_sem, at(x // 2 * 2 + 1, low)).start()

    for level in range(1, 5):

        @pl.when(q != holder[level])
        def _(level=level):
            n = lax.rem(q, 2**level)
            n = jnp.where(n > 2 ** (level - 1), n - 1, n)
            remote(send_kv.at[level - 1], z_recv.at[n], r_send, r_recv, at(x, holder[level])).start()

    def wait_lines(count, sem):
        lines = gain_z.at[pl.ds(0, count)]
        pltpu.make_async_copy(lines, lines, sem).wait()

    @pl.when(is_relay)
    def _():
        wait_lines(EARLY_Q - 1, gz_recv.at[0])
        line = terms + gain_z[NQ - 2]
        for n in range(EARLY_Q - 2):
            line = line + gain_z[n]
        gain_send[2] = line

        @pl.when(starts_last)
        def _():
            for xx, qq, yy in FIRST:
                remote(gain_send.at[2], gain_p.at[plane], gp_send, gp_recv, at(xx, qq, yy)).start()

    y_q[...] = jnp.transpose(dq_turned)
    for kind in range(2):
        cosine, sine = spread(table[pl.ds(pl.multiple_of(place[kind], T), T), :])
        for head in range(G):
            rows = pl.ds(kind * ROWS + head * T, T)
            columns = slice(head * D, (head + 1) * D)
            raw = q_raw[kind, :, columns].astype(F32)
            unit, factor = unit_of(raw)
            scaled = unturn(y_q[rows, :], cosine, sine) * q_gain
            inner = jnp.mean(scaled * unit, axis=-1, keepdims=True)
            dq_out[kind, :, columns] = (factor * (scaled - unit * inner)).astype(BF)

    def key_gradient(raw, turned, start):
        cosine, sine = spread(table[pl.ds(start, T), :])
        unit, factor = unit_of(raw.astype(F32))
        scaled = unturn(turned, cosine, sine) * k_gain
        inner = jnp.mean(scaled * unit, axis=-1, keepdims=True)
        return (factor * (scaled - unit * inner)).astype(BF)

    dk_out[0] = key_gradient(kv[0, 0], part[0, 0], DEPTH * T)
    dv_out[0] = part[0, 1].astype(BF)

    @pl.when(is_relay)
    def _():
        line = gain_send[2]
        wait_lines(NQ - EARLY_Q, gz_recv.at[1])
        line = line + tree_sum([gain_z[n] for n in range(EARLY_Q - 2, NQ - 2)])
        gain_send[1] = line
        gain_p[plane] = line
        for dx, dy in AWAY:
            xx, yy = lax.rem(x + dx, NX), lax.rem(y + dy, NY)
            first = first_relay(xx, yy)

            @pl.when(jnp.logical_not(jnp.logical_and(first, starts_last)))
            def _(xx=xx, yy=yy):
                remote(gain_send.at[1], gain_p.at[plane], gp_send, gp_recv, at(xx, 1, yy)).start()

        @pl.when(jnp.logical_not(starts_last))
        def _():
            remote(gain_send.at[1], gain_p.at[plane], gp_send, gp_recv, at(0, 3, 0)).start()

    def gather(level, count):
        settle(count, xr_sem)
        total = part[level]
        for n in range(count):
            total = total + x_recv[n].astype(F32)
        part[level] = total
        send_sum[...] = total.astype(BF)

    @pl.when(jnp.logical_and(z < 4, x == 2))
    def _():
        gather(6, 2 * NX - 1)

    @pl.when(jnp.logical_and(z < 4, lax.rem(x, 2) == 1))
    def _():
        gather(5, 3)

    sums = jnp.logical_and(x > 0, jnp.logical_and(z < 4, q != 0))

    @pl.when(sums)
    def _():
        remote(send_sum, z_recv.at[q - 1], s_send, r_recv, at(x, 0)).start()

    for places, count in (((1,), 11), ((5,), 9), ((9,), 5), ((13,), 7), ((4,), 7), ((12,), 5)):

        @pl.when(among(places))
        def _(count=count):
            settle(count, b_send)

    @pl.when(among((3, 7, 11, 15)))
    def _():
        settle(3, b_send)

    for level, count in ((2, 3), (4, 9), (5, 4), (6, 2 * NX)):

        @pl.when(hosted == level)
        def _(count=count):
            settle(count, b_send)

    @pl.when(hosted <= DEPTH)
    def _():
        size = jnp.int32(NQ)
        for level, count in ((1, 2), (2, 4), (3, 8), (5, 8), (6, 8)):
            size = jnp.where(hosted == level, count, size)
        for level in range(1, DEPTH + 1):

            @pl.when(hosted == level)
            def _(level=level):
                settle(2**level - 1 if level < 5 else NQ // 2 - 1, r_recv)

        def add(n, total):
            return total + z_recv[n].astype(F32)

        total = lax.fori_loop(0, size - 1, add, part[hosted])
        dk_out[1] = key_gradient(own[0], total[0], pl.multiple_of(place[1], T))
        dv_out[1] = total[1].astype(BF)

    @pl.when(hosted > DEPTH)
    def _():
        dk_out[1] = jnp.zeros((T, D), BF)
        dv_out[1] = jnp.zeros((T, D), BF)

    last_lines = [xx * NY + yy for xx in range(NX) for yy in LAST_Y]

    def total_of_lines(senders, straight):
        lines = gain_p.at[pl.ds(0, senders)]
        pltpu.make_async_copy(lines, lines, gp_recv).wait()
        others = tree_sum([gain_p[n] for n in range(NX * NY) if n not in last_lines])
        if straight:
            pltpu.make_async_copy(gain_d, gain_d, gd_recv).wait()
        late = []
        for n, there in enumerate(last_lines):
            line = gain_p[there]
            if straight:
                line = line + tree_sum([gain_d[n, k] for k in range(NQ - EARLY_Q)])
            late.append(line)
        gain_total[...] = others + tree_sum(late)

    def pass_on(when, targets):
        @pl.when(when)
        def _():
            for qq in targets:
                remote(gain_total, gain_total, gt_send, gt_recv, at(x, qq)).start()

    @pl.when(jnp.logical_and(is_relay, is_first))
    def _():
        total_of_lines(NX * NY - 1, True)

    @pl.when(jnp.logical_and(is_relay, jnp.logical_not(is_first)))
    def _():
        total_of_lines(NX * NY - 1, False)

    @pl.when(is_extra)
    def _():
        total_of_lines(NX * NY, True)

    pass_on(jnp.logical_and(is_relay, plane > 0), (3, 5, 7, 0))
    pass_on(is_extra, (5, 7, 2, 0))

    @pl.when(is_relay)
    def _():
        pltpu.make_async_copy(gain_p, gain_p, gp_send).wait()

    @pl.when(sends_six)
    def _():
        settle(1, x_sem.at[0])

    @pl.when(sends_five)
    def _():
        settle(1, x_sem.at[1])

    @pl.when(hosted < 5)
    def _():
        settle(3, r_send)

    @pl.when(hosted >= 5)
    def _():
        settle(4, r_send)

    @pl.when(sums)
    def _():
        settle(1, s_send)

    @pl.when(jnp.logical_not(is_relay))
    def _():
        pltpu.make_async_copy(gain_total, gain_total, gz_send).wait()

        @pl.when(direct)
        def _():
            sent = gain_z.at[pl.ds(0, len(FIRST))]
            pltpu.make_async_copy(sent, sent, gd_send).wait()


        @pl.when(jnp.logical_not(is_extra))
        def _():
            pltpu.make_async_copy(gain_total, gain_total, gt_recv).wait()

    pass_one = jnp.logical_and(among((3, 7, 9, 11, 13, 15)), jnp.logical_not(is_extra))
    pass_on(q == 5, (9, 11, 13, 15, 4))
    pass_on(pass_one, (q - 1,))
    dqg_out[...] = gain_total[0:1]
    dkg_out[...] = gain_total[1:2]

    def passed(when, count):
        @pl.when(when)
        def _():
            sent = gain_z.at[pl.ds(0, count)]
            pltpu.make_async_copy(sent, sent, gt_send).wait()

    passed(jnp.logical_or(is_extra, jnp.logical_and(is_relay, plane > 0)), 4)
    passed(q == 5, 5)
    passed(pass_one, 1)


def hand_over(*refs):
    copies = [pltpu.make_async_copy(refs[n], refs[5 + n], refs[10].at[n]) for n in range(5)]
    for copy in copies:
        copy.start()
    for copy in copies:
        copy.wait()


def on_device(queries, keys, values, output_gradient, q_gain, k_gain, leaf_len):
    dma = pltpu.SemaphoreType.DMA
    anywhere = pl.BlockSpec(memory_space=pl.ANY)
    in_hbm = pl.BlockSpec(memory_space=pltpu.HBM)
    results = pl.pallas_call(
        kernel,
        name="tree_backward",
        out_shape=[
            pltpu.VMEM(queries.shape, BF),
            pltpu.VMEM(keys.shape, BF),
            pltpu.VMEM(values.shape, BF),
            pltpu.VMEM((1, D), F32),
            pltpu.VMEM((1, D), F32),
        ],
        in_specs=[anywhere] * 7 + [pl.BlockSpec(memory_space=pltpu.SMEM)],
        out_specs=[pl.BlockSpec(memory_space=pltpu.VMEM)] * 5,
        scratch_shapes=[
            pltpu.VMEM((2, T, G * D), BF),
            pltpu.VMEM((2, T, G * D), BF),
            pltpu.VMEM((2, T, D), BF),
            pltpu.VMEM((SLOTS, 2, T, D), BF),
            pltpu.VMEM((1, D), F32),
            pltpu.VMEM((1, D), F32),
            pltpu.VMEM((KEYS, D), F32),
            pltpu.VMEM((2 * ROWS, D), BF),
            pltpu.VMEM((2 * ROWS, D), BF),
            pltpu.VMEM((KEYS, D), BF),
            pltpu.VMEM((KEYS, D), BF),
            pltpu.VMEM((D, 2 * ROWS), F32),
            pltpu.VMEM((D, 2 * ROWS), F32),
            pltpu.VMEM((KEYS, D), F32),
            pltpu.VMEM((KEYS, D), F32),
            pltpu.VMEM((KEYS, 2 * ROWS), F32),
            pltpu.VMEM(((SLOTS - 1) * T, 2 * ROWS), F32),
            pltpu.VMEM((16, 2 * ROWS), F32),
            pltpu.VMEM((KEYS, 2 * ROWS), BF),
            pltpu.VMEM((KEYS, 2 * ROWS), BF),
            pltpu.VMEM((SLOTS, 2, T, D), F32),
            pltpu.VMEM((2 * ROWS, D), F32),
            pltpu.VMEM((NQ, 2, T, D), BF),
            pltpu.VMEM((DEPTH, 2, T, D), BF),
            pltpu.VMEM((2, T, D), BF),
            pltpu.VMEM((2 * NX - 1, 2, T, D), BF),
            pltpu.VMEM((NQ, 2, T, D), BF),
            pltpu.VMEM((3, 2, D), F32),
            pltpu.VMEM((NQ, 2, D), F32),
            pltpu.VMEM((NX * NY, 2, D), F32),
            pltpu.VMEM((NX * len(LAST_Y), NQ - EARLY_Q, 2, D), F32),
            pltpu.VMEM((2, D), F32),
            dma((8,)),
            dma(()),
            dma((SLOTS,)),
            dma(()),
            dma(()),
            dma((2,)),
            dma(()),
            dma(()),
            dma(()),
            dma((2,)),
            dma(()),
            dma(()),
            dma(()),
            dma(()),
            dma(()),
            dma(()),
        ],
        compiler_params=pltpu.CompilerParams(
            collective_id=0, has_side_effects=True, vmem_limit_bytes=40 * 2**20
        ),
        cost_estimate=pl.CostEstimate(flops=10 * 2 * ROWS * KEYS * D, bytes_accessed=2**20, transcendentals=2 * ROWS * KEYS),
    )(
        *(
            pltpu.with_memory_space_constraint(array, pltpu.HBM)
            for array in (
                queries,
                keys,
                values,
                output_gradient,
                q_gain.reshape(1, D),
                k_gain.reshape(1, D),
                jnp.asarray(rope_table()),
            )
        ),
        leaf_len,
    )
    dq, dk, dv, dq_gain, dk_gain = pl.pallas_call(
        hand_over,
        name="hand_over",
        out_shape=[jax.ShapeDtypeStruct(r.shape, r.dtype) for r in results],
        in_specs=[anywhere] * 5,
        out_specs=[in_hbm] * 5,
        scratch_shapes=[dma((5,))],
        compiler_params=pltpu.CompilerParams(vmem_limit_bytes=8 * 2**20),
    )(*(pltpu.with_memory_space_constraint(r, pltpu.VMEM) for r in results))
    return dq, dk, dv, dq_gain.reshape(D), dk_gain.reshape(D)


def solution(mesh):
    shape = dict(mesh.shape)
    if shape != {"leaf": NX * NZ * NC, "head": NY}:
        raise ValueError("another mesh")
    split = P(None, "leaf", "head")
    return jax.shard_map(
        on_device,
        mesh=mesh,
        in_specs=(split, split, split, split, P(), P(), P("leaf")),
        out_specs=(split, split, split, P(), P()),
        check_vma=False,
    )
```
